32 devices in a mesh: dp: 2 (over x), fsdp: 4 (over y, core), seq: 4 (over z).
Axes of the slice: x: 2, y: 2, z: 4, core: 2. Of those that a mesh axis runs over, the one named last changes fastest.
Arguments:
- inputs: bfloat16 [24, 1024, 1024], P(('dp', 'fsdp'), 'seq'), may hold values from -6 to 6
- segment_ids: int32 [24, 1024], P(('dp', 'fsdp'), 'seq'), may hold values from 0 to 17, as said below
- out_cotangent: bfloat16 [24, 1024, 1024], P(('dp', 'fsdp'), 'seq'), may hold values from -6 to 6
- mixer_gain: bfloat16 [1024], P('fsdp'), may hold values from 0.5 to 1.5
- qkv_weight: bfloat16 [1024, 3072], P('fsdp'), may hold values from -0.1875 to 0.1875
- gate_weight: bfloat16 [1024, 1536], P('fsdp'), may hold values from -0.1875 to 0.1875
- decay_weight: bfloat16 [1024, 12], P('fsdp'), may hold values from -0.375 to 0.375
- conv_weight: bfloat16 [4, 3072], P(None, 'fsdp'), may hold values from -3 to 3
- decay_log: float32 [6], replicated, may hold values from -1 to 1
- decay_bias: float32 [6], replicated, may hold values from -8 to -3
- head_gain: bfloat16 [256], P('fsdp'), may hold values from 0.5 to 1.5
- out_weight: bfloat16 [1536, 1024], P('fsdp'), may hold values from -0.3125 to 0.3125
- ffn_gain: bfloat16 [1024], P('fsdp'), may hold values from 0.5 to 1.5
- ffn_in_weight: bfloat16 [1024, 5632], P('fsdp'), may hold values from -0.1875 to 0.1875
- down_weight: bfloat16 [2816, 1024], P('fsdp'), may hold values from -0.15625 to 0.15625
Outputs:
- output: bfloat16 [24, 1024, 1024], P(('dp', 'fsdp'), 'seq')
- input_grad: bfloat16 [24, 1024, 1024], P(('dp', 'fsdp'), 'seq')
- grad_mixer_gain: float32 [1024], P('fsdp')
- grad_qkv_weight: float32 [1024, 3072], P('fsdp')
- grad_gate_weight: float32 [1024, 1536], P('fsdp')
- grad_decay_weight: float32 [1024, 12], P('fsdp')
- grad_conv_weight: float32 [4, 3072], P(None, 'fsdp')
- grad_decay_log: float32 [6], replicated
- grad_decay_bias: float32 [6], replicated
- grad_head_gain: float32 [256], P('fsdp')
- grad_out_weight: float32 [1536, 1024], P('fsdp')
- grad_ffn_gain: float32 [1024], P('fsdp')
- grad_ffn_in_weight: float32 [1024, 5632], P('fsdp')
- grad_down_weight: float32 [2816, 1024], P('fsdp')
The draws below stay inside these ranges and needn't reach their ends.
Inputs may be any that keep to these rules, and one draw needn't show every extreme that they name: `segment_ids`: within a sequence the ids start at 0 and rise by one where a document starts; a document has 60 to 800 tokens, except a sequence's last, which may be shorter. Of sequences 3 * j to 3 * j + 2, one drawn at random is a single document.
All inputs are finite; a program needn't handle non-finite values.
Results may differ from the reference program's by a relative error of at most 0.02.
Values may be sent and summed in bfloat16 or wider, within the bound.
No kernel may reach another device: no remote copies, remote signals or barrier semaphores. Data moves between devices by JAX's collectives and lax.ppermute only.
A program may use at most 384 MiB of HBM per device.

```python
import jax
import jax.numpy as jnp
from jax import lax

D = 1024
H = 6
DK = 128
DV = 256
FF = 2816
CONV = 4
BLOCK = 64
SEQS = 3
DOC_MIN = 60
DOC_MAX = 800
KD = 768
VD = 1536
C3 = 3072
LEN = 1024
NS = 24


def draw_segment_ids(key, part):
    key = jax.random.fold_in(key, 7)
    length_key, pick_key, dense_key = jax.random.split(key, 3)
    pieces = LEN // DOC_MIN + 1
    lengths = jax.random.randint(length_key, (NS, pieces), DOC_MIN, DOC_MAX + 1, dtype=jnp.int32)
    starts = jnp.cumsum(lengths, axis=1) - lengths
    position = jnp.arange(LEN, dtype=jnp.int32)
    begun = (starts[:, None, :] <= position[None, :, None]).astype(jnp.int32)
    seg_ids = jnp.sum(begun, axis=2) - 1
    chosen = jax.random.randint(pick_key, (NS // SEQS,), 0, SEQS, dtype=jnp.int32)
    rows = jnp.arange(NS, dtype=jnp.int32)
    whole = rows % SEQS == jnp.repeat(chosen, SEQS)
    dense_row = jax.random.randint(dense_key, (), 0, NS, dtype=jnp.int32)
    in_group = dense_row % SEQS
    base_row = dense_row - in_group
    dense_row = jnp.where(whole[dense_row], base_row + (in_group + 1) % SEQS, dense_row)
    dense_ids = position // DOC_MIN
    seg_ids = jnp.where((rows == dense_row)[:, None], dense_ids[None, :], seg_ids)
    return jnp.where(whole[:, None], 0, seg_ids).astype(jnp.int32)


def block_scale(own_key, shape, cuts, least, largest):
    def one(axis_at, blocks):
        steps = jax.random.uniform(jax.random.fold_in(jax.random.fold_in(own_key, 6), axis_at), (blocks,), jnp.float32, least / len(cuts), largest / len(cuts))
        return jnp.repeat(jnp.exp(steps), shape[axis_at] // blocks).reshape((-1,) + (1,) * (len(shape) - axis_at - 1))

    loudness = one(*cuts[0])
    for cut in cuts[1:]:
        loudness = loudness * one(*cut)
    return loudness


def noise(rng, extent, scale, most, cuts=(), kind=jnp.bfloat16):
    values = jax.random.normal(rng, extent, jnp.float32) * scale
    if len(cuts) > 0:
        values = block_scale(rng, extent, cuts, -0.22, 0.18) * values
    return jnp.clip(values, min=-most, max=most).astype(kind)


def setup_inputs(seed: int = 0) -> dict:
    key_list = jax.random.split(jax.random.key(seed), 16)
    return {
        "inputs": noise(key_list[0], (NS, LEN, D), 1.0, 6.0, ((0, 8), (1, 4))),
        "segment_ids": draw_segment_ids(jax.random.fold_in(key_list[15], 71), 0),
        "out_cotangent": noise(key_list[2], (NS, LEN, D), 1.0, 6.0, ((0, 8), (1, 4))),
        "mixer_gain": jnp.clip(1.0 + 0.1 * jax.random.normal(key_list[3], (D,), jnp.float32), 0.5, 1.5).astype(jnp.bfloat16),
        "qkv_weight": noise(key_list[4], (D, C3), D ** -0.5, 0.1875, ((0, 4),)),
        "gate_weight": noise(key_list[5], (D, VD), D ** -0.5, 0.1875, ((0, 4),)),
        "decay_weight": noise(key_list[6], (D, 2 * H), (D // 4) ** -0.5, 0.375, ((0, 4),)),
        "conv_weight": noise(key_list[7], (CONV, C3), CONV ** -0.5, 3.0, ((1, 4),)),
        "decay_log": jnp.clip(jax.random.uniform(key_list[8], (H,), jnp.float32, -1.0, 1.0), -1.0, 1.0),
        "decay_bias": jnp.clip(jax.random.uniform(key_list[9], (H,), jnp.float32, -8.0, -3.0), -8.0, -3.0),
        "head_gain": jnp.clip(1.0 + 0.1 * jax.random.normal(key_list[10], (DV,), jnp.float32), 0.5, 1.5).astype(jnp.bfloat16),
        "out_weight": noise(key_list[11], (VD, D), (VD // 4) ** -0.5, 0.3125, ((0, 4),)),
        "ffn_gain": jnp.clip(1.0 + 0.1 * jax.random.normal(key_list[12], (D,), jnp.float32), 0.5, 1.5).astype(jnp.bfloat16),
        "ffn_in_weight": noise(key_list[13], (D, 2 * FF), D ** -0.5, 0.1875, ((0, 4),)),
        "down_weight": noise(key_list[14], (FF, D), (FF // 2) ** -0.5, 0.15625, ((0, 4),)),
    }


EPSILON = 1e-06
HEAD_EPSILON = 0.001
PRECISE = lax.Precision.HIGHEST

@jax.custom_vjp
def low(v):
    return lax.optimization_barrier(v.astype(jnp.bfloat16)).astype(jnp.float32)

@jax.custom_vjp
def low_back(v):
    return v

def low_keep(v):
    return (low(v), None)

def low_pass(kept, grad):
    return (grad,)

def back_keep(v):
    return (v, None)

def back_low(kept, grad):
    return (low(grad),)
low.defvjp(low_keep, low_pass)
low_back.defvjp(back_keep, back_low)

def matmul(left, right):
    return jnp.dot(left.astype(jnp.float32), right.astype(jnp.float32), precision=PRECISE, preferred_element_type=jnp.float32)

def rms_norm(values, gain):
    return values * lax.rsqrt(lax.optimization_barrier(jnp.mean(values * values, axis=-1, keepdims=True)) + EPSILON) * gain

def unit_rows(values):
    return values * lax.rsqrt(lax.optimization_barrier(jnp.sum(values * values, axis=-1, keepdims=True)) + EPSILON)

def block_step(carry, block):
    state, prev_id = carry
    query, key, value, log_decay, beta, seg_ids = block
    count = seg_ids.shape[0]
    order = jnp.arange(count, dtype=jnp.int32)
    causal = order[:, None] >= order[None, :]
    same = (seg_ids[:, None] == seg_ids[None, :]) & causal
    strict = (same & (order[:, None] > order[None, :])).astype(state.dtype)
    totals = jnp.cumsum(log_decay, axis=0)
    spread = jnp.transpose(totals[:, None, :] - totals[None, :, :], (2, 0, 1))
    within = jnp.where(same[None], spread, 0.0)
    decay = jnp.exp(within) * same[None].astype(state.dtype)
    alive = (seg_ids == prev_id).astype(state.dtype)
    from_start = jnp.transpose(jnp.exp(totals) * alive[:, None])
    beta_rows = jnp.transpose(beta)
    key_key = jnp.einsum('thd,shd->hts', key, key, precision=PRECISE)
    query_key = jnp.einsum('thd,shd->hts', query, key, precision=PRECISE)
    key_state = jnp.einsum('thd,hdw->htw', key, state, precision=PRECISE)
    query_state = jnp.einsum('thd,hdw->htw', query, state, precision=PRECISE)
    lower = beta_rows[:, :, None] * key_key * decay * strict[None]
    system = jnp.eye(count, dtype=state.dtype)[None] + lower
    target = beta_rows[:, :, None] * (jnp.transpose(value, (1, 0, 2)) - from_start[:, :, None] * key_state)
    fresh = jax.scipy.linalg.solve_triangular(system, target, lower=True)
    result = from_start[:, :, None] * query_state + jnp.einsum('hts,hsw->htw', query_key * decay, fresh, precision=PRECISE)
    ending = decay[:, count - 1, :]
    new_state = from_start[:, count - 1][:, None, None] * state + jnp.einsum('shd,hs,hsw->hdw', key, ending, fresh, precision=PRECISE)
    return ((new_state, seg_ids[count - 1]), jnp.transpose(result, (1, 0, 2)))

def delta_sequence(query, key, value, log_decay, beta, seg_ids):
    blocks = query.shape[0] // BLOCK

    def blocks_of(array):
        return array.reshape((blocks, BLOCK) + array.shape[1:])
    start = (jnp.zeros((H, DK, DV), jnp.float32), jnp.int32(-1))
    final, outputs = lax.scan(jax.checkpoint(block_step), start, (blocks_of(query), blocks_of(key), blocks_of(value), blocks_of(log_decay), blocks_of(beta), blocks_of(seg_ids)))
    return outputs.reshape((blocks * BLOCK,) + outputs.shape[2:])

def conv_taps(padded, padded_ids, conv_weight):
    length = padded.shape[1] - (CONV - 1)
    current = padded_ids[:, CONV - 1:]
    mixed = jnp.zeros((padded.shape[0], length, padded.shape[2]), padded.dtype)
    for tap in range(CONV):
        keep = (padded_ids[:, tap:tap + length] == current).astype(padded.dtype)
        mixed = mixed + conv_weight[tap] * padded[:, tap:tap + length, :] * keep[:, :, None]
    return jax.nn.silu(mixed)

def short_conv(pre_conv, seg_ids, conv_weight):
    batch, length, channels = pre_conv.shape
    margin = CONV - 1
    padded = jnp.concatenate([jnp.zeros((batch, margin, channels), pre_conv.dtype), pre_conv], axis=1)
    padded_ids = jnp.concatenate([jnp.full((batch, margin), -1, jnp.int32), seg_ids], axis=1)
    return conv_taps(padded, padded_ids, conv_weight)

def head_out(mixed, gate_out, head_gain):
    normed = mixed * lax.rsqrt(lax.optimization_barrier(jnp.mean(mixed * mixed, axis=-1, keepdims=True)) + HEAD_EPSILON) * head_gain
    return normed * jax.nn.silu(gate_out.reshape(mixed.shape))

def forward(seg_ids, inputs, mixer_gain, qkv_weight, gate_weight, decay_weight, conv_weight, decay_log, decay_bias, head_gain, out_weight, ffn_gain, ffn_in_weight, down_weight):
    batch, length, width = inputs.shape
    rows = inputs.reshape(batch * length, width)
    normed = low(rms_norm(rows, mixer_gain))
    pre_conv = low_back(low(matmul(normed, qkv_weight)))
    gate_out = low_back(matmul(normed, gate_weight))
    decay_in = low_back(matmul(normed, decay_weight)).reshape(batch, length, 2 * H)
    conv_out = short_conv(pre_conv.reshape(batch, length, C3), seg_ids, conv_weight)
    query = low(unit_rows(conv_out[:, :, :KD].reshape(batch, length, H, DK)) * DK ** (-0.5))
    key = low(unit_rows(conv_out[:, :, KD:2 * KD].reshape(batch, length, H, DK)))
    value = low(conv_out[:, :, 2 * KD:].reshape(batch, length, H, DV))
    log_decay = -jnp.exp(decay_log) * jax.nn.softplus(decay_in[:, :, :H] + decay_bias)
    beta = jax.nn.sigmoid(decay_in[:, :, H:])
    mixed = jax.vmap(delta_sequence)(query, key, value, log_decay, beta, seg_ids)
    heads = low(head_out(mixed, gate_out, head_gain).reshape(batch * length, VD))
    middle = rows + low_back(matmul(heads, out_weight))
    normed_ffn = low(rms_norm(middle, ffn_gain))
    gate_up = low_back(matmul(normed_ffn, ffn_in_weight))
    hidden = low(jax.nn.silu(gate_up[:, :FF]) * gate_up[:, FF:])
    result = middle + low_back(matmul(hidden, down_weight))
    return result.reshape(batch, length, width)

def reference(inputs, segment_ids, out_cotangent, mixer_gain, qkv_weight, gate_weight, decay_weight, conv_weight, decay_log, decay_bias, head_gain, out_weight, ffn_gain, ffn_in_weight, down_weight):
    weights = tuple((array.astype(jnp.float32) for array in (mixer_gain, qkv_weight, gate_weight, decay_weight, conv_weight, decay_log, decay_bias, head_gain, out_weight, ffn_gain, ffn_in_weight, down_weight)))
    groups = inputs.shape[0] // SEQS
    shape = (groups, SEQS, LEN, D)
    stacked = (inputs.astype(jnp.float32).reshape(shape), segment_ids.reshape(groups, SEQS, LEN), out_cotangent.astype(jnp.float32).reshape(shape))

    def one_group(totals, item):
        group_in, group_ids, group_cot = item

        def run(group_in, *params):
            return forward(group_ids, group_in, *params)
        result, pullback = jax.vjp(run, group_in, *weights)
        grads = pullback(group_cot)
        totals = tuple((total + grad for total, grad in zip(totals, grads[1:])))
        return (totals, (result, grads[0]))
    zeros = tuple((jnp.zeros_like(array) for array in weights))
    totals, (outputs, input_grads) = lax.scan(one_group, zeros, stacked)
    grad_mixer, grad_qkv, grad_gate, grad_decay, grad_conv, grad_alog, grad_bias, grad_head, grad_out, grad_ffn, grad_ffn_in, grad_down = totals
    return (outputs.reshape(inputs.shape).astype(jnp.bfloat16), input_grads.reshape(inputs.shape).astype(jnp.bfloat16), grad_mixer, grad_qkv, grad_gate, grad_decay, grad_conv, grad_alog, grad_bias, grad_head, grad_out, grad_ffn, grad_ffn_in, grad_down)
```

```python
from functools import partial

import jax
import jax.numpy as jnp
from jax import lax
from jax.experimental import pallas as pl
from jax.experimental.pallas import tpu as pltpu
from jax.sharding import PartitionSpec as P

H = 6
DK = 128
DV = 256
CONV = 4
KD = 768
VD = 1536
C3 = 3072
RIM = 8

EPSILON = 1e-06
HEAD_EPSILON = 0.001
PRECISE = lax.Precision.HIGHEST
LOW = jnp.bfloat16
F32 = jnp.float32

NN = (((1,), (0,)), ((), ()))
NT = (((1,), (1,)), ((), ()))
TN = (((0,), (0,)), ((), ()))


def mm(left, right, dims=NN):
    return lax.dot_general(
        left.astype(LOW), right.astype(LOW), dims, preferred_element_type=F32
    )


def passed_along(value, axis, steps):
    count = lax.axis_size(axis)
    leading, last = (max(0, -steps), min(count, count - steps))
    return lax.ppermute(value, axis, [(source, source + steps) for source in range(leading, last)])


def rms_norm(values, gain):
    return values * lax.rsqrt(jnp.mean(values * values, axis=-1, keepdims=True) + EPSILON) * gain


def swiglu(gate_up):
    half = gate_up.shape[1] // 2
    return jax.nn.silu(gate_up[:, :half]) * gate_up[:, half:]


def iotas(count):
    shape = (count, count)
    return lax.broadcasted_iota(jnp.int32, shape, 0), lax.broadcasted_iota(jnp.int32, shape, 1)


def conv_head(s, parts, rims, taps, cols, pad_ref):
    at = 0
    for part, rim in zip(parts, rims):
        width = part.shape[-1]
        pad_ref[s, 0:RIM, at : at + width] = rim[s].astype(F32)
        pad_ref[s, RIM:, at : at + width] = part[s].astype(F32)
        at += width
    count = parts[0].shape[1]
    shifted = []
    total = None
    for tap in range(CONV):
        first = RIM - (CONV - 1) + tap
        values = pad_ref[s, first : first + count, :]
        if tap < CONV - 1:
            values = values * cols[:, 4 + tap : 5 + tap]
        shifted.append(values)
        term = values * taps[tap : tap + 1, :]
        total = term if total is None else total + term
    sig = jax.nn.sigmoid(total)
    return shifted, total, sig, total * sig


def unit(values):
    scale = lax.rsqrt(jnp.sum(values * values, axis=-1, keepdims=True) + EPSILON)
    return values * scale, scale


def decays(cols, rows, order, other):
    causal = (cols[:, 7:8] == rows[1:2, :]) & (order >= other)
    decay = jnp.exp(jnp.where(causal, cols[:, 0:1] - rows[0:1, :], -1e30))
    return decay, jnp.where(order > other, decay, 0.0)


def forward_kernel(
    q_ref, k_ref, v_ref, rq_ref, rk_ref, rv_ref, wq_ref, wk_ref, wv_ref, cols_ref, rows_ref,
    t_ref, uw_ref, local_ref, carried_ref, through_ref, offsets_ref, pad_ref,
):
    seqs, count = q_ref.shape[0], q_ref.shape[1]
    order, other = iotas(count)
    taps = jnp.concatenate([wq_ref[...], wk_ref[...], wv_ref[...]], axis=1)
    state = []
    for s in range(seqs):
        cols, rows = cols_ref[0, s], rows_ref[0, s]
        _, _, _, out = conv_head(
            s, (q_ref, k_ref, v_ref), (rq_ref, rk_ref, rv_ref), taps, cols, pad_ref
        )
        query = (unit(out[:, :DK])[0] * DK ** (-0.5)).astype(LOW)
        key = unit(out[:, DK : 2 * DK])[0].astype(LOW)
        value = out[:, 2 * DK :].astype(LOW)
        decay, strict = decays(cols, rows, order, other)
        beta, start, end = cols[:, 1:2], cols[:, 2:3], cols[:, 3:4]
        lower = beta * mm(key, key, NT) * strict
        attend = (mm(query, key, NT) * decay).astype(LOW)
        keyf = key.astype(F32)
        target = jnp.concatenate([beta * value.astype(F32), beta * start * keyf], axis=1).astype(LOW)
        state.append(dict(lower=lower, attend=attend, target=target, query=query,
                          ending=(end * keyf).astype(LOW), start=start))
    eye = (order == other).astype(F32)
    inverse = [eye - jnp.where((order >> 1 == other >> 1) & (order > other), x["lower"], 0.0) for x in state]
    level = 1
    while (2 << level) <= count:
        pick = (
            (order >> (level + 1) == other >> (level + 1))
            & ((order >> level) & 1 == 1)
            & ((other >> level) & 1 == 0)
        )
        half = []
        for s in range(seqs):
            half.append(mm(jnp.where(pick, state[s]["lower"], 0.0), inverse[s]))
        for s in range(seqs):
            inverse[s] = inverse[s] - mm(inverse[s], half[s])
        level += 1
    for s in range(seqs):
        x = state[s]
        t = inverse[s].astype(LOW)
        t_ref[0, s] = t
        uw = mm(t, x["target"]).astype(LOW)
        uw_ref[0, s] = uw
        both = mm(x["attend"], uw)
        local_ref[s] = both[:, :DV]
        carried_ref[s] = (x["start"] * x["query"].astype(F32) - both[:, DV:]).astype(LOW)
        ends = mm(x["ending"], uw, TN)
        offsets_ref[0, s] = ends[:, :DV]
        small, small_other = iotas(DK)
        last = x["start"][count - 1 : count, :]
        through_ref[0, s] = (jnp.where(small == small_other, last, 0.0) - ends[:, DV:]).astype(LOW)


def heads_kernel(local_ref, carried_ref, state_ref, gate_ref, gain_ref, heads_ref):
    for s in range(local_ref.shape[0]):
        mixed = local_ref[s] + mm(carried_ref[s], state_ref[0, s])
        scale = lax.rsqrt(jnp.mean(mixed * mixed, axis=-1, keepdims=True) + HEAD_EPSILON)
        gate = gate_ref[s]
        heads_ref[s] = (mixed * scale * gain_ref[...] * (gate * jax.nn.sigmoid(gate))).astype(LOW)


def heads_back_kernel(
    local_ref, carried_ref, state_ref, gate_ref, gain_ref, grad_ref,
    mixed_ref, ggate_ref, ggain_ref, gstate_ref,
):
    gain = gain_ref[...]
    total = jnp.zeros_like(gain)
    for s in range(local_ref.shape[0]):
        mixed = local_ref[s] + mm(carried_ref[s], state_ref[0, s])
        scale = lax.rsqrt(jnp.mean(mixed * mixed, axis=-1, keepdims=True) + HEAD_EPSILON)
        normed = mixed * scale
        gate = gate_ref[s]
        sig = jax.nn.sigmoid(gate)
        act = gate * sig
        grad = grad_ref[s]
        gn = grad * normed
        total = total + jnp.sum(gn * act, axis=0, keepdims=True)
        ggate_ref[s] = (gn * gain * (sig + act * (1.0 - sig))).astype(LOW)
        e = grad * gain * act
        gmixed = (scale * (e - normed * jnp.mean(e * normed, axis=-1, keepdims=True))).astype(LOW)
        mixed_ref[s] = gmixed
        gstate_ref[0, s] = mm(carried_ref[s], gmixed, TN)
    ggain_ref[0] = total


def backward_kernel(
    q_ref, k_ref, v_ref, rq_ref, rk_ref, rv_ref, wq_ref, wk_ref, wv_ref, cols_ref, rows_ref,
    t_ref, uw_ref, state_ref, gout_ref, gend_ref,
    gpre_ref, grim_ref, gtail_ref, gtaps_ref, gcols_ref, pad_ref, shift_ref,
):
    head = pl.program_id(0)
    seqs, count = q_ref.shape[0], q_ref.shape[1]
    order, other = iotas(count)
    taps = jnp.concatenate([wq_ref[...], wk_ref[...], wv_ref[...]], axis=1)
    before = (order < other).astype(LOW)
    gtaps = [None] * CONV
    at = (
        pl.ds(pl.multiple_of(head * DK, DK), DK),
        pl.ds(pl.multiple_of(KD + head * DK, DK), DK),
        pl.ds(pl.multiple_of(2 * KD + head * DV, DV), DV),
    )
    spans = ((0, DK), (DK, 2 * DK), (2 * DK, 2 * DK + DV))
    for s in range(seqs):
        cols, rows = cols_ref[0, s], rows_ref[0, s]
        shifted, total, sig, out = conv_head(
            s, (q_ref, k_ref, v_ref), (rq_ref, rk_ref, rv_ref), taps, cols, pad_ref
        )
        qhat, qscale = unit(out[:, :DK])
        khat, kscale = unit(out[:, DK : 2 * DK])
        query = (qhat * DK ** (-0.5)).astype(LOW)
        key = khat.astype(LOW)
        value = out[:, 2 * DK :]
        decay, strict = decays(cols, rows, order, other)
        beta, start, end = cols[:, 1:2], cols[:, 2:3], cols[:, 3:4]
        keyf = key.astype(F32)
        weight = beta * strict
        lower = mm(key, key, NT) * weight
        attend = mm(query, key, NT) * decay
        state = state_ref[0, s]
        gend = gend_ref[0, s]
        gout = gout_ref[s]
        uw = uw_ref[0, s]
        fresh = uw[:, :DV].astype(F32) - mm(uw[:, DV:], state)
        freshl = fresh.astype(LOW)
        gfresh = mm(attend, gout, TN) + mm(end * keyf, gend)
        gtarget = mm(t_ref[0, s], gfresh, TN)
        gattend = mm(gout, freshl, NT)
        glower = -mm(gtarget, freshl, NT)
        cross = gattend * attend + glower * lower
        high = cross.astype(LOW)
        reach = mm(high, before) + mm(cross - high.astype(F32), before)
        gqk = (gattend * decay).astype(LOW)
        gkk = (glower * weight).astype(LOW)
        gout_state = mm(gout, state, NT)
        gtarget_state = beta * mm(gtarget, state, NT)
        ends = mm(freshl, gend, NT)
        gquery = mm(gqk, key) + start * gout_state
        gkey = (
            mm(gqk, query, TN)
            + mm(gkk, key)
            + mm(gkk, key, TN)
            - start * gtarget_state
            + end * ends
        )
        gvalue = beta * gtarget
        from_start = start * jnp.sum(
            query.astype(F32) * gout_state - keyf * gtarget_state, axis=-1, keepdims=True
        )
        to_end = end * jnp.sum(keyf * ends, axis=-1, keepdims=True)
        through = jnp.sum(gend.astype(F32) * state.astype(F32)) * start[count - 1 : count, :]
        glog = jnp.sum(jnp.where(order >= other, reach + from_start, to_end), axis=0, keepdims=True)
        gbeta = jnp.sum(gtarget * fresh, axis=-1, keepdims=True) * (1.0 - beta)
        gbeta = jnp.sum(jnp.where(order == other, gbeta, 0.0), axis=0, keepdims=True)
        gcols_ref[0, s] = jnp.concatenate(
            [glog + through, gbeta, jnp.zeros((6, count), F32)], axis=0
        )
        gq = gquery * DK ** (-0.5)
        gq = qscale * (gq - qhat * jnp.sum(qhat * gq, axis=-1, keepdims=True))
        gk = kscale * (gkey - khat * jnp.sum(khat * gkey, axis=-1, keepdims=True))
        gconv = jnp.concatenate([gq, gk, gvalue], axis=1) * (sig + out * (1.0 - sig))
        for tap in range(CONV):
            part = jnp.sum(gconv * shifted[tap], axis=0, keepdims=True)
            gtaps[tap] = part if gtaps[tap] is None else gtaps[tap] + part
        width = gconv.shape[1]
        blank = jnp.zeros((RIM, width), F32)
        back = None
        for tap in range(CONV):
            term = gconv * taps[tap : tap + 1, :]
            if tap < CONV - 1:
                term = term * cols[:, 4 + tap : 5 + tap]
            shift_ref[tap, 0:RIM, :] = blank
            shift_ref[tap, RIM : RIM + count, :] = term
            shift_ref[tap, RIM + count :, :] = blank
            first = CONV - 1 - tap
            moved = shift_ref[tap, first : first + RIM + count, :]
            back = moved if back is None else back + moved
        for place, (low, top) in zip(at, spans):
            gpre_ref[s, :, place] = back[RIM:, low:top].astype(LOW)
            grim_ref[s, :, place] = back[:RIM, low:top]
            gtail_ref[s, :, place] = back[count:, low:top]
    for tap in range(CONV):
        for place, (low, top) in zip(at, spans):
            gtaps_ref[tap : tap + 1, place] = gtaps[tap][:, low:top]


def head_specs(seqs, count):
    def cut(rows, width, first):
        return pl.BlockSpec((seqs, rows, width), lambda h: (0, 0, first + h))

    def taps(width, first):
        return pl.BlockSpec((CONV, width), lambda h: (0, first + h))

    channel = [cut(count, DK, 0), cut(count, DK, H), cut(count, DV, H)]
    rim = [cut(RIM, DK, 0), cut(RIM, DK, H), cut(RIM, DV, H)]
    weight = [taps(DK, 0), taps(DK, H), taps(DV, H)]
    return channel + rim + weight + [per_head(seqs, count, 8), per_head(seqs, 8, count)]


def per_head(seqs, rows, width):
    return pl.BlockSpec((1, seqs, rows, width), lambda h: (h, 0, 0, 0))


def by_column(seqs, count, width):
    return pl.BlockSpec((seqs, count, width), lambda h: (0, 0, h))


def whole(*shape):
    return pl.BlockSpec(shape, lambda h: (0,) * len(shape))


def params(limit=48):
    return pltpu.CompilerParams(
        dimension_semantics=("arbitrary",), vmem_limit_bytes=limit * 2**20
    )


def mixer_forward(pre_conv, rim, taps, cols, rows):
    seqs, count = pre_conv.shape[0], pre_conv.shape[1]
    return pl.pallas_call(
        forward_kernel,
        grid=(H,),
        in_specs=head_specs(seqs, count),
        out_specs=[
            per_head(seqs, count, count),
            per_head(seqs, count, DV + DK),
            by_column(seqs, count, DV),
            by_column(seqs, count, DK),
            per_head(seqs, DK, DK),
            per_head(seqs, DK, DV),
        ],
        out_shape=[
            jax.ShapeDtypeStruct((H, seqs, count, count), LOW),
            jax.ShapeDtypeStruct((H, seqs, count, DV + DK), LOW),
            jax.ShapeDtypeStruct((seqs, count, VD), F32),
            jax.ShapeDtypeStruct((seqs, count, KD), LOW),
            jax.ShapeDtypeStruct((H, seqs, DK, DK), LOW),
            jax.ShapeDtypeStruct((H, seqs, DK, DV), F32),
        ],
        scratch_shapes=[pltpu.VMEM((seqs, RIM + count, 2 * DK + DV), F32)],
        compiler_params=params(),
        name="mixer_forward",
    )(pre_conv, pre_conv, pre_conv, rim, rim, rim, taps, taps, taps, cols, rows)


def heads_forward(local_part, carried, state, gate, gain):
    seqs, count = local_part.shape[0], local_part.shape[1]
    return pl.pallas_call(
        heads_kernel,
        grid=(H,),
        in_specs=[
            by_column(seqs, count, DV),
            by_column(seqs, count, DK),
            per_head(seqs, DK, DV),
            by_column(seqs, count, DV),
            whole(1, DV),
        ],
        out_specs=by_column(seqs, count, DV),
        out_shape=jax.ShapeDtypeStruct((seqs, count, VD), LOW),
        compiler_params=params(),
        name="heads_forward",
    )(local_part, carried, state, gate, gain)


def heads_backward(local_part, carried, state, gate, gain, grad):
    seqs, count = local_part.shape[0], local_part.shape[1]
    return pl.pallas_call(
        heads_back_kernel,
        grid=(H,),
        in_specs=[
            by_column(seqs, count, DV),
            by_column(seqs, count, DK),
            per_head(seqs, DK, DV),
            by_column(seqs, count, DV),
            whole(1, DV),
            by_column(seqs, count, DV),
        ],
        out_specs=[
            by_column(seqs, count, DV),
            by_column(seqs, count, DV),
            pl.BlockSpec((1, 1, DV), lambda h: (h, 0, 0)),
            per_head(seqs, DK, DV),
        ],
        out_shape=[
            jax.ShapeDtypeStruct((seqs, count, VD), LOW),
            jax.ShapeDtypeStruct((seqs, count, VD), LOW),
            jax.ShapeDtypeStruct((H, 1, DV), F32),
            jax.ShapeDtypeStruct((H, seqs, DK, DV), F32),
        ],
        compiler_params=params(),
        name="heads_backward",
    )(local_part, carried, state, gate, gain, grad)


def mixer_backward(pre_conv, rim, taps, cols, rows, t, uw, state, gout, gend):
    seqs, count = pre_conv.shape[0], pre_conv.shape[1]
    return pl.pallas_call(
        backward_kernel,
        grid=(H,),
        in_specs=head_specs(seqs, count)
        + [
            per_head(seqs, count, count),
            per_head(seqs, count, DV + DK),
            per_head(seqs, DK, DV),
            by_column(seqs, count, DV),
            per_head(seqs, DK, DV),
        ],
        out_specs=[
            whole(seqs, count, C3),
            whole(seqs, RIM, C3),
            whole(seqs, RIM, C3),
            whole(CONV, C3),
            per_head(seqs, 8, count),
        ],
        out_shape=[
            jax.ShapeDtypeStruct((seqs, count, C3), LOW),
            jax.ShapeDtypeStruct((seqs, RIM, C3), F32),
            jax.ShapeDtypeStruct((seqs, RIM, C3), F32),
            jax.ShapeDtypeStruct((CONV, C3), F32),
            jax.ShapeDtypeStruct((H, seqs, 8, count), F32),
        ],
        scratch_shapes=[
            pltpu.VMEM((seqs, RIM + count, 2 * DK + DV), F32),
            pltpu.VMEM((CONV, 2 * RIM + count, 2 * DK + DV), F32),
        ],
        compiler_params=params(),
        name="mixer_backward",
    )(
        pre_conv, pre_conv, pre_conv, rim, rim, rim, taps, taps, taps, cols, rows,
        t, uw, state, gout, gend,
    )


def token_columns(log_decay, beta, seg_ids, rim_seg):
    seqs, count = seg_ids.shape
    order = jnp.arange(count, dtype=jnp.int32)
    ones = (order[:, None] >= order[None, :]).astype(F32)
    running = jnp.einsum("ts,bsh->hbt", ones, log_decay, precision=PRECISE)
    ids = jnp.broadcast_to(seg_ids.astype(F32)[None], running.shape)
    alive = (seg_ids == rim_seg[:, -1:]).astype(F32)[None]
    ending = (seg_ids == seg_ids[:, -1:]).astype(F32)[None]
    start = jnp.exp(running) * alive
    end = jnp.exp(running[:, :, -1:] - running) * ending
    padded_ids = jnp.concatenate([rim_seg, seg_ids], axis=1)
    keeps = [
        jnp.broadcast_to(
            (padded_ids[:, tap : tap + count] == seg_ids).astype(F32)[None], running.shape
        )
        for tap in range(CONV - 1)
    ]
    betas = jnp.transpose(beta, (2, 0, 1))
    cols = jnp.stack([running, betas, start, end] + keeps + [ids], axis=-1)
    blank = jnp.zeros_like(running)
    rows = jnp.stack([running, ids] + [blank] * 6, axis=2)
    return cols, rows


def local(
    inputs,
    segment_ids,
    out_cotangent,
    mixer_gain,
    qkv_weight,
    gate_weight,
    decay_weight,
    conv_weight,
    decay_log,
    decay_bias,
    head_gain,
    out_weight,
    ffn_gain,
    ffn_in_weight,
    down_weight,
):
    batch, length, width = inputs.shape
    count = batch * length
    margin = CONV - 1
    group = lax.axis_size("fsdp")
    share = width // group
    small = jnp.concatenate(
        [
            mixer_gain,
            ffn_gain,
            head_gain,
            conv_weight.reshape(-1),
            decay_weight.reshape(-1),
        ]
    )
    small = lax.all_gather(small, "fsdp", axis=0)
    cuts = [mixer_gain.size, ffn_gain.size, head_gain.size, conv_weight.size, decay_weight.size]
    pieces, first = [], 0
    for size in cuts:
        pieces.append(small[:, first : first + size])
        first += size
    full_mixer_gain = pieces[0].reshape(-1).astype(F32)
    full_ffn_gain = pieces[1].reshape(-1).astype(F32)
    full_head_gain = pieces[2].reshape(1, -1).astype(F32)
    full_conv = jnp.transpose(pieces[3].reshape(group, CONV, -1), (1, 0, 2)).reshape(CONV, C3)
    full_conv = full_conv.astype(F32)
    full_decay = pieces[4].reshape(width, 2 * H)
    full_qkv = lax.all_gather(qkv_weight, "fsdp", axis=0, tiled=True)
    full_gate = lax.all_gather(gate_weight, "fsdp", axis=0, tiled=True)
    full_out = lax.all_gather(out_weight, "fsdp", axis=0, tiled=True)
    full_ffn_in = lax.all_gather(ffn_in_weight, "fsdp", axis=0, tiled=True)
    full_down = lax.all_gather(down_weight, "fsdp", axis=0, tiled=True)

    rows_in = inputs.astype(F32).reshape(count, width)
    normed, pull_mixer_norm = jax.vjp(rms_norm, rows_in, full_mixer_gain)
    normed_low = normed.astype(LOW)
    pre_conv = (
        jnp.dot(normed_low, full_qkv, preferred_element_type=F32)
        .astype(LOW)
        .reshape(batch, length, C3)
    )
    gate_out = jnp.dot(normed_low, full_gate, preferred_element_type=F32)
    gate_out = gate_out.reshape(batch, length, VD)
    decay_in = jnp.dot(normed_low, full_decay, preferred_element_type=F32).reshape(
        batch, length, 2 * H
    )
    rim_seg = passed_along(segment_ids[:, length - margin :], "seq", 1)
    rim = passed_along(pre_conv[:, length - margin :, :], "seq", 1).astype(F32)
    rim = jnp.pad(rim, ((0, 0), (RIM - margin, 0), (0, 0)))
    rate = jnp.exp(decay_log)
    shifted_decay = decay_in[:, :, :H] + decay_bias
    log_decay = -rate * jax.nn.softplus(shifted_decay)
    beta = jax.nn.sigmoid(decay_in[:, :, H:])
    cols, rows = token_columns(log_decay, beta, segment_ids, rim_seg)
    t, uw, local_part, carried, through, offsets = mixer_forward(
        pre_conv, rim, full_conv, cols, rows
    )

    steps = lax.axis_size("seq") - 1
    state_in = jnp.zeros(offsets.shape, LOW)
    for step in range(steps):
        leaving = offsets
        if step > 0:
            leaving = offsets + jnp.einsum(
                "hsij,hsjv->hsiv", through, state_in, preferred_element_type=F32
            )
        state_in = passed_along(leaving.astype(LOW), "seq", 1)

    heads_low = heads_forward(local_part, carried, state_in, gate_out, full_head_gain)
    heads_low = heads_low.reshape(count, VD)
    middle = rows_in + jnp.dot(heads_low, full_out, preferred_element_type=F32)
    normed_ffn, pull_ffn_norm = jax.vjp(rms_norm, middle, full_ffn_gain)
    normed_ffn_low = normed_ffn.astype(LOW)
    gate_up = jnp.dot(normed_ffn_low, full_ffn_in, preferred_element_type=F32)
    hidden, pull_swiglu = jax.vjp(swiglu, gate_up)
    hidden_low = hidden.astype(LOW)
    result = middle + jnp.dot(hidden_low, full_down, preferred_element_type=F32)
    output = result.astype(LOW).reshape(batch, length, width)

    def reduced(grad):
        shard = lax.psum_scatter(grad.astype(LOW), "fsdp", scatter_dimension=0, tiled=True)
        return lax.psum(shard, ("dp", "seq")).astype(F32)

    grad_rows = out_cotangent.reshape(count, width)
    grad_down = jnp.einsum("rf,rd->fd", hidden_low, grad_rows, preferred_element_type=F32)
    sum_down = reduced(grad_down)
    grad_hidden = jnp.einsum("rd,fd->rf", grad_rows, full_down, preferred_element_type=F32)
    (grad_gate_up,) = pull_swiglu(grad_hidden)
    grad_gate_up_low = grad_gate_up.astype(LOW)
    grad_ffn_in = jnp.einsum(
        "rd,rf->df", normed_ffn_low, grad_gate_up_low, preferred_element_type=F32
    )
    sum_ffn_in = reduced(grad_ffn_in)
    grad_normed_ffn = jnp.einsum(
        "rf,df->rd", grad_gate_up_low, full_ffn_in, preferred_element_type=F32
    )
    grad_middle_norm, grad_ffn_gain = pull_ffn_norm(grad_normed_ffn)
    grad_middle = grad_rows.astype(F32) + grad_middle_norm
    grad_branch = grad_middle.astype(LOW)
    grad_out = jnp.einsum("rv,rd->vd", heads_low, grad_branch, preferred_element_type=F32)
    sum_out = reduced(grad_out)
    grad_heads = jnp.einsum("rd,vd->rv", grad_branch, full_out, preferred_element_type=F32)
    grad_mixed, grad_gate_low, grad_head_gain, grad_state_in = heads_backward(
        local_part, carried, state_in, gate_out, full_head_gain,
        grad_heads.reshape(batch, length, VD),
    )
    grad_gate_low = grad_gate_low.reshape(count, VD)
    grad_gate = jnp.einsum("rd,rc->dc", normed_low, grad_gate_low, preferred_element_type=F32)
    sum_gate = reduced(grad_gate)

    grad_state_out = jnp.zeros(grad_state_in.shape, LOW)
    for step in range(steps):
        entering = grad_state_in
        if step > 0:
            entering = grad_state_in + jnp.einsum(
                "hsji,hsjv->hsiv", through, grad_state_out, preferred_element_type=F32
            )
        grad_state_out = passed_along(entering.astype(LOW), "seq", -1)

    grad_pre, grad_rim, grad_tail, grad_conv, grad_cols = mixer_backward(
        pre_conv, rim, full_conv, cols, rows, t, uw, state_in, grad_mixed, grad_state_out
    )
    grad_rim = passed_along(grad_rim[:, RIM - margin :, :].astype(LOW), "seq", -1).astype(F32)
    grad_tail = (grad_tail[:, RIM - margin :, :] + grad_rim).astype(LOW)
    grad_pre_low = lax.dynamic_update_slice(grad_pre, grad_tail, (0, length - margin, 0))
    grad_pre_low = grad_pre_low.reshape(count, C3)
    grad_qkv = jnp.einsum("rd,rc->dc", normed_low, grad_pre_low, preferred_element_type=F32)
    sum_qkv = reduced(grad_qkv)

    grad_log_decay = jnp.transpose(grad_cols[:, :, 0, :], (1, 2, 0))
    grad_decay_b = jnp.transpose(grad_cols[:, :, 1, :], (1, 2, 0))
    grad_decay_a = grad_log_decay * (-rate) * jax.nn.sigmoid(shifted_decay)
    grad_decay_bias = jnp.sum(grad_decay_a, axis=(0, 1))
    grad_decay_log = jnp.sum(grad_log_decay * log_decay, axis=(0, 1))
    grad_decay_low = jnp.concatenate([grad_decay_a, grad_decay_b], axis=-1).astype(LOW)
    grad_decay_low = grad_decay_low.reshape(count, 2 * H)
    grad_decay = jnp.einsum("rd,rc->dc", normed_low, grad_decay_low, preferred_element_type=F32)
    grad_normed = jnp.einsum("rc,dc->rd", grad_pre_low, full_qkv, preferred_element_type=F32)
    grad_normed = grad_normed + jnp.einsum(
        "rc,dc->rd", grad_gate_low, full_gate, preferred_element_type=F32
    )
    grad_normed = grad_normed + jnp.einsum(
        "rc,dc->rd", grad_decay_low, full_decay, preferred_element_type=F32
    )
    grad_rows_norm, grad_mixer_gain = pull_mixer_norm(grad_normed)
    input_grad = (grad_middle + grad_rows_norm).astype(LOW).reshape(batch, length, width)

    little = (
        grad_mixer_gain,
        grad_ffn_gain,
        jnp.sum(grad_head_gain, axis=(0, 1)),
        grad_conv.reshape(-1),
        grad_decay.reshape(-1),
        grad_decay_log,
        grad_decay_bias,
    )
    flat = lax.psum(jnp.concatenate(little), ("dp", "fsdp", "seq"))
    parts, first = [], 0
    for item in little:
        parts.append(flat[first : first + item.size])
        first += item.size
    place = lax.axis_index("fsdp")

    def own(values, axis=0):
        size = values.shape[axis] // group
        return lax.dynamic_slice_in_dim(values, place * size, size, axis)

    return (
        output,
        input_grad,
        own(parts[0]),
        sum_qkv,
        sum_gate,
        own(parts[4].reshape(width, 2 * H)),
        own(parts[3].reshape(CONV, C3), 1),
        parts[5],
        parts[6],
        own(parts[2]),
        sum_out,
        own(parts[1]),
        sum_ffn_in,
        sum_down,
    )


def solution(mesh):
    rows = P(("dp", "fsdp"), "seq", None)
    split = P("fsdp", None)
    placed = (
        rows,
        P(("dp", "fsdp"), "seq"),
        rows,
        P("fsdp"),
        split,
        split,
        split,
        P(None, "fsdp"),
        P(),
        P(),
        P("fsdp"),
        split,
        P("fsdp"),
        split,
        split,
    )
    return jax.shard_map(
        local,
        mesh=mesh,
        in_specs=placed,
        out_specs=(
            rows,
            rows,
            P("fsdp"),
            split,
            split,
            split,
            P(None, "fsdp"),
            P(),
            P(),
            P("fsdp"),
            split,
            P("fsdp"),
            split,
            split,
        ),
        check_vma=False,
    )
```

```python
from functools import partial

import jax
import jax.numpy as jnp
from jax import lax
from jax.experimental import pallas as pl
from jax.experimental.pallas import tpu as pltpu
from jax.sharding import PartitionSpec as P

H = 6
DK = 128
DV = 256
CONV = 4
KD = 768
VD = 1536
C3 = 3072
RIM = 8
HEAD = 2 * DK + DV
GROUPS = 3

EPSILON = 1e-06
HEAD_EPSILON = 0.001
PRECISE = lax.Precision.HIGHEST
LOW = jnp.bfloat16
F32 = jnp.float32

NN = (((1,), (0,)), ((), ()))
NT = (((1,), (1,)), ((), ()))
TN = (((0,), (0,)), ((), ()))


def mm(left, right, dims=NN):
    return lax.dot_general(
        left.astype(LOW), right.astype(LOW), dims, preferred_element_type=F32
    )


def passed_along(value, axis, steps):
    count = lax.axis_size(axis)
    leading, last = (max(0, -steps), min(count, count - steps))
    return lax.ppermute(value, axis, [(source, source + steps) for source in range(leading, last)])


def rms_norm(values, gain):
    return values * lax.rsqrt(jnp.mean(values * values, axis=-1, keepdims=True) + EPSILON) * gain


def swiglu(gate_up):
    half = gate_up.shape[1] // 2
    return jax.nn.silu(gate_up[:, :half]) * gate_up[:, half:]


def iotas(count):
    shape = (count, count)
    return lax.broadcasted_iota(jnp.int32, shape, 0), lax.broadcasted_iota(jnp.int32, shape, 1)


def conv_head(s, parts, rims, taps, cols, pad_ref):
    count = pad_ref.shape[1] - RIM
    margin = CONV - 1
    at = 0
    for part, rim in zip(parts, rims):
        width = part.shape[-1]
        pad_ref[s, RIM:, at : at + width] = part[s * count : (s + 1) * count, :].astype(F32)
        edge = rim[...].astype(F32)[margin * s : margin * (s + 1), :]
        pad_ref[s, RIM - margin : RIM, at : at + width] = edge
        at += width
    shifted = []
    total = None
    for tap in range(CONV):
        first = RIM - margin + tap
        values = pad_ref[s, first : first + count, :]
        if tap < margin:
            values = values * cols[:, 4 + tap : 5 + tap]
        shifted.append(values)
        term = values * taps[tap : tap + 1, :]
        total = term if total is None else total + term
    sig = jax.nn.sigmoid(total)
    return shifted, total, sig, total * sig


def unit(values):
    scale = lax.rsqrt(jnp.sum(values * values, axis=-1, keepdims=True) + EPSILON)
    return values * scale, scale


def decays(cols, rows, order, other):
    causal = (cols[:, 7:8] == rows[1:2, :]) & (order >= other)
    decay = jnp.exp(jnp.where(causal, cols[:, 0:1] - rows[0:1, :], -1e30))
    return decay, jnp.where(order > other, decay, 0.0)


def forward_kernel(
    q_ref, k_ref, v_ref, rq_ref, rk_ref, rv_ref, wq_ref, wk_ref, wv_ref, cols_ref, rows_ref,
    t_ref, uw_ref, local_ref, carried_ref,
    through_ref, offsets_ref, pad_ref,
):
    seqs, count = cols_ref.shape[1], cols_ref.shape[2]
    order, other = iotas(count)
    taps = jnp.concatenate([wq_ref[...], wk_ref[...], wv_ref[...]], axis=1)
    state = []
    for s in range(seqs):
        cols, rows = cols_ref[0, s], rows_ref[0, s]
        _, _, _, out = conv_head(
            s, (q_ref, k_ref, v_ref), (rq_ref, rk_ref, rv_ref), taps, cols, pad_ref
        )
        query = (unit(out[:, :DK])[0] * DK ** (-0.5)).astype(LOW)
        key = unit(out[:, DK : 2 * DK])[0].astype(LOW)
        value = out[:, 2 * DK :].astype(LOW)
        decay, strict = decays(cols, rows, order, other)
        beta, start, end = cols[:, 1:2], cols[:, 2:3], cols[:, 3:4]
        lower = beta * mm(key, key, NT) * strict
        attend = (mm(query, key, NT) * decay).astype(LOW)
        keyf = key.astype(F32)
        target = jnp.concatenate([beta * value.astype(F32), beta * start * keyf], axis=1).astype(LOW)
        state.append(dict(lower=lower, attend=attend, target=target, query=query,
                          ending=(end * keyf).astype(LOW), start=start))
    eye = (order == other).astype(F32)
    inverse = [eye - jnp.where((order >> 1 == other >> 1) & (order > other), x["lower"], 0.0) for x in state]
    level = 1
    while (2 << level) <= count:
        pick = (
            (order >> (level + 1) == other >> (level + 1))
            & ((order >> level) & 1 == 1)
            & ((other >> level) & 1 == 0)
        )
        half = []
        for s in range(seqs):
            half.append(mm(jnp.where(pick, state[s]["lower"], 0.0), inverse[s]))
        for s in range(seqs):
            inverse[s] = inverse[s] - mm(inverse[s], half[s])
        level += 1
    for s in range(seqs):
        x = state[s]
        t = inverse[s].astype(LOW)
        t_ref[0, s] = t
        uw = mm(t, x["target"]).astype(LOW)
        uw_ref[0, s] = uw
        both = mm(x["attend"], uw)
        local_ref[s] = both[:, :DV]
        carried_ref[s] = (x["start"] * x["query"].astype(F32) - both[:, DV:]).astype(LOW)
        ends = mm(x["ending"], uw, TN)
        offsets_ref[0, s] = ends[:, :DV]
        small, small_other = iotas(DK)
        last = x["start"][count - 1 : count, :]
        through_ref[0, s] = (jnp.where(small == small_other, last, 0.0) - ends[:, DV:]).astype(LOW)


def heads_kernel(local_ref, carried_ref, state_ref, gate_ref, gain_ref, heads_ref):
    for s in range(local_ref.shape[0]):
        mixed = local_ref[s] + mm(carried_ref[s], state_ref[0, s])
        scale = lax.rsqrt(jnp.mean(mixed * mixed, axis=-1, keepdims=True) + HEAD_EPSILON)
        gate = gate_ref[s]
        heads_ref[s] = (mixed * scale * gain_ref[...] * (gate * jax.nn.sigmoid(gate))).astype(LOW)


def heads_back_kernel(
    local_ref, carried_ref, state_ref, gate_ref, gain_ref, grad_ref,
    mixed_ref, ggate_ref, ggain_ref, gstate_ref,
):
    gain = gain_ref[...]
    total = jnp.zeros_like(gain)
    for s in range(local_ref.shape[0]):
        mixed = local_ref[s] + mm(carried_ref[s], state_ref[0, s])
        scale = lax.rsqrt(jnp.mean(mixed * mixed, axis=-1, keepdims=True) + HEAD_EPSILON)
        normed = mixed * scale
        gate = gate_ref[s]
        sig = jax.nn.sigmoid(gate)
        act = gate * sig
        grad = grad_ref[s]
        gn = grad * normed
        total = total + jnp.sum(gn * act, axis=0, keepdims=True)
        ggate_ref[s] = (gn * gain * (sig + act * (1.0 - sig))).astype(LOW)
        e = grad * gain * act
        gmixed = (scale * (e - normed * jnp.mean(e * normed, axis=-1, keepdims=True))).astype(LOW)
        mixed_ref[s] = gmixed
        gstate_ref[0, s] = mm(carried_ref[s], gmixed, TN)
    ggain_ref[0] = total


def backward_kernel(
    q_ref, k_ref, v_ref, rq_ref, rk_ref, rv_ref, wq_ref, wk_ref, wv_ref, cols_ref, rows_ref,
    t_ref, uw_ref, state_ref, gout_ref, gend_ref,
    gpre_ref, grim_ref, gtail_ref, gtaps_ref, gcols_ref, pad_ref, shift_ref,
):
    seqs, count = cols_ref.shape[1], cols_ref.shape[2]
    order, other = iotas(count)
    taps = jnp.concatenate([wq_ref[...], wk_ref[...], wv_ref[...]], axis=1)
    before = (order < other).astype(LOW)
    head, heads = pl.program_id(0), pl.num_programs(0)
    at = (
        pl.ds(pl.multiple_of(head * DK, DK), DK),
        pl.ds(pl.multiple_of((heads + head) * DK, DK), DK),
        pl.ds(pl.multiple_of(2 * heads * DK + head * DV, DV), DV),
    )
    spans = ((0, DK), (DK, 2 * DK), (2 * DK, HEAD))
    gtaps = [None] * CONV
    for s in range(seqs):
        cols, rows = cols_ref[0, s], rows_ref[0, s]
        shifted, total, sig, out = conv_head(
            s, (q_ref, k_ref, v_ref), (rq_ref, rk_ref, rv_ref), taps, cols, pad_ref
        )
        qhat, qscale = unit(out[:, :DK])
        khat, kscale = unit(out[:, DK : 2 * DK])
        query = (qhat * DK ** (-0.5)).astype(LOW)
        key = khat.astype(LOW)
        value = out[:, 2 * DK :]
        decay, strict = decays(cols, rows, order, other)
        beta, start, end = cols[:, 1:2], cols[:, 2:3], cols[:, 3:4]
        keyf = key.astype(F32)
        weight = beta * strict
        lower = mm(key, key, NT) * weight
        attend = mm(query, key, NT) * decay
        state = state_ref[0, s]
        gend = gend_ref[0, s]
        gout = gout_ref[s]
        uw = uw_ref[0, s]
        fresh = uw[:, :DV].astype(F32) - mm(uw[:, DV:], state)
        freshl = fresh.astype(LOW)
        gfresh = mm(attend, gout, TN) + mm(end * keyf, gend)
        gtarget = mm(t_ref[0, s], gfresh, TN)
        gattend = mm(gout, freshl, NT)
        glower = -mm(gtarget, freshl, NT)
        cross = gattend * attend + glower * lower
        high = cross.astype(LOW)
        reach = mm(high, before) + mm(cross - high.astype(F32), before)
        gqk = (gattend * decay).astype(LOW)
        gkk = (glower * weight).astype(LOW)
        gout_state = mm(gout, state, NT)
        gtarget_state = beta * mm(gtarget, state, NT)
        ends = mm(freshl, gend, NT)
        gquery = mm(gqk, key) + start * gout_state
        gkey = (
            mm(gqk, query, TN)
            + mm(gkk, key)
            + mm(gkk, key, TN)
            - start * gtarget_state
            + end * ends
        )
        gvalue = beta * gtarget
        from_start = start * jnp.sum(
            query.astype(F32) * gout_state - keyf * gtarget_state, axis=-1, keepdims=True
        )
        to_end = end * jnp.sum(keyf * ends, axis=-1, keepdims=True)
        through = jnp.sum(gend.astype(F32) * state.astype(F32)) * start[count - 1 : count, :]
        glog = jnp.sum(jnp.where(order >= other, reach + from_start, to_end), axis=0, keepdims=True)
        gbeta = jnp.sum(gtarget * fresh, axis=-1, keepdims=True) * (1.0 - beta)
        gbeta = jnp.sum(jnp.where(order == other, gbeta, 0.0), axis=0, keepdims=True)
        gcols_ref[0, s] = jnp.concatenate(
            [glog + through, gbeta, jnp.zeros((6, count), F32)], axis=0
        )
        gq = gquery * DK ** (-0.5)
        gq = qscale * (gq - qhat * jnp.sum(qhat * gq, axis=-1, keepdims=True))
        gk = kscale * (gkey - khat * jnp.sum(khat * gkey, axis=-1, keepdims=True))
        gconv = jnp.concatenate([gq, gk, gvalue], axis=1) * (sig + out * (1.0 - sig))
        for tap in range(CONV):
            part = jnp.sum(gconv * shifted[tap], axis=0, keepdims=True)
            gtaps[tap] = part if gtaps[tap] is None else gtaps[tap] + part
        width = gconv.shape[1]
        blank = jnp.zeros((RIM, width), F32)
        back = None
        for tap in range(CONV):
            term = gconv * taps[tap : tap + 1, :]
            if tap < CONV - 1:
                term = term * cols[:, 4 + tap : 5 + tap]
            shift_ref[tap, 0:RIM, :] = blank
            shift_ref[tap, RIM : RIM + count, :] = term
            shift_ref[tap, RIM + count :, :] = blank
            first = CONV - 1 - tap
            moved = shift_ref[tap, first : first + RIM + count, :]
            back = moved if back is None else back + moved
        for place, (low, top) in zip(at, spans):
            gpre_ref[s, :, place] = back[RIM:, low:top].astype(LOW)
            grim_ref[s, :, place] = back[:RIM, low:top]
            gtail_ref[s, :, place] = back[count:, low:top]
    gtaps = jnp.concatenate(gtaps, axis=0)
    for place, (low, top) in zip(at, spans):
        gtaps_ref[:, place] = gtaps[:, low:top]


def per_head(seqs, rows, width, first=0):
    return pl.BlockSpec((1, seqs, rows, width), lambda h: (first + h, 0, 0, 0))


def by_column(seqs, count, width, first=0):
    return pl.BlockSpec((seqs, count, width), lambda h: (0, 0, first + h))


def head_specs(seqs, count, first, heads):
    def cut(rows, row, width, column):
        return pl.BlockSpec((rows, width), lambda h: (row, column + h))

    rows, edge = seqs * count, edge_rows(seqs)
    late = 2 * heads * DK // DV
    specs = [cut(rows, 0, DK, 0), cut(rows, 0, DK, heads), cut(rows, 0, DV, late)]
    at = rows // edge
    specs += [cut(edge, at, DK, 0), cut(edge, at, DK, heads), cut(edge, at, DV, late)]
    specs += [cut(CONV, 0, DK, 0), cut(CONV, 0, DK, heads), cut(CONV, 0, DV, late)]
    return specs + [per_head(seqs, count, 8, first), per_head(seqs, 8, count, first)]


def edge_rows(seqs):
    return -(-seqs * (CONV - 1) // 16) * 16


def whole(*shape):
    return pl.BlockSpec(shape, lambda h: (0,) * len(shape))


def params(limit=48):
    return pltpu.CompilerParams(
        dimension_semantics=("arbitrary",), vmem_limit_bytes=limit * 2**20
    )


def mixer_forward(pre_conv, taps, cols, rows, first, heads):
    seqs, count = cols.shape[1], cols.shape[2]
    return pl.pallas_call(
        forward_kernel,
        grid=(heads,),
        in_specs=head_specs(seqs, count, first, heads),
        out_specs=[
            per_head(seqs, count, count),
            per_head(seqs, count, DV + DK),
            by_column(seqs, count, DV),
            by_column(seqs, count, DK),
            per_head(seqs, DK, DK),
            per_head(seqs, DK, DV),
        ],
        out_shape=[
            jax.ShapeDtypeStruct((heads, seqs, count, count), LOW),
            jax.ShapeDtypeStruct((heads, seqs, count, DV + DK), LOW),
            jax.ShapeDtypeStruct((seqs, count, heads * DV), F32),
            jax.ShapeDtypeStruct((seqs, count, heads * DK), LOW),
            jax.ShapeDtypeStruct((heads, seqs, DK, DK), LOW),
            jax.ShapeDtypeStruct((heads, seqs, DK, DV), F32),
        ],
        scratch_shapes=[pltpu.VMEM((seqs, RIM + count, HEAD), F32)],
        compiler_params=params(),
        name="mixer_forward",
    )(*[pre_conv] * 6, *[taps] * 3, cols, rows)


def heads_forward(local_part, carried, state, gate, gain, first, kept):
    seqs, count = local_part.shape[0], local_part.shape[1]
    heads = state.shape[0]
    operands = [local_part, carried, state, gate, gain]
    in_specs = [
        by_column(seqs, count, DV),
        by_column(seqs, count, DK),
        per_head(seqs, DK, DV),
        by_column(seqs, count, DV, first),
        pl.BlockSpec((1, DV), lambda h: (0, 0)),
    ]
    aliases = {}
    if kept is not None:
        operands.append(kept)
        in_specs.append(pl.BlockSpec(memory_space=pl.ANY))
        aliases = {5: 0}

    def kernel(*refs):
        heads_kernel(*refs[:5], refs[-1])

    return pl.pallas_call(
        kernel,
        grid=(heads,),
        in_specs=in_specs,
        out_specs=by_column(seqs, count, DV, first),
        out_shape=jax.ShapeDtypeStruct((seqs, count, VD), LOW),
        input_output_aliases=aliases,
        compiler_params=params(),
        name="heads_forward",
    )(*operands)


def heads_backward(local_part, carried, state, gate, gain, grad, first, kept):
    seqs, count = local_part.shape[0], local_part.shape[1]
    heads = state.shape[0]
    operands = [local_part, carried, state, gate, gain, grad]
    in_specs = [
        by_column(seqs, count, DV),
        by_column(seqs, count, DK),
        per_head(seqs, DK, DV),
        by_column(seqs, count, DV, first),
        pl.BlockSpec((1, DV), lambda h: (0, 0)),
        by_column(seqs, count, DV, first),
    ]
    aliases = {}
    if kept is not None:
        operands.append(kept)
        in_specs.append(pl.BlockSpec(memory_space=pl.ANY))
        aliases = {6: 1}

    def kernel(*refs):
        heads_back_kernel(*refs[:6], *refs[-4:])

    return pl.pallas_call(
        kernel,
        grid=(heads,),
        in_specs=in_specs,
        out_specs=[
            by_column(seqs, count, DV),
            by_column(seqs, count, DV, first),
            pl.BlockSpec((1, 1, DV), lambda h: (h, 0, 0)),
            per_head(seqs, DK, DV),
        ],
        out_shape=[
            jax.ShapeDtypeStruct((seqs, count, heads * DV), LOW),
            jax.ShapeDtypeStruct((seqs, count, VD), LOW),
            jax.ShapeDtypeStruct((heads, 1, DV), F32),
            jax.ShapeDtypeStruct((heads, seqs, DK, DV), F32),
        ],
        input_output_aliases=aliases,
        compiler_params=params(),
        name="heads_backward",
    )(*operands)


def mixer_backward(pre_conv, taps, cols, rows, t, uw, state, gout, gend, first):
    seqs, count = cols.shape[1], cols.shape[2]
    heads = state.shape[0]
    return pl.pallas_call(
        backward_kernel,
        grid=(heads,),
        in_specs=head_specs(seqs, count, first, heads)
        + [
            per_head(seqs, count, count),
            per_head(seqs, count, DV + DK),
            per_head(seqs, DK, DV),
            by_column(seqs, count, DV),
            per_head(seqs, DK, DV),
        ],
        out_specs=[
            whole(seqs, count, heads * HEAD),
            whole(seqs, RIM, heads * HEAD),
            whole(seqs, RIM, heads * HEAD),
            whole(CONV, heads * HEAD),
            per_head(seqs, 8, count),
        ],
        out_shape=[
            jax.ShapeDtypeStruct((seqs, count, heads * HEAD), LOW),
            jax.ShapeDtypeStruct((seqs, RIM, heads * HEAD), F32),
            jax.ShapeDtypeStruct((seqs, RIM, heads * HEAD), F32),
            jax.ShapeDtypeStruct((CONV, heads * HEAD), F32),
            jax.ShapeDtypeStruct((heads, seqs, 8, count), F32),
        ],
        scratch_shapes=[
            pltpu.VMEM((seqs, RIM + count, HEAD), F32),
            pltpu.VMEM((CONV, 2 * RIM + count, HEAD), F32),
        ],
        compiler_params=params(),
        name="mixer_backward",
    )(*[pre_conv] * 6, *[taps] * 3, cols, rows, t, uw, state, gout, gend)


def group_cuts(g):
    heads = H // GROUPS
    return (
        (g * heads * DK, heads * DK),
        (KD + g * heads * DK, heads * DK),
        (2 * KD + g * heads * DV, heads * DV),
    )


def of_group(values, g):
    return jnp.concatenate([values[:, at : at + size] for at, size in group_cuts(g)], axis=1)


def pack_groups(weight):
    rows = weight.shape[0]
    width = C3 // GROUPS

    def kernel(weight_ref, *outs):
        for g, out in enumerate(outs):
            first = 0
            for at, size in group_cuts(g):
                out[:, first : first + size] = weight_ref[:, at : at + size]
                first += size

    return pl.pallas_call(
        kernel,
        out_shape=[jax.ShapeDtypeStruct((rows, width), weight.dtype)] * GROUPS,
        compiler_params=pltpu.CompilerParams(vmem_limit_bytes=48 * 2**20),
        name="pack_groups",
    )(weight)


def unpack_groups(parts):
    rows = parts[0].shape[0]

    def kernel(*refs):
        for g, part in enumerate(refs[:-1]):
            first = 0
            for at, size in group_cuts(g):
                refs[-1][:, at : at + size] = part[:, first : first + size].astype(F32)
                first += size

    return pl.pallas_call(
        kernel,
        out_shape=jax.ShapeDtypeStruct((rows, C3), F32),
        compiler_params=pltpu.CompilerParams(vmem_limit_bytes=48 * 2**20),
        name="unpack_groups",
    )(*parts)


def swap(values, axis, bit):
    count = lax.axis_size(axis)
    return lax.ppermute(values, axis, [(at, at ^ bit) for at in range(count)])


def my_bit(axis, bit):
    return (lax.axis_index(axis) // bit) % 2


def plus(left, right):
    return (left.astype(F32) + right.astype(F32)).astype(LOW)


def bits_of(axis):
    count, bits, bit = lax.axis_size(axis), [], 1
    while bit < count:
        bits.append(bit)
        bit *= 2
    return bits if bit == count else None


def split(values):
    return values.reshape((2, values.shape[0] // 2) + values.shape[1:])


class Mover:
    pending = None
    value = None

    def __init__(self):
        self.todo = []

    def begin(self):
        if self.todo:
            send, self.then = self.todo.pop(0)
            self.pending = send()
        return self

    def settle(self, came):
        self.pending = None
        self.value = self.then(came)

    def finish(self):
        while self.todo or self.pending is not None:
            if self.pending is None:
                self.begin()
            self.settle(self.pending)
        return self.value


class ShardSum(Mover):
    def __init__(self, grad, scattered=False):
        super().__init__()
        self.value = grad.astype(LOW)
        self.plain = any(bits_of(axis) is None for axis in ("fsdp", "dp", "seq"))
        if self.plain:
            shard = lax.psum_scatter(self.value, "fsdp", scatter_dimension=0, tiled=True)
            self.value = lax.psum(shard, ("dp", "seq"))
            return
        if scattered:
            self.value = lax.psum_scatter(
                self.value, ("fsdp", "dp"), scatter_dimension=0, tiled=True
            )
        else:
            bits = bits_of("fsdp")
            self.value = self.value.reshape((2,) * len(bits) + (-1, grad.shape[1]))
            for at, bit in enumerate(bits):
                self.halved("fsdp", bit, len(bits) - 1 - at)
        undo = []
        for axis in ("dp", "seq"):
            bits = bits_of(axis)
            if axis == "dp" and scattered:
                undo += [(axis, bit) for bit in reversed(bits)]
                continue
            for bit in bits:
                if axis == "seq" and bit == bits[-1]:
                    self.added(axis, bit)
                else:
                    self.halved(axis, bit, None)
                    undo.append((axis, bit))
        for axis, bit in reversed(undo):
            self.joined(axis, bit)

    def halved(self, axis, bit, dim):
        def entries():
            return (split(self.value), 0) if dim is None else (self.value, dim)

        def send():
            values, at = entries()
            part = lax.dynamic_index_in_dim(values, 1 - my_bit(axis, bit), at, keepdims=False)
            return swap(part, axis, bit)

        def then(came):
            values, at = entries()
            part = lax.dynamic_index_in_dim(values, my_bit(axis, bit), at, keepdims=False)
            return plus(part, came)

        self.todo.append((send, then))

    def added(self, axis, bit):
        self.todo.append(
            (lambda: swap(self.value, axis, bit), lambda came: plus(self.value, came))
        )

    def joined(self, axis, bit):
        self.todo.append(
            (lambda: swap(self.value, axis, bit), lambda came: put_together(self.value, came, axis, bit))
        )


class AllSum(Mover):
    def __init__(self, values):
        super().__init__()
        self.value = values
        for axis in ("fsdp", "dp", "seq"):
            bits = bits_of(axis)
            if bits is None:
                self.value = lax.psum(self.value, axis)
            else:
                for bit in bits:
                    self.step(axis, bit)

    def step(self, axis, bit):
        self.todo.append(
            (lambda: swap(self.value, axis, bit), lambda came: self.value + came)
        )


def meet(movers, *arrays):
    movers = [mover for mover in movers if mover.pending is not None]
    count = len(arrays)
    out = lax.optimization_barrier(tuple(arrays) + tuple(mover.pending for mover in movers))
    for mover, came in zip(movers, out[count:]):
        mover.settle(came)
    return out[:count]


def begin(*movers):
    for mover in movers:
        mover.begin()


def put_together(mine, came, axis, bit):
    first = my_bit(axis, bit) == 0
    both = jnp.where(first, jnp.stack([mine, came]), jnp.stack([came, mine]))
    return both.reshape((2 * mine.shape[0],) + mine.shape[1:])


class ShardGather(Mover):
    def __init__(self, shard):
        super().__init__()
        if lax.axis_size("fsdp") != 4:
            self.value = lax.all_gather(shard, "fsdp", axis=0, tiled=True)
            return
        beside = swap(shard, "fsdp", 1)
        self.todo = [
            (lambda: swap(shard, "fsdp", 2), lambda came: came),
            (
                lambda: swap(self.value, "fsdp", 1),
                lambda came: assemble((shard, beside, self.value, came)),
            ),
        ]


def assemble(pieces):
    rows, width = pieces[0].shape
    tiles = 1
    rows_at = rows // tiles

    def piece_at(i):
        def at(j, t, me):
            return (jnp.where(j == i, t, jnp.where(j < i, 0, tiles - 1)), 0)

        return pl.BlockSpec((rows_at, width), at)

    def kernel(me_ref, *refs):
        for i in range(4):

            @pl.when(pl.program_id(0) == i)
            def _():
                refs[4][...] = refs[i][...]

    return pl.pallas_call(
        kernel,
        grid_spec=pltpu.PrefetchScalarGridSpec(
            num_scalar_prefetch=1,
            grid=(4, tiles),
            in_specs=[piece_at(i) for i in range(4)],
            out_specs=pl.BlockSpec((rows_at, width), lambda j, t, me: ((me[0] ^ j) * tiles + t, 0)),
        ),
        out_shape=jax.ShapeDtypeStruct((4 * rows, width), pieces[0].dtype),
        compiler_params=pltpu.CompilerParams(
            dimension_semantics=("arbitrary", "arbitrary"), vmem_limit_bytes=48 * 2**20
        ),
        name="assemble",
    )(lax.axis_index("fsdp").astype(jnp.int32).reshape(1), *pieces)


def token_columns(log_decay, beta, seg_ids, rim_seg):
    seqs, count = seg_ids.shape
    order = jnp.arange(count, dtype=jnp.int32)
    ones = (order[:, None] >= order[None, :]).astype(F32)
    running = jnp.einsum("ts,bsh->hbt", ones, log_decay, precision=PRECISE)
    ids = jnp.broadcast_to(seg_ids.astype(F32)[None], running.shape)
    alive = (seg_ids == rim_seg[:, -1:]).astype(F32)[None]
    ending = (seg_ids == seg_ids[:, -1:]).astype(F32)[None]
    start = jnp.exp(running) * alive
    end = jnp.exp(running[:, :, -1:] - running) * ending
    padded_ids = jnp.concatenate([rim_seg, seg_ids], axis=1)
    keeps = [
        jnp.broadcast_to(
            (padded_ids[:, tap : tap + count] == seg_ids).astype(F32)[None], running.shape
        )
        for tap in range(CONV - 1)
    ]
    betas = jnp.transpose(beta, (2, 0, 1))
    cols = jnp.stack([running, betas, start, end] + keeps + [ids], axis=-1)
    blank = jnp.zeros_like(running)
    rows = jnp.stack([running, ids] + [blank] * 6, axis=2)
    return cols, rows


def local(
    inputs,
    segment_ids,
    out_cotangent,
    mixer_gain,
    qkv_weight,
    gate_weight,
    decay_weight,
    conv_weight,
    decay_log,
    decay_bias,
    head_gain,
    out_weight,
    ffn_gain,
    ffn_in_weight,
    down_weight,
):
    batch, length, width = inputs.shape
    count = batch * length
    margin = CONV - 1
    group = lax.axis_size("fsdp")
    share = width // group
    small = jnp.concatenate(
        [
            mixer_gain,
            ffn_gain,
            head_gain,
            conv_weight.reshape(-1),
            decay_weight.reshape(-1),
        ]
    )
    small = lax.all_gather(small, "fsdp", axis=0)
    cuts = [mixer_gain.size, ffn_gain.size, head_gain.size, conv_weight.size, decay_weight.size]
    pieces, first = [], 0
    for size in cuts:
        pieces.append(small[:, first : first + size])
        first += size
    full_mixer_gain = pieces[0].reshape(-1).astype(F32)
    full_ffn_gain = pieces[1].reshape(-1).astype(F32)
    full_head_gain = pieces[2].reshape(1, -1).astype(F32)
    full_conv = jnp.transpose(pieces[3].reshape(group, CONV, -1), (1, 0, 2)).reshape(CONV, C3)
    full_conv = [of_group(full_conv.astype(F32), g) for g in range(GROUPS)]
    full_decay = pieces[4].reshape(width, 2 * H)
    packed = list(pack_groups(qkv_weight))
    gathers = [ShardGather(packed[0])]
    begin(gathers[0])
    full_gate = lax.all_gather(gate_weight, "fsdp", axis=0, tiled=True)
    full_out = lax.all_gather(out_weight, "fsdp", axis=0, tiled=True)
    full_ffn_in = lax.all_gather(ffn_in_weight, "fsdp", axis=0, tiled=True)
    full_down = lax.all_gather(down_weight, "fsdp", axis=0, tiled=True)

    rows_in = inputs.astype(F32).reshape(count, width)
    normed, pull_mixer_norm = jax.vjp(rms_norm, rows_in, full_mixer_gain)
    normed_low = normed.astype(LOW)
    edge = passed_along(inputs[:, length - margin :, :], "seq", 1).reshape(-1, width)
    edge = jnp.pad(edge, ((0, edge_rows(batch) - edge.shape[0]), (0, 0)))
    edge = rms_norm(edge.astype(F32), full_mixer_gain).astype(LOW)
    normed_all = jnp.concatenate([normed_low, edge], axis=0)
    decay_in = jnp.dot(normed_low, full_decay, preferred_element_type=F32).reshape(
        batch, length, 2 * H
    )
    rim_seg = passed_along(segment_ids[:, length - margin :], "seq", 1)
    rate = jnp.exp(decay_log)
    shifted_decay = decay_in[:, :, :H] + decay_bias
    log_decay = -rate * jax.nn.softplus(shifted_decay)
    beta = jax.nn.sigmoid(decay_in[:, :, H:])
    cols, rows = token_columns(log_decay, beta, segment_ids, rim_seg)
    hops = lax.axis_size("seq") - 1
    heads = H // GROUPS
    made, states, pre_convs, full_qkv = [], [None] * GROUPS, [], []

    def state_hop(hop, g):
        _, _, _, _, through, offsets = made[g]
        leaving = offsets
        if hop > 0:
            leaving = leaving + jnp.einsum(
                "hsij,hsjv->hsiv", through, states[g], preferred_element_type=F32
            )
        came = lax.ppermute(leaving.astype(LOW), "seq", [(hop, hop + 1)])
        states[g] = came if hop == 0 else states[g] + came

    def mixer_group(g):
        weight = gathers[g].finish()
        full_qkv.append(weight)
        pre_convs.append(jnp.dot(normed_all, weight, preferred_element_type=F32).astype(LOW))
        made.append(mixer_forward(pre_convs[g], full_conv[g], cols, rows, g * heads, heads))

    normed_all, cols, packed[1] = meet([gathers[0]], normed_all, cols, packed[1])
    gathers.append(ShardGather(packed[1]))
    begin(*gathers)
    mixer_group(0)
    state_hop(0, 0)
    normed_all, packed[2], _ = meet([gathers[1]], normed_all, packed[2], made[0][1])
    gathers.append(ShardGather(packed[2]))
    begin(*gathers)
    mixer_group(1)
    state_hop(0, 1)
    state_hop(1, 0)
    normed_all, _ = meet([gathers[2]], normed_all, made[1][1])
    mixer_group(2)
    state_hop(0, 2)
    state_hop(1, 1)
    state_hop(2, 0)
    state_hop(1, 2)
    state_hop(2, 1)
    state_hop(2, 2)
    gate_out = jnp.dot(normed_low, full_gate, preferred_element_type=F32)
    gate_out = gate_out.reshape(batch, length, VD)
    heads_low = None
    for g in range(GROUPS):
        _, _, local_part, carried, _, _ = made[g]
        heads_low = heads_forward(
            local_part, carried, states[g], gate_out, full_head_gain, g * heads, heads_low
        )
    heads_low = heads_low.reshape(count, VD)
    middle = rows_in + jnp.dot(heads_low, full_out, preferred_element_type=F32)
    normed_ffn, pull_ffn_norm = jax.vjp(rms_norm, middle, full_ffn_gain)
    normed_ffn_low = normed_ffn.astype(LOW)
    gate_up = jnp.dot(normed_ffn_low, full_ffn_in, preferred_element_type=F32)
    hidden, pull_swiglu = jax.vjp(swiglu, gate_up)
    hidden_low = hidden.astype(LOW)

    grad_rows = out_cotangent.reshape(count, width)
    grad_hidden = jnp.einsum("rd,fd->rf", grad_rows, full_down, preferred_element_type=F32)
    (grad_gate_up,) = pull_swiglu(grad_hidden)
    grad_gate_up_low = grad_gate_up.astype(LOW)
    grad_down = jnp.einsum("rf,rd->fd", hidden_low, grad_rows, preferred_element_type=F32)
    grad_gate_up_low, grad_down = meet([], grad_gate_up_low, grad_down.astype(LOW))
    r_down = ShardSum(grad_down, True)
    grad_normed_ffn = jnp.einsum(
        "rf,df->rd", grad_gate_up_low, full_ffn_in, preferred_element_type=F32
    )
    grad_middle_norm, grad_ffn_gain = pull_ffn_norm(grad_normed_ffn)
    grad_middle = grad_rows.astype(F32) + grad_middle_norm
    grad_branch, grad_gate_up_low = meet([], grad_middle.astype(LOW), grad_gate_up_low)
    grad_in = jnp.einsum(
        "rd,rf->df", normed_ffn_low, grad_gate_up_low, preferred_element_type=F32
    )
    grad_heads = jnp.einsum("rd,vd->rv", grad_branch, full_out, preferred_element_type=F32)
    grad_out = jnp.einsum("rv,rd->vd", heads_low, grad_branch, preferred_element_type=F32)
    grad_heads, grad_in, grad_out, r_down.value, hidden_low = meet(
        [], grad_heads, grad_in.astype(LOW), grad_out.astype(LOW), r_down.value, hidden_low
    )
    r_in = ShardSum(grad_in, True)
    r_out = ShardSum(grad_out, True)
    begin(r_down)
    grad_heads = grad_heads.reshape(batch, length, VD)
    back, grad_gate_low = [], None
    for g in range(GROUPS):
        _, _, local_part, carried, _, _ = made[g]
        back.append(
            heads_backward(
                local_part, carried, states[g], gate_out, full_head_gain, grad_heads,
                g * heads, grad_gate_low,
            )
        )
        grad_gate_low = back[g][1]
    grad_head_gain = sum(jnp.sum(item[2], axis=(0, 1)) for item in back)
    grad_gate_low = grad_gate_low.reshape(count, VD)
    grad_gate = jnp.einsum("rd,rc->dc", normed_low, grad_gate_low, preferred_element_type=F32)
    result = middle + jnp.dot(hidden_low, full_down, preferred_element_type=F32)
    output = result.astype(LOW).reshape(batch, length, width)

    grad_states = [None] * GROUPS
    for hop in range(hops, 0, -1):
        for g in range(GROUPS):
            entering = back[g][3]
            if hop < hops:
                entering = entering + jnp.einsum(
                    "hsji,hsjv->hsiv", made[g][4], grad_states[g], preferred_element_type=F32
                )
            came = lax.ppermute(entering.astype(LOW), "seq", [(hop, hop - 1)])
            grad_states[g] = came if hop == hops else grad_states[g] + came
    mixed_a, grad_gate, output = meet([r_down], back[0][0], grad_gate.astype(LOW), output)
    r_gate = ShardSum(grad_gate, True)
    begin(r_down)
    mixed_a, grad_states[0] = meet([r_down], mixed_a, grad_states[0])

    def mixer_back(g, grad_mixed):
        t, uw, _, _, _, _ = made[g]
        return mixer_backward(
            pre_convs[g], full_conv[g], cols, rows, t, uw, states[g], grad_mixed, grad_states[g],
            g * heads,
        )

    def with_rim(grad_pre, grad_rim, grad_tail):
        came = passed_along(grad_rim[:, RIM - margin :, :].astype(LOW), "seq", -1).astype(F32)
        grad_tail = (grad_tail[:, RIM - margin :, :] + came).astype(LOW)
        grad_pre = lax.dynamic_update_slice(grad_pre, grad_tail, (0, length - margin, 0))
        return grad_pre.reshape(count, heads * HEAD)

    def qkv_sum(grad_pre):
        grad = jnp.einsum("rd,rc->dc", normed_low, grad_pre, preferred_element_type=F32)
        return ShardSum(grad)

    def normed_part(grad_pre, weight):
        return jnp.einsum("rc,dc->rd", grad_pre, weight, preferred_element_type=F32)

    begin(r_down)
    got_a = mixer_back(0, mixed_a)
    mixed_b, pre_a, rim_a, tail_a, r_in.value = meet(
        [r_down], back[1][0], got_a[0], got_a[1], got_a[2], r_in.value
    )
    begin(r_down, r_in)
    got_b = mixer_back(1, mixed_b)
    pre_a = with_rim(pre_a, rim_a, tail_a)
    mixed_c, pre_a, pre_b, rim_b, tail_b, r_out.value = meet(
        [r_down, r_in], back[2][0], pre_a, got_b[0], got_b[1], got_b[2], r_out.value
    )
    sum_a = qkv_sum(pre_a)
    begin(r_in, sum_a, r_out)
    got_c = mixer_back(2, mixed_c)
    pre_b = with_rim(pre_b, rim_b, tail_b)
    pre_b, pre_c, rim_c, tail_c, grad_gate_low = meet(
        [r_in, sum_a, r_out], pre_b, got_c[0], got_c[1], got_c[2], grad_gate_low
    )
    begin(r_in, sum_a, r_out)
    sum_b = qkv_sum(pre_b)
    pre_c = with_rim(pre_c, rim_c, tail_c)
    pre_c, sum_b.value, grad_gate_low = meet([], pre_c, sum_b.value, grad_gate_low)
    sum_c = qkv_sum(pre_c)
    begin(sum_b, sum_c)
    grad_normed = normed_part(pre_a, full_qkv[0]) + normed_part(pre_b, full_qkv[1])
    pre_c, grad_normed = meet([r_in, sum_a, r_out, sum_b, sum_c], pre_c, grad_normed)
    begin(r_in, sum_a, r_out, sum_b, sum_c)
    grad_normed = grad_normed + normed_part(pre_c, full_qkv[2])
    grad_cols = jnp.concatenate([got_a[4], got_b[4], got_c[4]], axis=0)
    conv_parts = [got_a[3], got_b[3], got_c[3]]
    spans = [0, heads * DK, 2 * heads * DK, heads * HEAD]
    grad_conv = jnp.concatenate(
        [part[:, low:top] for low, top in zip(spans, spans[1:]) for part in conv_parts], axis=1
    )
    grad_log_decay = jnp.transpose(grad_cols[:, :, 0, :], (1, 2, 0))
    grad_decay_b = jnp.transpose(grad_cols[:, :, 1, :], (1, 2, 0))
    grad_decay_a = grad_log_decay * (-rate) * jax.nn.sigmoid(shifted_decay)
    grad_decay_bias = jnp.sum(grad_decay_a, axis=(0, 1))
    grad_decay_log = jnp.sum(grad_log_decay * log_decay, axis=(0, 1))
    grad_decay_low = jnp.concatenate([grad_decay_a, grad_decay_b], axis=-1).astype(LOW)
    grad_decay_low = grad_decay_low.reshape(count, 2 * H)
    grad_decay = jnp.einsum("rd,rc->dc", normed_low, grad_decay_low, preferred_element_type=F32)
    grad_normed = grad_normed + jnp.einsum(
        "rc,dc->rd", grad_gate_low, full_gate, preferred_element_type=F32
    )
    grad_normed = grad_normed + jnp.einsum(
        "rc,dc->rd", grad_decay_low, full_decay, preferred_element_type=F32
    )
    grad_rows_norm, grad_mixer_gain = pull_mixer_norm(grad_normed)
    input_grad = (grad_middle + grad_rows_norm).astype(LOW).reshape(batch, length, width)

    little = (
        grad_mixer_gain,
        grad_ffn_gain,
        grad_head_gain,
        grad_conv.reshape(-1),
        grad_decay.reshape(-1),
        grad_decay_log,
        grad_decay_bias,
    )
    small_grads = jnp.concatenate(little)
    movers = [r_down, r_in, sum_a, sum_b, r_out, sum_c, r_gate]
    small_grads, r_gate.value = meet(movers, small_grads, r_gate.value)
    all_sum = AllSum(small_grads)
    movers.append(all_sum)
    while any(mover.todo for mover in movers):
        begin(*movers)
        meet(movers, small_grads)
    flat = all_sum.value
    sum_qkv = unpack_groups([sum_a.value, sum_b.value, sum_c.value])
    parts, first = [], 0
    for item in little:
        parts.append(flat[first : first + item.size])
        first += item.size
    place = lax.axis_index("fsdp")

    def own(values, axis=0):
        size = values.shape[axis] // group
        return lax.dynamic_slice_in_dim(values, place * size, size, axis)

    return (
        output,
        input_grad,
        own(parts[0]),
        sum_qkv,
        r_gate.value.astype(F32),
        own(parts[4].reshape(width, 2 * H)),
        own(parts[3].reshape(CONV, C3), 1),
        parts[5],
        parts[6],
        own(parts[2]),
        r_out.value.astype(F32),
        own(parts[1]),
        r_in.value.astype(F32),
        r_down.value.astype(F32),
    )


def solution(mesh):
    rows = P(("dp", "fsdp"), "seq", None)
    split = P("fsdp", None)
    placed = (
        rows,
        P(("dp", "fsdp"), "seq"),
        rows,
        P("fsdp"),
        split,
        split,
        split,
        P(None, "fsdp"),
        P(),
        P(),
        P("fsdp"),
        split,
        P("fsdp"),
        split,
        split,
    )
    return jax.shard_map(
        local,
        mesh=mesh,
        in_specs=placed,
        out_specs=(
            rows,
            rows,
            P("fsdp"),
            split,
            split,
            split,
            P(None, "fsdp"),
            P(),
            P(),
            P("fsdp"),
            split,
            P("fsdp"),
            split,
            split,
        ),
        check_vma=False,
    )
```

```python
from functools import partial

import jax
import jax.numpy as jnp
from jax import lax
from jax.experimental import pallas as pl
from jax.experimental.pallas import tpu as pltpu
from jax.sharding import PartitionSpec as P

H = 6
DK = 128
DV = 256
CONV = 4
KD = 768
VD = 1536
C3 = 3072
RIM = 8
HEAD = 2 * DK + DV
GROUPS = 3

EPSILON = 1e-06
HEAD_EPSILON = 0.001
PRECISE = lax.Precision.HIGHEST
LOW = jnp.bfloat16
F32 = jnp.float32

NN = (((1,), (0,)), ((), ()))
NT = (((1,), (1,)), ((), ()))
TN = (((0,), (0,)), ((), ()))


def mm(left, right, dims=NN):
    return lax.dot_general(
        left.astype(LOW), right.astype(LOW), dims, preferred_element_type=F32
    )


def passed_along(value, axis, steps):
    count = lax.axis_size(axis)
    leading, last = (max(0, -steps), min(count, count - steps))
    return lax.ppermute(value, axis, [(source, source + steps) for source in range(leading, last)])


def rms_norm(values, gain):
    return values * lax.rsqrt(jnp.mean(values * values, axis=-1, keepdims=True) + EPSILON) * gain


def iotas(count):
    shape = (count, count)
    return lax.broadcasted_iota(jnp.int32, shape, 0), lax.broadcasted_iota(jnp.int32, shape, 1)


def conv_head(s, parts, rims, taps, cols, pad_ref):
    count = pad_ref.shape[1] - RIM
    margin = CONV - 1
    at = 0
    for part, rim in zip(parts, rims):
        width = part.shape[-1]
        pad_ref[s, RIM:, at : at + width] = part[s * count : (s + 1) * count, :].astype(F32)
        edge = rim[...].astype(F32)[margin * s : margin * (s + 1), :]
        pad_ref[s, RIM - margin : RIM, at : at + width] = edge
        at += width
    shifted = []
    total = None
    for tap in range(CONV):
        first = RIM - margin + tap
        values = pad_ref[s, first : first + count, :]
        if tap < margin:
            values = values * cols[:, 4 + tap : 5 + tap]
        shifted.append(values)
        term = values * taps[tap : tap + 1, :]
        total = term if total is None else total + term
    sig = jax.nn.sigmoid(total)
    return shifted, total, sig, total * sig


def unit(values):
    scale = lax.rsqrt(jnp.sum(values * values, axis=-1, keepdims=True) + EPSILON)
    return values * scale, scale


def decays(cols, rows, order, other):
    causal = (cols[:, 7:8] == rows[1:2, :]) & (order >= other)
    decay = jnp.exp(jnp.where(causal, cols[:, 0:1] - rows[0:1, :], -1e30))
    return decay, jnp.where(order > other, decay, 0.0)


def forward_kernel(
    q_ref, k_ref, v_ref, rq_ref, rk_ref, rv_ref, wq_ref, wk_ref, wv_ref, cols_ref, rows_ref,
    t_ref, uw_ref, local_ref, carried_ref,
    through_ref, offsets_ref, pad_ref,
):
    seqs, count = cols_ref.shape[1], cols_ref.shape[2]
    order, other = iotas(count)
    taps = jnp.concatenate([wq_ref[...], wk_ref[...], wv_ref[...]], axis=1)
    state = []
    for s in range(seqs):
        cols, rows = cols_ref[0, s], rows_ref[0, s]
        _, _, _, out = conv_head(
            s, (q_ref, k_ref, v_ref), (rq_ref, rk_ref, rv_ref), taps, cols, pad_ref
        )
        query = (unit(out[:, :DK])[0] * DK ** (-0.5)).astype(LOW)
        key = unit(out[:, DK : 2 * DK])[0].astype(LOW)
        value = out[:, 2 * DK :].astype(LOW)
        decay, strict = decays(cols, rows, order, other)
        beta, start, end = cols[:, 1:2], cols[:, 2:3], cols[:, 3:4]
        lower = beta * mm(key, key, NT) * strict
        attend = (mm(query, key, NT) * decay).astype(LOW)
        keyf = key.astype(F32)
        target = jnp.concatenate([beta * value.astype(F32), beta * start * keyf], axis=1).astype(LOW)
        state.append(dict(lower=lower, attend=attend, target=target, query=query,
                          ending=(end * keyf).astype(LOW), start=start))
    inverse, lowers = [], []
    joined = order ^ other
    eye = (joined == 0).astype(LOW)
    for x in state:
        lower = x["lower"].astype(LOW)
        lowers.append(lower)
        inverse.append(eye - lower * ((joined == 1) & (order > other)).astype(LOW))
    level = 1
    while (4 << level) <= count:
        pick = ((joined >> level) == 1).astype(LOW)
        half = [mm(lowers[s] * pick, inverse[s]).astype(LOW) for s in range(seqs)]
        for s in range(seqs):
            inverse[s] = inverse[s] - mm(inverse[s], half[s]).astype(LOW)
        level += 1
    mid = count // 2
    corner = [mm(lowers[s][mid:, :mid], inverse[s][:mid, :mid]) for s in range(seqs)]
    blank = jnp.zeros((mid, mid), LOW)
    for s in range(seqs):
        left = mm(inverse[s][mid:, mid:], corner[s]).astype(LOW)
        inverse[s] = jnp.concatenate(
            [
                jnp.concatenate([inverse[s][:mid, :mid], blank], axis=1),
                jnp.concatenate([-left, inverse[s][mid:, mid:]], axis=1),
            ],
            axis=0,
        )
    for s in range(seqs):
        x = state[s]
        t = inverse[s]
        t_ref[0, s] = t
        uw = mm(t, x["target"]).astype(LOW)
        uw_ref[0, s] = uw
        both = mm(x["attend"], uw)
        local_ref[s] = both[:, :DV]
        carried_ref[s] = (x["start"] * x["query"].astype(F32) - both[:, DV:]).astype(LOW)
        ends = mm(x["ending"], uw, TN)
        offsets_ref[0, s] = ends[:, :DV]
        small, small_other = iotas(DK)
        last = x["start"][count - 1 : count, :]
        through_ref[0, s] = (jnp.where(small == small_other, last, 0.0) - ends[:, DV:]).astype(LOW)


def heads_kernel(local_ref, carried_ref, state_ref, gate_ref, gain_ref, heads_ref):
    for s in range(local_ref.shape[0]):
        mixed = local_ref[s] + mm(carried_ref[s], state_ref[0, s])
        scale = lax.rsqrt(jnp.mean(mixed * mixed, axis=-1, keepdims=True) + HEAD_EPSILON)
        gate = gate_ref[s]
        heads_ref[s] = (mixed * scale * gain_ref[...] * (gate * jax.nn.sigmoid(gate))).astype(LOW)


def heads_back_kernel(
    local_ref, carried_ref, state_ref, gate_ref, gain_ref, grad_ref,
    mixed_ref, ggate_ref, ggain_ref, gstate_ref,
):
    gain = gain_ref[...]
    total = jnp.zeros_like(gain)
    for s in range(local_ref.shape[0]):
        mixed = local_ref[s] + mm(carried_ref[s], state_ref[0, s])
        scale = lax.rsqrt(jnp.mean(mixed * mixed, axis=-1, keepdims=True) + HEAD_EPSILON)
        normed = mixed * scale
        gate = gate_ref[s]
        sig = jax.nn.sigmoid(gate)
        act = gate * sig
        grad = grad_ref[s]
        gn = grad * normed
        total = total + jnp.sum(gn * act, axis=0, keepdims=True)
        ggate_ref[s] = (gn * gain * (sig + act * (1.0 - sig))).astype(LOW)
        e = grad * gain * act
        gmixed = (scale * (e - normed * jnp.mean(e * normed, axis=-1, keepdims=True))).astype(LOW)
        mixed_ref[s] = gmixed
        gstate_ref[0, s] = mm(carried_ref[s], gmixed, TN)
    ggain_ref[0] = total


def backward_kernel(
    q_ref, k_ref, v_ref, rq_ref, rk_ref, rv_ref, wq_ref, wk_ref, wv_ref, cols_ref, rows_ref,
    t_ref, uw_ref, state_ref, gout_ref, gend_ref,
    gpre_ref, grim_ref, gtail_ref, gtaps_ref, gcols_ref, pad_ref, shift_ref,
):
    seqs, count = cols_ref.shape[1], cols_ref.shape[2]
    order, other = iotas(count)
    taps = jnp.concatenate([wq_ref[...], wk_ref[...], wv_ref[...]], axis=1)
    before = (order < other).astype(LOW)
    head, heads = pl.program_id(0), pl.num_programs(0)
    at = (
        pl.ds(pl.multiple_of(head * DK, DK), DK),
        pl.ds(pl.multiple_of((heads + head) * DK, DK), DK),
        pl.ds(pl.multiple_of(2 * heads * DK + head * DV, DV), DV),
    )
    spans = ((0, DK), (DK, 2 * DK), (2 * DK, HEAD))
    gtaps = [None] * CONV
    for s in range(seqs):
        cols, rows = cols_ref[0, s], rows_ref[0, s]
        shifted, total, sig, out = conv_head(
            s, (q_ref, k_ref, v_ref), (rq_ref, rk_ref, rv_ref), taps, cols, pad_ref
        )
        qhat, qscale = unit(out[:, :DK])
        khat, kscale = unit(out[:, DK : 2 * DK])
        query = (qhat * DK ** (-0.5)).astype(LOW)
        key = khat.astype(LOW)
        value = out[:, 2 * DK :]
        decay, strict = decays(cols, rows, order, other)
        beta, start, end = cols[:, 1:2], cols[:, 2:3], cols[:, 3:4]
        keyf = key.astype(F32)
        weight = beta * strict
        lower = mm(key, key, NT) * weight
        attend = mm(query, key, NT) * decay
        state = state_ref[0, s]
        gend = gend_ref[0, s]
        gout = gout_ref[s]
        uw = uw_ref[0, s]
        fresh = uw[:, :DV].astype(F32) - mm(uw[:, DV:], state)
        freshl = fresh.astype(LOW)
        gfresh = mm(attend, gout, TN) + mm(end * keyf, gend)
        gtarget = mm(t_ref[0, s], gfresh, TN)
        gattend = mm(gout, freshl, NT)
        glower = -mm(gtarget, freshl, NT)
        cross = gattend * attend + glower * lower
        high = cross.astype(LOW)
        reach = mm(high, before) + mm(cross - high.astype(F32), before)
        gqk = (gattend * decay).astype(LOW)
        gkk = (glower * weight).astype(LOW)
        gout_state = mm(gout, state, NT)
        gtarget_state = beta * mm(gtarget, state, NT)
        ends = mm(freshl, gend, NT)
        gquery = mm(gqk, key) + start * gout_state
        gkey = (
            mm(gqk, query, TN)
            + mm(gkk, key)
            + mm(gkk, key, TN)
            - start * gtarget_state
            + end * ends
        )
        gvalue = beta * gtarget
        from_start = start * jnp.sum(
            query.astype(F32) * gout_state - keyf * gtarget_state, axis=-1, keepdims=True
        )
        to_end = end * jnp.sum(keyf * ends, axis=-1, keepdims=True)
        through = jnp.sum(gend.astype(F32) * state.astype(F32)) * start[count - 1 : count, :]
        glog = jnp.sum(jnp.where(order >= other, reach + from_start, to_end), axis=0, keepdims=True)
        gbeta = jnp.sum(gtarget * fresh, axis=-1, keepdims=True) * (1.0 - beta)
        gbeta = jnp.sum(jnp.where(order == other, gbeta, 0.0), axis=0, keepdims=True)
        gcols_ref[0, s] = jnp.concatenate(
            [glog + through, gbeta, jnp.zeros((6, count), F32)], axis=0
        )
        gq = gquery * DK ** (-0.5)
        gq = qscale * (gq - qhat * jnp.sum(qhat * gq, axis=-1, keepdims=True))
        gk = kscale * (gkey - khat * jnp.sum(khat * gkey, axis=-1, keepdims=True))
        gconv = jnp.concatenate([gq, gk, gvalue], axis=1) * (sig + out * (1.0 - sig))
        for tap in range(CONV):
            part = jnp.sum(gconv * shifted[tap], axis=0, keepdims=True)
            gtaps[tap] = part if gtaps[tap] is None else gtaps[tap] + part
        width = gconv.shape[1]
        blank = jnp.zeros((RIM, width), F32)
        back = None
        for tap in range(CONV):
            term = gconv * taps[tap : tap + 1, :]
            if tap < CONV - 1:
                term = term * cols[:, 4 + tap : 5 + tap]
            shift_ref[tap, 0:RIM, :] = blank
            shift_ref[tap, RIM : RIM + count, :] = term
            shift_ref[tap, RIM + count :, :] = blank
            first = CONV - 1 - tap
            moved = shift_ref[tap, first : first + RIM + count, :]
            back = moved if back is None else back + moved
        for place, (low, top) in zip(at, spans):
            gpre_ref[s, :, place] = back[RIM:, low:top].astype(LOW)
            grim_ref[s, :, place] = back[:RIM, low:top]
            gtail_ref[s, :, place] = back[count:, low:top]
    gtaps = jnp.concatenate(gtaps, axis=0)
    for place, (low, top) in zip(at, spans):
        gtaps_ref[:, place] = gtaps[:, low:top]


def per_head(seqs, rows, width, first=0):
    return pl.BlockSpec((1, seqs, rows, width), lambda h: (first + h, 0, 0, 0))


def by_column(seqs, count, width, first=0):
    return pl.BlockSpec((seqs, count, width), lambda h: (0, 0, first + h))


def head_specs(seqs, count, first, heads):
    def cut(rows, row, width, column):
        return pl.BlockSpec((rows, width), lambda h: (row, column + h))

    rows, edge = seqs * count, edge_rows(seqs)
    late = 2 * heads * DK // DV
    specs = [cut(rows, 0, DK, 0), cut(rows, 0, DK, heads), cut(rows, 0, DV, late)]
    at = rows // edge
    specs += [cut(edge, at, DK, 0), cut(edge, at, DK, heads), cut(edge, at, DV, late)]
    specs += [cut(CONV, 0, DK, 0), cut(CONV, 0, DK, heads), cut(CONV, 0, DV, late)]
    return specs + [per_head(seqs, count, 8, first), per_head(seqs, 8, count, first)]


def edge_rows(seqs):
    return -(-seqs * (CONV - 1) // 16) * 16


def whole(*shape):
    return pl.BlockSpec(shape, lambda h: (0,) * len(shape))


def params(limit=48):
    return pltpu.CompilerParams(
        dimension_semantics=("arbitrary",), vmem_limit_bytes=limit * 2**20
    )


def mixer_forward(pre_conv, taps, cols, rows, first, heads):
    seqs, count = cols.shape[1], cols.shape[2]
    return pl.pallas_call(
        forward_kernel,
        grid=(heads,),
        in_specs=head_specs(seqs, count, first, heads),
        out_specs=[
            per_head(seqs, count, count),
            per_head(seqs, count, DV + DK),
            by_column(seqs, count, DV),
            by_column(seqs, count, DK),
            per_head(seqs, DK, DK),
            per_head(seqs, DK, DV),
        ],
        out_shape=[
            jax.ShapeDtypeStruct((heads, seqs, count, count), LOW),
            jax.ShapeDtypeStruct((heads, seqs, count, DV + DK), LOW),
            jax.ShapeDtypeStruct((seqs, count, heads * DV), F32),
            jax.ShapeDtypeStruct((seqs, count, heads * DK), LOW),
            jax.ShapeDtypeStruct((heads, seqs, DK, DK), LOW),
            jax.ShapeDtypeStruct((heads, seqs, DK, DV), F32),
        ],
        scratch_shapes=[pltpu.VMEM((seqs, RIM + count, HEAD), F32)],
        compiler_params=params(),
        name="mixer_forward",
    )(*[pre_conv] * 6, *[taps] * 3, cols, rows)


def heads_forward(local_part, carried, state, gate, gain, first, kept):
    seqs, count = local_part.shape[0], local_part.shape[1]
    heads = state.shape[0]
    operands = [local_part, carried, state, gate, gain]
    in_specs = [
        by_column(seqs, count, DV),
        by_column(seqs, count, DK),
        per_head(seqs, DK, DV),
        by_column(seqs, count, DV, first),
        pl.BlockSpec((1, DV), lambda h: (0, 0)),
    ]
    aliases = {}
    if kept is not None:
        operands.append(kept)
        in_specs.append(pl.BlockSpec(memory_space=pl.ANY))
        aliases = {5: 0}

    def kernel(*refs):
        heads_kernel(*refs[:5], refs[-1])

    return pl.pallas_call(
        kernel,
        grid=(heads,),
        in_specs=in_specs,
        out_specs=by_column(seqs, count, DV, first),
        out_shape=jax.ShapeDtypeStruct((seqs, count, VD), LOW),
        input_output_aliases=aliases,
        compiler_params=params(),
        name="heads_forward",
    )(*operands)


def heads_backward(local_part, carried, state, gate, gain, grad, first, kept):
    seqs, count = local_part.shape[0], local_part.shape[1]
    heads = state.shape[0]
    operands = [local_part, carried, state, gate, gain, grad]
    in_specs = [
        by_column(seqs, count, DV),
        by_column(seqs, count, DK),
        per_head(seqs, DK, DV),
        by_column(seqs, count, DV, first),
        pl.BlockSpec((1, DV), lambda h: (0, 0)),
        by_column(seqs, count, DV, first),
    ]
    aliases = {}
    if kept is not None:
        operands.append(kept)
        in_specs.append(pl.BlockSpec(memory_space=pl.ANY))
        aliases = {6: 1}

    def kernel(*refs):
        heads_back_kernel(*refs[:6], *refs[-4:])

    return pl.pallas_call(
        kernel,
        grid=(heads,),
        in_specs=in_specs,
        out_specs=[
            by_column(seqs, count, DV),
            by_column(seqs, count, DV, first),
            pl.BlockSpec((1, 1, DV), lambda h: (h, 0, 0)),
            per_head(seqs, DK, DV),
        ],
        out_shape=[
            jax.ShapeDtypeStruct((seqs, count, heads * DV), LOW),
            jax.ShapeDtypeStruct((seqs, count, VD), LOW),
            jax.ShapeDtypeStruct((heads, 1, DV), F32),
            jax.ShapeDtypeStruct((heads, seqs, DK, DV), F32),
        ],
        input_output_aliases=aliases,
        compiler_params=params(),
        name="heads_backward",
    )(*operands)


def mixer_backward(
    pre_conv, taps, cols, rows, t, uw, state, gout, gend, first, place, width, rims, kept
):
    seqs, count = cols.shape[1], cols.shape[2]
    heads = state.shape[0]
    run = heads * HEAD

    def at(*shape):
        return pl.BlockSpec(shape, lambda h: (0, 0, place))

    operands = [*[pre_conv] * 6, *[taps] * 3, cols, rows, t, uw, state, gout, gend]
    inputs = len(operands)
    aliases = {inputs + i: i for i in range(len(kept))}

    def kernel(*refs):
        backward_kernel(*refs[:inputs], *refs[inputs + len(kept) :])

    return pl.pallas_call(
        kernel,
        grid=(heads,),
        in_specs=head_specs(seqs, count, first, heads)
        + [
            per_head(seqs, count, count),
            per_head(seqs, count, DV + DK),
            per_head(seqs, DK, DV),
            by_column(seqs, count, DV),
            per_head(seqs, DK, DV),
        ]
        + [pl.BlockSpec(memory_space=pl.ANY)] * len(kept),
        out_specs=[
            at(seqs, count, run),
            at(seqs, RIM, run),
            at(seqs, RIM, run),
            whole(CONV, run),
            per_head(seqs, 8, count),
        ],
        out_shape=[
            jax.ShapeDtypeStruct((seqs, count, width), LOW),
            jax.ShapeDtypeStruct((seqs, RIM, rims), F32),
            jax.ShapeDtypeStruct((seqs, RIM, rims), F32),
            jax.ShapeDtypeStruct((CONV, run), F32),
            jax.ShapeDtypeStruct((heads, seqs, 8, count), F32),
        ],
        scratch_shapes=[
            pltpu.VMEM((seqs, RIM + count, HEAD), F32),
            pltpu.VMEM((CONV, 2 * RIM + count, HEAD), F32),
        ],
        input_output_aliases=aliases,
        compiler_params=params(),
        name="mixer_backward",
    )(*operands, *kept)


def ffn_kernel(x_ref, up_ref, side_ref, grad_ref, down_ref, hidden_ref, back_ref):
    tile = up_ref.shape[1]
    half = back_ref.shape[1] // 2
    at = pl.program_id(0) * tile
    rows = x_ref.shape[0]
    step = 256 if rows % 256 == 0 else rows

    def part(i, _):
        here = pl.ds(pl.multiple_of(i * step, step), step)
        x = x_ref[here, :]
        a = mm(x, up_ref[...])
        b = mm(x, side_ref[...])
        grad = mm(grad_ref[here, :], down_ref[...], NT)
        sig = jax.nn.sigmoid(a)
        act = a * sig
        hidden_ref[here, :] = (act * b).astype(LOW)
        first = grad * b * (sig + act * (1.0 - sig))
        back_ref[here, pl.ds(pl.multiple_of(at, tile), tile)] = first.astype(LOW)
        back_ref[here, pl.ds(pl.multiple_of(half + at, tile), tile)] = (grad * act).astype(LOW)
        return 0

    lax.fori_loop(0, rows // step, part, 0)


def ffn_middle(x, weight, grad, down):
    rows, width = x.shape
    units = down.shape[0]
    tile = 256
    tiles = units // tile
    return pl.pallas_call(
        ffn_kernel,
        grid=(tiles,),
        in_specs=[
            pl.BlockSpec((rows, width), lambda j: (0, 0)),
            pl.BlockSpec((width, tile), lambda j: (0, j)),
            pl.BlockSpec((width, tile), lambda j: (0, tiles + j)),
            pl.BlockSpec((rows, width), lambda j: (0, 0)),
            pl.BlockSpec((tile, width), lambda j: (j, 0)),
        ],
        out_specs=[
            pl.BlockSpec((rows, tile), lambda j: (0, j)),
            pl.BlockSpec((rows, 2 * units), lambda j: (0, 0)),
        ],
        out_shape=[
            jax.ShapeDtypeStruct((rows, units), LOW),
            jax.ShapeDtypeStruct((rows, 2 * units), LOW),
        ],
        compiler_params=params(),
        name="ffn_middle",
    )(x, weight, weight, grad, down)


def group_cuts(g):
    heads = H // GROUPS
    return (
        (g * heads * DK, heads * DK),
        (KD + g * heads * DK, heads * DK),
        (2 * KD + g * heads * DV, heads * DV),
    )


def of_group(values, g):
    return jnp.concatenate([values[:, at : at + size] for at, size in group_cuts(g)], axis=1)


def pack_groups(weight):
    rows = weight.shape[0]
    width = C3 // GROUPS

    def kernel(weight_ref, *outs):
        for g, out in enumerate(outs):
            first = 0
            for at, size in group_cuts(g):
                out[:, first : first + size] = weight_ref[:, at : at + size]
                first += size

    return pl.pallas_call(
        kernel,
        out_shape=[jax.ShapeDtypeStruct((rows, width), weight.dtype)] * GROUPS,
        compiler_params=pltpu.CompilerParams(vmem_limit_bytes=48 * 2**20),
        name="pack_groups",
    )(weight)


def unpack_groups(first, last):
    rows = first.shape[0]
    run = C3 // GROUPS

    def kernel(first_ref, last_ref, qkv_ref):
        for g in range(GROUPS):
            part, at = (last_ref, 0) if g == GROUPS - 1 else (first_ref, g * run)
            for to, size in group_cuts(g):
                qkv_ref[:, to : to + size] = part[:, at : at + size].astype(F32)
                at += size

    return pl.pallas_call(
        kernel,
        out_shape=jax.ShapeDtypeStruct((rows, C3), F32),
        compiler_params=pltpu.CompilerParams(vmem_limit_bytes=48 * 2**20),
        name="unpack_groups",
    )(first, last)


def swap(values, axis, bit):
    count = lax.axis_size(axis)
    return lax.ppermute(values, axis, [(at, at ^ bit) for at in range(count)])


def my_bit(axis, bit):
    return (lax.axis_index(axis) // bit) % 2


def plus(left, right):
    return (left.astype(F32) + right.astype(F32)).astype(LOW)


def bits_of(axis):
    count, bits, bit = lax.axis_size(axis), [], 1
    while bit < count:
        bits.append(bit)
        bit *= 2
    return bits if bit == count else None


def split(values):
    return values.reshape((2, values.shape[0] // 2) + values.shape[1:])


class Mover:
    pending = None
    value = None

    def __init__(self):
        self.todo = []

    def begin(self):
        if self.todo:
            send, self.then = self.todo.pop(0)
            self.pending = send()
        return self

    def settle(self, came):
        self.pending = None
        self.value = self.then(came)

    def finish(self):
        while self.todo or self.pending is not None:
            if self.pending is None:
                self.begin()
            self.settle(self.pending)
        return self.value


def scattered_sums():
    return all(bits_of(axis) is not None for axis in ("fsdp", "dp", "seq"))


def scatter(grad):
    if not scattered_sums():
        shard = lax.psum_scatter(grad, "fsdp", scatter_dimension=0, tiled=True)
        return lax.psum(shard, ("dp", "seq"))
    return lax.psum_scatter(grad, ("fsdp", "dp"), scatter_dimension=0, tiled=True)


class ShardSum(Mover):
    def __init__(self, grad, scattered=False, ready=False):
        super().__init__()
        self.value = grad.astype(LOW)
        if ready and not scattered_sums():
            return
        self.plain = any(bits_of(axis) is None for axis in ("fsdp", "dp", "seq"))
        if self.plain:
            shard = lax.psum_scatter(self.value, "fsdp", scatter_dimension=0, tiled=True)
            self.value = lax.psum(shard, ("dp", "seq"))
            return
        if ready:
            scattered = True
        elif scattered:
            self.value = lax.psum_scatter(
                self.value, ("fsdp", "dp"), scatter_dimension=0, tiled=True
            )
        else:
            bits = bits_of("fsdp")
            self.value = self.value.reshape((2,) * len(bits) + (-1, grad.shape[1]))
            for at, bit in enumerate(bits):
                self.halved("fsdp", bit, len(bits) - 1 - at)
        undo = []
        for axis in ("dp", "seq"):
            bits = bits_of(axis)
            if axis == "dp" and scattered:
                undo += [(axis, bit) for bit in reversed(bits)]
                continue
            for bit in bits:
                if axis == "seq" and bit == bits[-1]:
                    self.added(axis, bit)
                else:
                    self.halved(axis, bit, None)
                    undo.append((axis, bit))
        for axis, bit in reversed(undo):
            self.joined(axis, bit)

    def halved(self, axis, bit, dim):
        def entries():
            return (split(self.value), 0) if dim is None else (self.value, dim)

        def send():
            values, at = entries()
            part = lax.dynamic_index_in_dim(values, 1 - my_bit(axis, bit), at, keepdims=False)
            return swap(part, axis, bit)

        def then(came):
            values, at = entries()
            part = lax.dynamic_index_in_dim(values, my_bit(axis, bit), at, keepdims=False)
            return plus(part, came)

        self.todo.append((send, then))

    def added(self, axis, bit):
        self.todo.append(
            (lambda: swap(self.value, axis, bit), lambda came: plus(self.value, came))
        )

    def joined(self, axis, bit):
        self.todo.append(
            (lambda: swap(self.value, axis, bit), lambda came: put_together(self.value, came, axis, bit))
        )


class Chain(Mover):
    def __init__(self, through, offsets, spec, step):
        super().__init__()
        last = lax.axis_size("seq") - 1
        for hop in range(last) if step > 0 else range(last, 0, -1):
            self.todo.append((partial(self.leave, through, offsets, spec, hop, step), self.take))

    def leave(self, through, offsets, spec, hop, step):
        leaving = offsets
        if self.value is not None:
            leaving = leaving + jnp.einsum(spec, through, self.value, preferred_element_type=F32)
        return lax.ppermute(leaving.astype(LOW), "seq", [(hop, hop + step)])

    def take(self, came):
        return came if self.value is None else self.value + came


class AllSum(Mover):
    def __init__(self, values):
        super().__init__()
        self.value = values
        for axis in ("fsdp", "dp", "seq"):
            bits = bits_of(axis)
            if bits is None:
                self.value = lax.psum(self.value, axis)
            else:
                for bit in bits:
                    self.step(axis, bit)

    def step(self, axis, bit):
        self.todo.append(
            (lambda: swap(self.value, axis, bit), lambda came: self.value + came)
        )


def meet(movers, *arrays):
    movers = [mover for mover in movers if mover.pending is not None]
    count = len(arrays)
    out = lax.optimization_barrier(tuple(arrays) + tuple(mover.pending for mover in movers))
    for mover, came in zip(movers, out[count:]):
        mover.settle(came)
    return out[:count]


def begin(*movers):
    for mover in movers:
        mover.begin()


def put_together(mine, came, axis, bit):
    first = my_bit(axis, bit) == 0
    both = jnp.where(first, jnp.stack([mine, came]), jnp.stack([came, mine]))
    return both.reshape((2 * mine.shape[0],) + mine.shape[1:])


class ShardGather(Mover):
    def __init__(self, shard):
        super().__init__()
        if lax.axis_size("fsdp") != 4:
            self.value = lax.all_gather(shard, "fsdp", axis=0, tiled=True)
            return
        beside = swap(shard, "fsdp", 1)
        self.todo = [
            (lambda: swap(shard, "fsdp", 2), lambda came: came),
            (
                lambda: swap(self.value, "fsdp", 1),
                lambda came: assemble((shard, beside, self.value, came)),
            ),
        ]


def gather_halves(shard):
    count = lax.axis_size("dp")
    part = shard.reshape((count, shard.shape[0] // count) + shard.shape[1:])
    part = lax.dynamic_index_in_dim(part, lax.axis_index("dp"), 0, keepdims=False)
    return lax.all_gather(part, ("fsdp", "dp"), axis=0, tiled=True)


def gather_small(values):
    if lax.axis_size("fsdp") != 4:
        return lax.all_gather(values, "fsdp", axis=0)
    me = lax.axis_index("fsdp")
    rows = [values] + [swap(values, "fsdp", bit) for bit in (1, 2, 3)]
    out = jnp.zeros((4, values.shape[0]), values.dtype)
    for i, row in enumerate(rows):
        out = lax.dynamic_update_slice(out, row[None], (me ^ i, 0))
    return out


def assemble(pieces):
    rows, width = pieces[0].shape
    tiles = 1
    rows_at = rows // tiles

    def piece_at(i):
        def at(j, t, me):
            return (jnp.where(j == i, t, jnp.where(j < i, 0, tiles - 1)), 0)

        return pl.BlockSpec((rows_at, width), at)

    def kernel(me_ref, *refs):
        for i in range(4):

            @pl.when(pl.program_id(0) == i)
            def _():
                refs[4][...] = refs[i][...]

    return pl.pallas_call(
        kernel,
        grid_spec=pltpu.PrefetchScalarGridSpec(
            num_scalar_prefetch=1,
            grid=(4, tiles),
            in_specs=[piece_at(i) for i in range(4)],
            out_specs=pl.BlockSpec((rows_at, width), lambda j, t, me: ((me[0] ^ j) * tiles + t, 0)),
        ),
        out_shape=jax.ShapeDtypeStruct((4 * rows, width), pieces[0].dtype),
        compiler_params=pltpu.CompilerParams(
            dimension_semantics=("arbitrary", "arbitrary"), vmem_limit_bytes=48 * 2**20
        ),
        name="assemble",
    )(lax.axis_index("fsdp").astype(jnp.int32).reshape(1), *pieces)


def token_columns(log_decay, beta, seg_ids, rim_seg):
    seqs, count = seg_ids.shape
    order = jnp.arange(count, dtype=jnp.int32)
    ones = (order[:, None] >= order[None, :]).astype(F32)
    running = jnp.einsum("ts,bsh->hbt", ones, log_decay, precision=PRECISE)
    ids = jnp.broadcast_to(seg_ids.astype(F32)[None], running.shape)
    alive = (seg_ids == rim_seg[:, -1:]).astype(F32)[None]
    ending = (seg_ids == seg_ids[:, -1:]).astype(F32)[None]
    start = jnp.exp(running) * alive
    end = jnp.exp(running[:, :, -1:] - running) * ending
    padded_ids = jnp.concatenate([rim_seg, seg_ids], axis=1)
    keeps = [
        jnp.broadcast_to(
            (padded_ids[:, tap : tap + count] == seg_ids).astype(F32)[None], running.shape
        )
        for tap in range(CONV - 1)
    ]
    betas = jnp.transpose(beta, (2, 0, 1))
    cols = jnp.stack([running, betas, start, end] + keeps + [ids], axis=-1)
    blank = jnp.zeros_like(running)
    rows = jnp.stack([running, ids] + [blank] * 6, axis=2)
    return cols, rows


def local(
    inputs,
    segment_ids,
    out_cotangent,
    mixer_gain,
    qkv_weight,
    gate_weight,
    decay_weight,
    conv_weight,
    decay_log,
    decay_bias,
    head_gain,
    out_weight,
    ffn_gain,
    ffn_in_weight,
    down_weight,
):
    batch, length, width = inputs.shape
    count = batch * length
    margin = CONV - 1
    group = lax.axis_size("fsdp")
    share = width // group
    small = jnp.concatenate(
        [
            mixer_gain,
            ffn_gain,
            head_gain,
            conv_weight.reshape(-1),
            decay_weight.reshape(-1),
        ]
    )
    small = gather_small(small)
    cuts = [mixer_gain.size, ffn_gain.size, head_gain.size, conv_weight.size, decay_weight.size]
    pieces, first = [], 0
    for size in cuts:
        pieces.append(small[:, first : first + size])
        first += size
    full_mixer_gain = pieces[0].reshape(-1).astype(F32)
    full_ffn_gain = pieces[1].reshape(-1).astype(F32)
    full_head_gain = pieces[2].reshape(1, -1).astype(F32)
    full_conv = jnp.transpose(pieces[3].reshape(group, CONV, -1), (1, 0, 2)).reshape(CONV, C3)
    full_conv = [of_group(full_conv.astype(F32), g) for g in range(GROUPS)]
    full_decay = pieces[4].reshape(width, 2 * H)
    packed = list(pack_groups(qkv_weight))
    gathers = [ShardGather(packed[0])]
    begin(gathers[0])
    full_gate = lax.all_gather(gate_weight, "fsdp", axis=0, tiled=True)
    full_down = gather_halves(down_weight)
    full_ffn_in = gather_halves(ffn_in_weight)

    rows_in = inputs.astype(F32).reshape(count, width)
    normed, pull_mixer_norm = jax.vjp(rms_norm, rows_in, full_mixer_gain)
    normed_low = normed.astype(LOW)
    edge = passed_along(inputs[:, length - margin :, :], "seq", 1).reshape(-1, width)
    edge = jnp.pad(edge, ((0, edge_rows(batch) - edge.shape[0]), (0, 0)))
    edge = rms_norm(edge.astype(F32), full_mixer_gain).astype(LOW)
    normed_all = jnp.concatenate([normed_low, edge], axis=0)
    decay_in = jnp.dot(normed_low, full_decay, preferred_element_type=F32).reshape(
        batch, length, 2 * H
    )
    rim_seg = passed_along(segment_ids[:, length - margin :], "seq", 1)
    rate = jnp.exp(decay_log)
    shifted_decay = decay_in[:, :, :H] + decay_bias
    log_decay = -rate * jax.nn.softplus(shifted_decay)
    beta = jax.nn.sigmoid(decay_in[:, :, H:])
    cols, rows = token_columns(log_decay, beta, segment_ids, rim_seg)
    heads = H // GROUPS
    made, states, pre_convs, full_qkv = [], [], [], []

    def mixer_group(g):
        weight = gathers[g].finish()
        full_qkv.append(weight)
        pre_convs.append(jnp.dot(normed_all, weight, preferred_element_type=F32).astype(LOW))
        made.append(mixer_forward(pre_convs[g], full_conv[g], cols, rows, g * heads, heads))
        states.append(Chain(made[g][4], made[g][5], "hsij,hsjv->hsiv", 1))

    def head_group(g, kept):
        _, _, local_part, carried, _, _ = made[g]
        state = states[g].finish()
        return heads_forward(
            local_part, carried, state, gate_out, full_head_gain, g * heads, kept
        )

    normed_all, cols, packed[1] = meet([gathers[0]], normed_all, cols, packed[1])
    gathers.append(ShardGather(packed[1]))
    begin(*gathers)
    mixer_group(0)
    begin(states[0])
    normed_all, packed[2], _ = meet([gathers[1]], normed_all, packed[2], made[0][1])
    gathers.append(ShardGather(packed[2]))
    begin(*gathers)
    mixer_group(1)
    begin(states[1])
    normed_all, out_shard, _ = meet([gathers[2], states[0]], normed_all, out_weight, made[1][1])
    gathers.append(ShardGather(out_shard))
    begin(gathers[2], states[0], gathers[3])
    mixer_group(2)
    begin(states[2])
    normed_gate, _ = meet([states[0], states[1]], normed_low, made[2][1])
    begin(states[0], states[1])
    gate_out = jnp.dot(normed_gate, full_gate, preferred_element_type=F32)
    (gate_out,) = meet([states[0], states[1], states[2], gathers[3]], gate_out)
    begin(states[1], states[2], gathers[3])
    gate_out = gate_out.reshape(batch, length, VD)
    heads_low = head_group(0, None)
    (heads_low,) = meet([states[1], states[2], gathers[3]], heads_low)
    begin(states[2])
    heads_low = head_group(1, heads_low)
    full_out = gathers[3].finish()
    (heads_low,) = meet([states[2]], heads_low)
    heads_low = head_group(2, heads_low)
    heads_low = heads_low.reshape(count, VD)
    middle = rows_in + jnp.dot(heads_low, full_out, preferred_element_type=F32)
    normed_ffn, pull_ffn_norm = jax.vjp(rms_norm, middle, full_ffn_gain)
    normed_ffn_low = normed_ffn.astype(LOW)
    grad_rows = out_cotangent.reshape(count, width)
    hidden_low, grad_gate_up_low = ffn_middle(normed_ffn_low, full_ffn_in, grad_rows, full_down)
    grad_in = jnp.einsum(
        "rd,rf->df", normed_ffn_low, grad_gate_up_low, preferred_element_type=F32
    )
    grad_gate_up_low, grad_in = meet([], grad_gate_up_low, grad_in.astype(LOW))
    r_in = ShardSum(grad_in, True)
    grad_normed_ffn = jnp.einsum(
        "rf,df->rd", grad_gate_up_low, full_ffn_in, preferred_element_type=F32
    )
    grad_middle_norm, grad_ffn_gain = pull_ffn_norm(grad_normed_ffn)
    grad_middle = grad_rows.astype(F32) + grad_middle_norm
    grad_branch = grad_middle.astype(LOW)
    grad_heads = jnp.einsum("rd,vd->rv", grad_branch, full_out, preferred_element_type=F32)
    grad_heads = grad_heads.reshape(batch, length, VD)
    back, grad_states = [], []

    def heads_back(g, grad, kept):
        _, _, local_part, carried, _, _ = made[g]
        back.append(
            heads_backward(
                local_part, carried, states[g].value, gate_out, full_head_gain, grad,
                g * heads, kept,
            )
        )
        grad_states.append(Chain(made[g][4], back[g][3], "hsji,hsjv->hsiv", -1))
        begin(grad_states[g])
        return back[g][1]

    kept = heads_back(0, grad_heads, None)
    grad_heads, kept = meet([], grad_heads, kept)
    kept = heads_back(1, grad_heads, kept)
    grad_heads, kept = meet([grad_states[0]], grad_heads, kept)
    begin(grad_states[0])
    grad_gate_low = heads_back(2, grad_heads, kept)
    hidden_late, heads_late, grad_gate_low = meet(
        [grad_states[0], grad_states[1]], hidden_low, heads_low, grad_gate_low
    )
    begin(grad_states[0], grad_states[1])
    grad_down = jnp.einsum("rf,rd->fd", hidden_late, grad_rows, preferred_element_type=F32)
    heads_late, grad_down, grad_gate_low = meet(
        grad_states, heads_late, grad_down.astype(LOW), grad_gate_low
    )
    p_down = scatter(grad_down)
    begin(grad_states[1], grad_states[2])
    grad_gate_low = grad_gate_low.reshape(count, VD)
    grad_out = jnp.einsum("rv,rd->vd", heads_late, grad_branch, preferred_element_type=F32)
    grad_gate = jnp.einsum("rd,rc->dc", normed_low, grad_gate_low, preferred_element_type=F32)
    mixed_a, grad_out, grad_gate, r_in.value = meet(
        [grad_states[1], grad_states[2]],
        back[0][0], grad_out.astype(LOW), grad_gate.astype(LOW), r_in.value,
    )
    p_out = scatter(grad_out)
    r_gate = ShardSum(grad_gate)
    begin(grad_states[2], r_gate, r_in)

    run = heads * HEAD

    def mixer_back(g, grad_mixed, place, width, kept):
        t, uw, _, _, _, _ = made[g]
        return mixer_backward(
            pre_convs[g], full_conv[g], cols, rows, t, uw, states[g].value, grad_mixed,
            grad_states[g].finish(), g * heads, place, width, width, kept,
        )

    def rim_swap(grad_rim):
        return passed_along(grad_rim[:, RIM - margin :, :].astype(LOW), "seq", -1)

    def with_rim(grad_pre, came, grad_tail):
        grad_tail = (grad_tail[:, RIM - margin :, :] + came.astype(F32)).astype(LOW)
        grad_pre = lax.dynamic_update_slice(grad_pre, grad_tail, (0, length - margin, 0))
        return grad_pre.reshape(count, grad_pre.shape[2])

    def weight_grad(grad):
        return jnp.einsum("rd,rc->dc", normed_low, grad, preferred_element_type=F32).astype(LOW)

    def normed_part(grad, weight):
        return jnp.einsum("rc,dc->rd", grad, weight, preferred_element_type=F32)

    got_a = mixer_back(0, mixed_a, 0, 2 * run, [])
    mixed_b, *kept = meet([grad_states[2], r_gate, r_in], back[1][0], *got_a[:3])
    begin(r_gate, r_in)
    got_b = mixer_back(1, mixed_b, 1, 2 * run, kept)
    mixed_c, pre_ab, rim_ab, tail_ab, grad_gate_low = meet(
        [r_gate], back[2][0], *got_b[:3], grad_gate_low
    )
    begin(r_gate)
    came_ab = rim_swap(rim_ab)
    grad_normed = normed_part(grad_gate_low, full_gate)
    pre_ab, came_ab, tail_ab, grad_normed = meet([], pre_ab, came_ab, tail_ab, grad_normed)
    pre_ab = with_rim(pre_ab, came_ab, tail_ab)
    grad_ab = weight_grad(pre_ab)
    mixed_c, grad_ab = meet([r_in, r_gate], mixed_c, grad_ab)
    sum_ab = ShardSum(grad_ab)
    begin(sum_ab, r_in, r_gate)
    got_c = mixer_back(2, mixed_c, 0, run, [])
    pre_c, rim_c, tail_c, pre_ab, grad_normed = meet(
        [sum_ab, r_in, r_gate], *got_c[:3], pre_ab, grad_normed
    )
    begin(sum_ab, r_in, r_gate)
    came_c = rim_swap(rim_c)
    grad_normed = grad_normed + normed_part(pre_ab[:, :run], full_qkv[0])
    pre_c, came_c, tail_c, grad_normed = meet([], pre_c, came_c, tail_c, grad_normed)
    pre_c = with_rim(pre_c, came_c, tail_c)
    grad_c = weight_grad(pre_c)
    grad_c, grad_normed, p_down, p_out = meet([r_gate], grad_c, grad_normed, p_down, p_out)
    sum_c = ShardSum(grad_c)
    r_late = ShardSum(jnp.concatenate([p_down, p_out], axis=0), ready=True)
    begin(sum_c, r_late, r_gate)
    grad_normed = grad_normed + normed_part(pre_ab[:, run:], full_qkv[1])
    grad_normed, pre_c = meet([sum_ab, sum_c, r_late, r_gate, r_in], grad_normed, pre_c)
    begin(sum_ab, sum_c, r_late, r_gate)
    grad_normed = grad_normed + normed_part(pre_c, full_qkv[2])
    made_late = [item for got in (got_a, got_b, got_c) for item in got[3:5]]
    hidden_late, grad_normed, *made_late = meet(
        [sum_ab, sum_c, r_late, r_gate], hidden_late, grad_normed, *made_late, *[item[2] for item in back]
    )
    made_late, head_gains = made_late[: 2 * GROUPS], made_late[2 * GROUPS :]
    grad_head_gain = sum(jnp.sum(item, axis=(0, 1)) for item in head_gains)
    begin(sum_ab, sum_c, r_late)
    result = middle + jnp.dot(hidden_late, full_down, preferred_element_type=F32)
    output = result.astype(LOW).reshape(batch, length, width)
    grad_cols = jnp.concatenate(made_late[1::2], axis=0)
    conv_parts = made_late[::2]
    spans = [0, heads * DK, 2 * heads * DK, heads * HEAD]
    grad_conv = jnp.concatenate(
        [part[:, low:top] for low, top in zip(spans, spans[1:]) for part in conv_parts], axis=1
    )
    grad_log_decay = jnp.transpose(grad_cols[:, :, 0, :], (1, 2, 0))
    grad_decay_b = jnp.transpose(grad_cols[:, :, 1, :], (1, 2, 0))
    grad_decay_a = grad_log_decay * (-rate) * jax.nn.sigmoid(shifted_decay)
    grad_decay_bias = jnp.sum(grad_decay_a, axis=(0, 1))
    grad_decay_log = jnp.sum(grad_log_decay * log_decay, axis=(0, 1))
    grad_decay_low = jnp.concatenate([grad_decay_a, grad_decay_b], axis=-1).astype(LOW)
    grad_decay_low = grad_decay_low.reshape(count, 2 * H)
    grad_decay = jnp.einsum("rd,rc->dc", normed_low, grad_decay_low, preferred_element_type=F32)
    grad_normed = grad_normed + jnp.einsum(
        "rc,dc->rd", grad_decay_low, full_decay, preferred_element_type=F32
    )
    grad_rows_norm, grad_mixer_gain = pull_mixer_norm(grad_normed)
    input_grad = (grad_middle + grad_rows_norm).astype(LOW).reshape(batch, length, width)

    little = (
        grad_mixer_gain,
        grad_ffn_gain,
        grad_head_gain,
        grad_conv.reshape(-1),
        grad_decay.reshape(-1),
        grad_decay_log,
        grad_decay_bias,
    )
    small_grads = jnp.concatenate(little)
    movers = [r_in, r_gate, sum_ab, sum_c, r_late]
    (small_grads,) = meet(movers, small_grads)
    all_sum = AllSum(small_grads)
    movers.append(all_sum)
    while any(mover.todo for mover in movers):
        begin(*movers)
        meet(movers, small_grads)
    flat = all_sum.value
    sum_qkv = unpack_groups(sum_ab.value, sum_c.value)
    late = r_late.value.reshape(-1, p_down.shape[0] + p_out.shape[0], width)
    sum_down = late[:, : p_down.shape[0]].reshape(-1, width)
    sum_out = late[:, p_down.shape[0] :].reshape(-1, width)
    parts, first = [], 0
    for item in little:
        parts.append(flat[first : first + item.size])
        first += item.size
    place = lax.axis_index("fsdp")

    def own(values, axis=0):
        size = values.shape[axis] // group
        return lax.dynamic_slice_in_dim(values, place * size, size, axis)

    return (
        output,
        input_grad,
        own(parts[0]),
        sum_qkv,
        r_gate.value.astype(F32),
        own(parts[4].reshape(width, 2 * H)),
        own(parts[3].reshape(CONV, C3), 1),
        parts[5],
        parts[6],
        own(parts[2]),
        sum_out.astype(F32),
        own(parts[1]),
        r_in.value.astype(F32),
        sum_down.astype(F32),
    )


def solution(mesh):
    rows = P(("dp", "fsdp"), "seq", None)
    split = P("fsdp", None)
    placed = (
        rows,
        P(("dp", "fsdp"), "seq"),
        rows,
        P("fsdp"),
        split,
        split,
        split,
        P(None, "fsdp"),
        P(),
        P(),
        P("fsdp"),
        split,
        P("fsdp"),
        split,
        split,
    )
    return jax.shard_map(
        local,
        mesh=mesh,
        in_specs=placed,
        out_specs=(
            rows,
            rows,
            P("fsdp"),
            split,
            split,
            split,
            P(None, "fsdp"),
            P(),
            P(),
            P("fsdp"),
            split,
            P("fsdp"),
            split,
            split,
        ),
        check_vma=False,
    )
```

```python
from functools import partial

import jax
import jax.numpy as jnp
from jax import lax
from jax.experimental import pallas as pl
from jax.experimental.pallas import tpu as pltpu
from jax.sharding import PartitionSpec as P

H = 6
DK = 128
DV = 256
CONV = 4
KD = 768
VD = 1536
C3 = 3072
RIM = 8
HEAD = 2 * DK + DV
GROUPS = 3

EPSILON = 1e-06
HEAD_EPSILON = 0.001
PRECISE = lax.Precision.HIGHEST
LOW = jnp.bfloat16
F32 = jnp.float32

NN = (((1,), (0,)), ((), ()))
NT = (((1,), (1,)), ((), ()))
TN = (((0,), (0,)), ((), ()))


def mm(left, right, dims=NN):
    return lax.dot_general(
        left.astype(LOW), right.astype(LOW), dims, preferred_element_type=F32
    )


def passed_along(value, axis, steps):
    count = lax.axis_size(axis)
    leading, last = (max(0, -steps), min(count, count - steps))
    return lax.ppermute(value, axis, [(source, source + steps) for source in range(leading, last)])


def rms_norm(values, gain):
    return values * lax.rsqrt(jnp.mean(values * values, axis=-1, keepdims=True) + EPSILON) * gain


def iotas(count):
    shape = (count, count)
    return lax.broadcasted_iota(jnp.int32, shape, 0), lax.broadcasted_iota(jnp.int32, shape, 1)


def conv_head(s, parts, rims, taps, cols, pad_ref):
    count = pad_ref.shape[1] - RIM
    margin = CONV - 1
    at = 0
    for part, rim in zip(parts, rims):
        width = part.shape[-1]
        pad_ref[s, RIM:, at : at + width] = part[s * count : (s + 1) * count, :].astype(F32)
        edge = rim[...].astype(F32)[margin * s : margin * (s + 1), :]
        pad_ref[s, RIM - margin : RIM, at : at + width] = edge
        at += width
    shifted = []
    total = None
    for tap in range(CONV):
        first = RIM - margin + tap
        values = pad_ref[s, first : first + count, :]
        if tap < margin:
            values = values * cols[:, 4 + tap : 5 + tap]
        shifted.append(values)
        term = values * taps[tap : tap + 1, :]
        total = term if total is None else total + term
    sig = jax.nn.sigmoid(total)
    return shifted, total, sig, total * sig


def unit(values):
    scale = lax.rsqrt(jnp.sum(values * values, axis=-1, keepdims=True) + EPSILON)
    return values * scale, scale


def decays(cols, rows, order, other):
    causal = (cols[:, 7:8] == rows[1:2, :]) & (order >= other)
    decay = jnp.exp(jnp.where(causal, cols[:, 0:1] - rows[0:1, :], -1e30))
    return decay, jnp.where(order > other, decay, 0.0)


def forward_kernel(
    q_ref, k_ref, v_ref, rq_ref, rk_ref, rv_ref, wq_ref, wk_ref, wv_ref, cols_ref, rows_ref,
    t_ref, uw_ref, local_ref, carried_ref,
    through_ref, offsets_ref, pad_ref,
):
    seqs, count = cols_ref.shape[1], cols_ref.shape[2]
    order, other = iotas(count)
    taps = jnp.concatenate([wq_ref[...], wk_ref[...], wv_ref[...]], axis=1)
    state = []
    for s in range(seqs):
        cols, rows = cols_ref[0, s], rows_ref[0, s]
        _, _, _, out = conv_head(
            s, (q_ref, k_ref, v_ref), (rq_ref, rk_ref, rv_ref), taps, cols, pad_ref
        )
        query = (unit(out[:, :DK])[0] * DK ** (-0.5)).astype(LOW)
        key = unit(out[:, DK : 2 * DK])[0].astype(LOW)
        value = out[:, 2 * DK :].astype(LOW)
        decay, strict = decays(cols, rows, order, other)
        beta, start, end = cols[:, 1:2], cols[:, 2:3], cols[:, 3:4]
        lower = beta * mm(key, key, NT) * strict
        attend = (mm(query, key, NT) * decay).astype(LOW)
        keyf = key.astype(F32)
        target = jnp.concatenate([beta * value.astype(F32), beta * start * keyf], axis=1).astype(LOW)
        state.append(dict(lower=lower, attend=attend, target=target, query=query,
                          ending=(end * keyf).astype(LOW), start=start))
    inverse, lowers = [], []
    joined = order ^ other
    eye = (joined == 0).astype(LOW)
    for x in state:
        lower = x["lower"].astype(LOW)
        lowers.append(lower)
        inverse.append(eye - lower * ((joined == 1) & (order > other)).astype(LOW))
    level = 1
    while (4 << level) <= count:
        pick = ((joined >> level) == 1).astype(LOW)
        half = [mm(lowers[s] * pick, inverse[s]).astype(LOW) for s in range(seqs)]
        for s in range(seqs):
            inverse[s] = inverse[s] - mm(inverse[s], half[s]).astype(LOW)
        level += 1
    mid = count // 2
    corner = [mm(lowers[s][mid:, :mid], inverse[s][:mid, :mid]) for s in range(seqs)]
    blank = jnp.zeros((mid, mid), LOW)
    for s in range(seqs):
        left = mm(inverse[s][mid:, mid:], corner[s]).astype(LOW)
        inverse[s] = jnp.concatenate(
            [
                jnp.concatenate([inverse[s][:mid, :mid], blank], axis=1),
                jnp.concatenate([-left, inverse[s][mid:, mid:]], axis=1),
            ],
            axis=0,
        )
    for s in range(seqs):
        x = state[s]
        t = inverse[s]
        t_ref[0, s] = t
        uw = mm(t, x["target"]).astype(LOW)
        uw_ref[0, s] = uw
        both = mm(x["attend"], uw)
        local_ref[s] = both[:, :DV]
        carried_ref[s] = (x["start"] * x["query"].astype(F32) - both[:, DV:]).astype(LOW)
        ends = mm(x["ending"], uw, TN)
        offsets_ref[0, s] = ends[:, :DV]
        small, small_other = iotas(DK)
        last = x["start"][count - 1 : count, :]
        through_ref[0, s] = (jnp.where(small == small_other, last, 0.0) - ends[:, DV:]).astype(LOW)


def heads_kernel(local_ref, carried_ref, state_ref, gate_ref, gain_ref, heads_ref):
    for s in range(local_ref.shape[0]):
        mixed = local_ref[s] + mm(carried_ref[s], state_ref[0, s])
        scale = lax.rsqrt(jnp.mean(mixed * mixed, axis=-1, keepdims=True) + HEAD_EPSILON)
        gate = gate_ref[s]
        heads_ref[s] = (mixed * scale * gain_ref[...] * (gate * jax.nn.sigmoid(gate))).astype(LOW)


def heads_back_kernel(
    local_ref, carried_ref, state_ref, gate_ref, gain_ref, grad_ref,
    mixed_ref, ggate_ref, ggain_ref, gstate_ref,
):
    gain = gain_ref[...]
    total = jnp.zeros_like(gain)
    for s in range(local_ref.shape[0]):
        mixed = local_ref[s] + mm(carried_ref[s], state_ref[0, s])
        scale = lax.rsqrt(jnp.mean(mixed * mixed, axis=-1, keepdims=True) + HEAD_EPSILON)
        normed = mixed * scale
        gate = gate_ref[s]
        sig = jax.nn.sigmoid(gate)
        act = gate * sig
        grad = grad_ref[s]
        gn = grad * normed
        total = total + jnp.sum(gn * act, axis=0, keepdims=True)
        ggate_ref[s] = (gn * gain * (sig + act * (1.0 - sig))).astype(LOW)
        e = grad * gain * act
        gmixed = (scale * (e - normed * jnp.mean(e * normed, axis=-1, keepdims=True))).astype(LOW)
        mixed_ref[s] = gmixed
        gstate_ref[0, s] = mm(carried_ref[s], gmixed, TN)
    ggain_ref[0] = total


def backward_kernel(
    q_ref, k_ref, v_ref, rq_ref, rk_ref, rv_ref, wq_ref, wk_ref, wv_ref, cols_ref, rows_ref,
    t_ref, uw_ref, state_ref, gout_ref, gend_ref,
    gpre_ref, grim_ref, gtail_ref, gtaps_ref, gcols_ref, pad_ref, shift_ref,
):
    seqs, count = cols_ref.shape[1], cols_ref.shape[2]
    order, other = iotas(count)
    taps = jnp.concatenate([wq_ref[...], wk_ref[...], wv_ref[...]], axis=1)
    before = (order < other).astype(LOW)
    head, heads = pl.program_id(0), pl.num_programs(0)
    at = (
        pl.ds(pl.multiple_of(head * DK, DK), DK),
        pl.ds(pl.multiple_of((heads + head) * DK, DK), DK),
        pl.ds(pl.multiple_of(2 * heads * DK + head * DV, DV), DV),
    )
    spans = ((0, DK), (DK, 2 * DK), (2 * DK, HEAD))
    gtaps = [None] * CONV
    for s in range(seqs):
        cols, rows = cols_ref[0, s], rows_ref[0, s]
        shifted, total, sig, out = conv_head(
            s, (q_ref, k_ref, v_ref), (rq_ref, rk_ref, rv_ref), taps, cols, pad_ref
        )
        qhat, qscale = unit(out[:, :DK])
        khat, kscale = unit(out[:, DK : 2 * DK])
        query = (qhat * DK ** (-0.5)).astype(LOW)
        key = khat.astype(LOW)
        value = out[:, 2 * DK :]
        decay, strict = decays(cols, rows, order, other)
        beta, start, end = cols[:, 1:2], cols[:, 2:3], cols[:, 3:4]
        keyf = key.astype(F32)
        weight = beta * strict
        lower = mm(key, key, NT) * weight
        attend = mm(query, key, NT) * decay
        state = state_ref[0, s]
        gend = gend_ref[0, s]
        gout = gout_ref[s]
        uw = uw_ref[0, s]
        fresh = uw[:, :DV].astype(F32) - mm(uw[:, DV:], state)
        freshl = fresh.astype(LOW)
        gfresh = mm(attend, gout, TN) + mm(end * keyf, gend)
        gtarget = mm(t_ref[0, s], gfresh, TN)
        gattend = mm(gout, freshl, NT)
        glower = -mm(gtarget, freshl, NT)
        cross = gattend * attend + glower * lower
        high = cross.astype(LOW)
        reach = mm(high, before) + mm(cross - high.astype(F32), before)
        gqk = (gattend * decay).astype(LOW)
        gkk = (glower * weight).astype(LOW)
        gout_state = mm(gout, state, NT)
        gtarget_state = beta * mm(gtarget, state, NT)
        ends = mm(freshl, gend, NT)
        gquery = mm(gqk, key) + start * gout_state
        gkey = (
            mm(gqk, query, TN)
            + mm(gkk, key)
            + mm(gkk, key, TN)
            - start * gtarget_state
            + end * ends
        )
        gvalue = beta * gtarget
        from_start = start * jnp.sum(
            query.astype(F32) * gout_state - keyf * gtarget_state, axis=-1, keepdims=True
        )
        to_end = end * jnp.sum(keyf * ends, axis=-1, keepdims=True)
        through = jnp.sum(gend.astype(F32) * state.astype(F32)) * start[count - 1 : count, :]
        glog = jnp.sum(jnp.where(order >= other, reach + from_start, to_end), axis=0, keepdims=True)
        gbeta = jnp.sum(gtarget * fresh, axis=-1, keepdims=True) * (1.0 - beta)
        gbeta = jnp.sum(jnp.where(order == other, gbeta, 0.0), axis=0, keepdims=True)
        gcols_ref[0, s] = jnp.concatenate(
            [glog + through, gbeta, jnp.zeros((6, count), F32)], axis=0
        )
        gq = gquery * DK ** (-0.5)
        gq = qscale * (gq - qhat * jnp.sum(qhat * gq, axis=-1, keepdims=True))
        gk = kscale * (gkey - khat * jnp.sum(khat * gkey, axis=-1, keepdims=True))
        gconv = jnp.concatenate([gq, gk, gvalue], axis=1) * (sig + out * (1.0 - sig))
        for tap in range(CONV):
            part = jnp.sum(gconv * shifted[tap], axis=0, keepdims=True)
            gtaps[tap] = part if gtaps[tap] is None else gtaps[tap] + part
        width = gconv.shape[1]
        blank = jnp.zeros((RIM, width), F32)
        back = None
        for tap in range(CONV):
            term = gconv * taps[tap : tap + 1, :]
            if tap < CONV - 1:
                term = term * cols[:, 4 + tap : 5 + tap]
            shift_ref[tap, 0:RIM, :] = blank
            shift_ref[tap, RIM : RIM + count, :] = term
            shift_ref[tap, RIM + count :, :] = blank
            first = CONV - 1 - tap
            moved = shift_ref[tap, first : first + RIM + count, :]
            back = moved if back is None else back + moved
        for place, (low, top) in zip(at, spans):
            gpre_ref[s, :, place] = back[RIM:, low:top].astype(LOW)
            grim_ref[s, :, place] = back[:RIM, low:top]
            gtail_ref[s, :, place] = back[count:, low:top]
    gtaps = jnp.concatenate(gtaps, axis=0)
    for place, (low, top) in zip(at, spans):
        gtaps_ref[:, place] = gtaps[:, low:top]


def per_head(seqs, rows, width, first=0):
    return pl.BlockSpec((1, seqs, rows, width), lambda h: (first + h, 0, 0, 0))


def by_column(seqs, count, width, first=0):
    return pl.BlockSpec((seqs, count, width), lambda h: (0, 0, first + h))


def head_specs(seqs, count, first, heads):
    def cut(rows, row, width, column):
        return pl.BlockSpec((rows, width), lambda h: (row, column + h))

    rows, edge = seqs * count, edge_rows(seqs)
    late = 2 * heads * DK // DV
    specs = [cut(rows, 0, DK, 0), cut(rows, 0, DK, heads), cut(rows, 0, DV, late)]
    at = rows // edge
    specs += [cut(edge, at, DK, 0), cut(edge, at, DK, heads), cut(edge, at, DV, late)]
    specs += [cut(CONV, 0, DK, 0), cut(CONV, 0, DK, heads), cut(CONV, 0, DV, late)]
    return specs + [per_head(seqs, count, 8, first), per_head(seqs, 8, count, first)]


def edge_rows(seqs):
    return -(-seqs * (CONV - 1) // 16) * 16


def whole(*shape):
    return pl.BlockSpec(shape, lambda h: (0,) * len(shape))


def params(limit=48):
    return pltpu.CompilerParams(
        dimension_semantics=("arbitrary",), vmem_limit_bytes=limit * 2**20
    )


def mixer_forward(pre_conv, taps, cols, rows, first, heads):
    seqs, count = cols.shape[1], cols.shape[2]
    return pl.pallas_call(
        forward_kernel,
        grid=(heads,),
        in_specs=head_specs(seqs, count, first, heads),
        out_specs=[
            per_head(seqs, count, count),
            per_head(seqs, count, DV + DK),
            by_column(seqs, count, DV),
            by_column(seqs, count, DK),
            per_head(seqs, DK, DK),
            per_head(seqs, DK, DV),
        ],
        out_shape=[
            jax.ShapeDtypeStruct((heads, seqs, count, count), LOW),
            jax.ShapeDtypeStruct((heads, seqs, count, DV + DK), LOW),
            jax.ShapeDtypeStruct((seqs, count, heads * DV), F32),
            jax.ShapeDtypeStruct((seqs, count, heads * DK), LOW),
            jax.ShapeDtypeStruct((heads, seqs, DK, DK), LOW),
            jax.ShapeDtypeStruct((heads, seqs, DK, DV), F32),
        ],
        scratch_shapes=[pltpu.VMEM((seqs, RIM + count, HEAD), F32)],
        compiler_params=params(),
        name="mixer_forward",
    )(*[pre_conv] * 6, *[taps] * 3, cols, rows)


def heads_forward(local_part, carried, state, gate, gain, first, kept):
    seqs, count = local_part.shape[0], local_part.shape[1]
    heads = state.shape[0]
    operands = [local_part, carried, state, gate, gain]
    in_specs = [
        by_column(seqs, count, DV),
        by_column(seqs, count, DK),
        per_head(seqs, DK, DV),
        by_column(seqs, count, DV, first),
        pl.BlockSpec((1, DV), lambda h: (0, 0)),
    ]
    aliases = {}
    if kept is not None:
        operands.append(kept)
        in_specs.append(pl.BlockSpec(memory_space=pl.ANY))
        aliases = {5: 0}

    def kernel(*refs):
        heads_kernel(*refs[:5], refs[-1])

    return pl.pallas_call(
        kernel,
        grid=(heads,),
        in_specs=in_specs,
        out_specs=by_column(seqs, count, DV, first),
        out_shape=jax.ShapeDtypeStruct((seqs, count, VD), LOW),
        input_output_aliases=aliases,
        compiler_params=params(),
        name="heads_forward",
    )(*operands)


def heads_backward(local_part, carried, state, gate, gain, grad, first, kept):
    seqs, count = local_part.shape[0], local_part.shape[1]
    heads = state.shape[0]
    operands = [local_part, carried, state, gate, gain, grad]
    in_specs = [
        by_column(seqs, count, DV),
        by_column(seqs, count, DK),
        per_head(seqs, DK, DV),
        by_column(seqs, count, DV, first),
        pl.BlockSpec((1, DV), lambda h: (0, 0)),
        by_column(seqs, count, DV, first),
    ]
    aliases = {}
    if kept is not None:
        operands.append(kept)
        in_specs.append(pl.BlockSpec(memory_space=pl.ANY))
        aliases = {6: 1}

    def kernel(*refs):
        heads_back_kernel(*refs[:6], *refs[-4:])

    return pl.pallas_call(
        kernel,
        grid=(heads,),
        in_specs=in_specs,
        out_specs=[
            by_column(seqs, count, DV),
            by_column(seqs, count, DV, first),
            pl.BlockSpec((1, 1, DV), lambda h: (h, 0, 0)),
            per_head(seqs, DK, DV),
        ],
        out_shape=[
            jax.ShapeDtypeStruct((seqs, count, heads * DV), LOW),
            jax.ShapeDtypeStruct((seqs, count, VD), LOW),
            jax.ShapeDtypeStruct((heads, 1, DV), F32),
            jax.ShapeDtypeStruct((heads, seqs, DK, DV), F32),
        ],
        input_output_aliases=aliases,
        compiler_params=params(),
        name="heads_backward",
    )(*operands)


def mixer_backward(
    pre_conv, taps, cols, rows, t, uw, state, gout, gend, first, place, width, rims, kept
):
    seqs, count = cols.shape[1], cols.shape[2]
    heads = state.shape[0]
    run = heads * HEAD

    def at(*shape):
        return pl.BlockSpec(shape, lambda h: (0, 0, place))

    operands = [*[pre_conv] * 6, *[taps] * 3, cols, rows, t, uw, state, gout, gend]
    inputs = len(operands)
    aliases = {inputs + i: i for i in range(len(kept))}

    def kernel(*refs):
        backward_kernel(*refs[:inputs], *refs[inputs + len(kept) :])

    return pl.pallas_call(
        kernel,
        grid=(heads,),
        in_specs=head_specs(seqs, count, first, heads)
        + [
            per_head(seqs, count, count),
            per_head(seqs, count, DV + DK),
            per_head(seqs, DK, DV),
            by_column(seqs, count, DV),
            per_head(seqs, DK, DV),
        ]
        + [pl.BlockSpec(memory_space=pl.ANY)] * len(kept),
        out_specs=[
            at(seqs, count, run),
            at(seqs, RIM, run),
            at(seqs, RIM, run),
            whole(CONV, run),
            per_head(seqs, 8, count),
        ],
        out_shape=[
            jax.ShapeDtypeStruct((seqs, count, width), LOW),
            jax.ShapeDtypeStruct((seqs, RIM, rims), F32),
            jax.ShapeDtypeStruct((seqs, RIM, rims), F32),
            jax.ShapeDtypeStruct((CONV, run), F32),
            jax.ShapeDtypeStruct((heads, seqs, 8, count), F32),
        ],
        scratch_shapes=[
            pltpu.VMEM((seqs, RIM + count, HEAD), F32),
            pltpu.VMEM((CONV, 2 * RIM + count, HEAD), F32),
        ],
        input_output_aliases=aliases,
        compiler_params=params(),
        name="mixer_backward",
    )(*operands, *kept)


def ffn_kernel(x_ref, up_ref, side_ref, grad_ref, down_ref, hidden_ref, back_ref):
    tile = up_ref.shape[1]
    half = back_ref.shape[1] // 2
    at = pl.program_id(0) * tile
    rows = x_ref.shape[0]
    step = 256 if rows % 256 == 0 else rows

    def part(i, _):
        here = pl.ds(pl.multiple_of(i * step, step), step)
        x = x_ref[here, :]
        a = mm(x, up_ref[...])
        b = mm(x, side_ref[...])
        grad = mm(grad_ref[here, :], down_ref[...], NT)
        sig = jax.nn.sigmoid(a)
        act = a * sig
        hidden_ref[here, :] = (act * b).astype(LOW)
        first = grad * b * (sig + act * (1.0 - sig))
        back_ref[here, pl.ds(pl.multiple_of(at, tile), tile)] = first.astype(LOW)
        back_ref[here, pl.ds(pl.multiple_of(half + at, tile), tile)] = (grad * act).astype(LOW)
        return 0

    lax.fori_loop(0, rows // step, part, 0)


def ffn_middle(x, weight, grad, down):
    rows, width = x.shape
    units = down.shape[0]
    tile = 256
    tiles = units // tile
    return pl.pallas_call(
        ffn_kernel,
        grid=(tiles,),
        in_specs=[
            pl.BlockSpec((rows, width), lambda j: (0, 0)),
            pl.BlockSpec((width, tile), lambda j: (0, j)),
            pl.BlockSpec((width, tile), lambda j: (0, tiles + j)),
            pl.BlockSpec((rows, width), lambda j: (0, 0)),
            pl.BlockSpec((tile, width), lambda j: (j, 0)),
        ],
        out_specs=[
            pl.BlockSpec((rows, tile), lambda j: (0, j)),
            pl.BlockSpec((rows, 2 * units), lambda j: (0, 0)),
        ],
        out_shape=[
            jax.ShapeDtypeStruct((rows, units), LOW),
            jax.ShapeDtypeStruct((rows, 2 * units), LOW),
        ],
        compiler_params=params(),
        name="ffn_middle",
    )(x, weight, weight, grad, down)


def group_cuts(g):
    heads = H // GROUPS
    return (
        (g * heads * DK, heads * DK),
        (KD + g * heads * DK, heads * DK),
        (2 * KD + g * heads * DV, heads * DV),
    )


def of_group(values, g):
    return jnp.concatenate([values[:, at : at + size] for at, size in group_cuts(g)], axis=1)


def pack_groups(weight):
    rows = weight.shape[0]
    width = C3 // GROUPS

    def kernel(weight_ref, *outs):
        for g, out in enumerate(outs):
            first = 0
            for at, size in group_cuts(g):
                out[:, first : first + size] = weight_ref[:, at : at + size]
                first += size

    return pl.pallas_call(
        kernel,
        out_shape=[jax.ShapeDtypeStruct((rows, width), weight.dtype)] * GROUPS,
        compiler_params=pltpu.CompilerParams(vmem_limit_bytes=48 * 2**20),
        name="pack_groups",
    )(weight)


def unpack_groups(first, last):
    rows = first.shape[0]
    run = C3 // GROUPS

    def kernel(first_ref, last_ref, qkv_ref):
        for g in range(GROUPS):
            part, at = (last_ref, 0) if g == GROUPS - 1 else (first_ref, g * run)
            for to, size in group_cuts(g):
                qkv_ref[:, to : to + size] = part[:, at : at + size].astype(F32)
                at += size

    return pl.pallas_call(
        kernel,
        out_shape=jax.ShapeDtypeStruct((rows, C3), F32),
        compiler_params=pltpu.CompilerParams(vmem_limit_bytes=48 * 2**20),
        name="unpack_groups",
    )(first, last)


def swap(values, axis, bit):
    count = lax.axis_size(axis)
    return lax.ppermute(values, axis, [(at, at ^ bit) for at in range(count)])


def my_bit(axis, bit):
    return (lax.axis_index(axis) // bit) % 2


def plus(left, right):
    return (left.astype(F32) + right.astype(F32)).astype(LOW)


def bits_of(axis):
    count, bits, bit = lax.axis_size(axis), [], 1
    while bit < count:
        bits.append(bit)
        bit *= 2
    return bits if bit == count else None


def split(values):
    return values.reshape((2, values.shape[0] // 2) + values.shape[1:])


class Mover:
    pending = None
    value = None

    def __init__(self):
        self.todo = []

    def begin(self):
        if self.todo:
            send, self.then = self.todo.pop(0)
            self.pending = send()
        return self

    def settle(self, came):
        self.pending = None
        self.value = self.then(came)

    def finish(self):
        while self.todo or self.pending is not None:
            if self.pending is None:
                self.begin()
            self.settle(self.pending)
        return self.value


def scattered_sums():
    return all(bits_of(axis) is not None for axis in ("fsdp", "dp", "seq"))


def scatter(grad):
    if not scattered_sums():
        shard = lax.psum_scatter(grad, "fsdp", scatter_dimension=0, tiled=True)
        return lax.psum(shard, ("dp", "seq"))
    return lax.psum_scatter(grad, ("fsdp", "dp"), scatter_dimension=0, tiled=True)


class ShardSum(Mover):
    def __init__(self, grad, scattered=False, ready=False):
        super().__init__()
        self.value = grad.astype(LOW)
        if ready and not scattered_sums():
            return
        self.plain = any(bits_of(axis) is None for axis in ("fsdp", "dp", "seq"))
        if self.plain:
            shard = lax.psum_scatter(self.value, "fsdp", scatter_dimension=0, tiled=True)
            self.value = lax.psum(shard, ("dp", "seq"))
            return
        if ready:
            scattered = True
        elif scattered:
            self.value = lax.psum_scatter(
                self.value, ("fsdp", "dp"), scatter_dimension=0, tiled=True
            )
        else:
            bits = bits_of("fsdp")
            self.value = self.value.reshape((2,) * len(bits) + (-1, grad.shape[1]))
            for at, bit in enumerate(bits):
                self.halved("fsdp", bit, len(bits) - 1 - at)
        undo = []
        for axis in ("dp", "seq"):
            bits = bits_of(axis)
            if axis == "dp" and scattered:
                undo += [(axis, bit) for bit in reversed(bits)]
                continue
            for bit in bits:
                if axis == "seq" and bit == bits[-1]:
                    self.added(axis, bit)
                else:
                    self.halved(axis, bit, None)
                    undo.append((axis, bit))
        for axis, bit in reversed(undo):
            self.joined(axis, bit)

    def halved(self, axis, bit, dim):
        def entries():
            return (split(self.value), 0) if dim is None else (self.value, dim)

        def send():
            values, at = entries()
            part = lax.dynamic_index_in_dim(values, 1 - my_bit(axis, bit), at, keepdims=False)
            return swap(part, axis, bit)

        def then(came):
            values, at = entries()
            part = lax.dynamic_index_in_dim(values, my_bit(axis, bit), at, keepdims=False)
            return plus(part, came)

        self.todo.append((send, then))

    def added(self, axis, bit):
        self.todo.append(
            (lambda: swap(self.value, axis, bit), lambda came: plus(self.value, came))
        )

    def joined(self, axis, bit):
        self.todo.append(
            (lambda: swap(self.value, axis, bit), lambda came: put_together(self.value, came, axis, bit))
        )


class Chain(Mover):
    def __init__(self, through, offsets, spec, step):
        super().__init__()
        last = lax.axis_size("seq") - 1
        for hop in range(last) if step > 0 else range(last, 0, -1):
            self.todo.append((partial(self.leave, through, offsets, spec, hop, step), self.take))

    def leave(self, through, offsets, spec, hop, step):
        leaving = offsets
        if self.value is not None:
            leaving = leaving + jnp.einsum(spec, through, self.value, preferred_element_type=F32)
        return lax.ppermute(leaving.astype(LOW), "seq", [(hop, hop + step)])

    def take(self, came):
        return came if self.value is None else self.value + came


class AllSum(Mover):
    def __init__(self, values):
        super().__init__()
        self.value = values
        for axis in ("fsdp", "dp", "seq"):
            count = lax.axis_size(axis)
            if bits_of(axis) is None or count > 4:
                self.value = lax.psum(self.value, axis)
            else:
                self.todo.append((partial(self.send, axis, count), self.take))

    def send(self, axis, count):
        return tuple(swap(self.value, axis, bit) for bit in range(1, count))

    def take(self, came):
        if len(came) == 1:
            return self.value + came[0]
        return (self.value + came[0]) + (came[1] + came[2])


def meet(movers, *arrays):
    movers = [mover for mover in movers if mover.pending is not None]
    arrays, came = lax.optimization_barrier((arrays, [mover.pending for mover in movers]))
    for mover, values in zip(movers, came):
        mover.settle(values)
    return arrays


def begin(*movers):
    for mover in movers:
        mover.begin()


def put_together(mine, came, axis, bit):
    first = my_bit(axis, bit) == 0
    both = jnp.where(first, jnp.stack([mine, came]), jnp.stack([came, mine]))
    return both.reshape((2 * mine.shape[0],) + mine.shape[1:])


class ShardGather(Mover):
    def __init__(self, shard):
        super().__init__()
        if lax.axis_size("fsdp") != 4:
            self.value = lax.all_gather(shard, "fsdp", axis=0, tiled=True)
            return
        beside = swap(shard, "fsdp", 1)
        self.todo = [
            (lambda: swap(shard, "fsdp", 2), lambda came: came),
            (
                lambda: swap(self.value, "fsdp", 1),
                lambda came: assemble((shard, beside, self.value, came)),
            ),
        ]


def gather_halves(shard):
    count = lax.axis_size("dp")
    part = shard.reshape((count, shard.shape[0] // count) + shard.shape[1:])
    part = lax.dynamic_index_in_dim(part, lax.axis_index("dp"), 0, keepdims=False)
    return lax.all_gather(part, ("fsdp", "dp"), axis=0, tiled=True)


def gather_small(values):
    if lax.axis_size("fsdp") != 4:
        return lax.all_gather(values, "fsdp", axis=0)
    me = lax.axis_index("fsdp")
    rows = [values] + [swap(values, "fsdp", bit) for bit in (1, 2, 3)]
    out = jnp.zeros((4, values.shape[0]), values.dtype)
    for i, row in enumerate(rows):
        out = lax.dynamic_update_slice(out, row[None], (me ^ i, 0))
    return out


def assemble(pieces):
    rows, width = pieces[0].shape
    tiles = 1
    rows_at = rows // tiles

    def piece_at(i):
        def at(j, t, me):
            return (jnp.where(j == i, t, jnp.where(j < i, 0, tiles - 1)), 0)

        return pl.BlockSpec((rows_at, width), at)

    def kernel(me_ref, *refs):
        for i in range(4):

            @pl.when(pl.program_id(0) == i)
            def _():
                refs[4][...] = refs[i][...]

    return pl.pallas_call(
        kernel,
        grid_spec=pltpu.PrefetchScalarGridSpec(
            num_scalar_prefetch=1,
            grid=(4, tiles),
            in_specs=[piece_at(i) for i in range(4)],
            out_specs=pl.BlockSpec((rows_at, width), lambda j, t, me: ((me[0] ^ j) * tiles + t, 0)),
        ),
        out_shape=jax.ShapeDtypeStruct((4 * rows, width), pieces[0].dtype),
        compiler_params=pltpu.CompilerParams(
            dimension_semantics=("arbitrary", "arbitrary"), vmem_limit_bytes=48 * 2**20
        ),
        name="assemble",
    )(lax.axis_index("fsdp").astype(jnp.int32).reshape(1), *pieces)


def token_columns(log_decay, beta, seg_ids, rim_seg):
    seqs, count = seg_ids.shape
    order = jnp.arange(count, dtype=jnp.int32)
    ones = (order[:, None] >= order[None, :]).astype(F32)
    running = jnp.einsum("ts,bsh->hbt", ones, log_decay, precision=PRECISE)
    ids = jnp.broadcast_to(seg_ids.astype(F32)[None], running.shape)
    alive = (seg_ids == rim_seg[:, -1:]).astype(F32)[None]
    ending = (seg_ids == seg_ids[:, -1:]).astype(F32)[None]
    start = jnp.exp(running) * alive
    end = jnp.exp(running[:, :, -1:] - running) * ending
    padded_ids = jnp.concatenate([rim_seg, seg_ids], axis=1)
    keeps = [
        jnp.broadcast_to(
            (padded_ids[:, tap : tap + count] == seg_ids).astype(F32)[None], running.shape
        )
        for tap in range(CONV - 1)
    ]
    betas = jnp.transpose(beta, (2, 0, 1))
    cols = jnp.stack([running, betas, start, end] + keeps + [ids], axis=-1)
    blank = jnp.zeros_like(running)
    rows = jnp.stack([running, ids] + [blank] * 6, axis=2)
    return cols, rows


def local(
    inputs,
    segment_ids,
    out_cotangent,
    mixer_gain,
    qkv_weight,
    gate_weight,
    decay_weight,
    conv_weight,
    decay_log,
    decay_bias,
    head_gain,
    out_weight,
    ffn_gain,
    ffn_in_weight,
    down_weight,
):
    batch, length, width = inputs.shape
    count = batch * length
    margin = CONV - 1
    group = lax.axis_size("fsdp")
    share = width // group
    small = jnp.concatenate(
        [
            mixer_gain,
            ffn_gain,
            head_gain,
            conv_weight.reshape(-1),
            decay_weight.reshape(-1),
        ]
    )
    small = gather_small(small)
    cuts = [mixer_gain.size, ffn_gain.size, head_gain.size, conv_weight.size, decay_weight.size]
    pieces, first = [], 0
    for size in cuts:
        pieces.append(small[:, first : first + size])
        first += size
    full_mixer_gain = pieces[0].reshape(-1).astype(F32)
    full_ffn_gain = pieces[1].reshape(-1).astype(F32)
    full_head_gain = pieces[2].reshape(1, -1).astype(F32)
    full_conv = jnp.transpose(pieces[3].reshape(group, CONV, -1), (1, 0, 2)).reshape(CONV, C3)
    full_conv = [of_group(full_conv.astype(F32), g) for g in range(GROUPS)]
    full_decay = pieces[4].reshape(width, 2 * H)
    packed = list(pack_groups(qkv_weight))
    gathers = [ShardGather(packed[0])]
    begin(gathers[0])
    full_gate = lax.all_gather(gate_weight, "fsdp", axis=0, tiled=True)
    full_down = gather_halves(down_weight)
    full_ffn_in = gather_halves(ffn_in_weight)

    rows_in = inputs.astype(F32).reshape(count, width)
    normed, pull_mixer_norm = jax.vjp(rms_norm, rows_in, full_mixer_gain)
    normed_low = normed.astype(LOW)
    edge = passed_along(inputs[:, length - margin :, :], "seq", 1).reshape(-1, width)
    edge = jnp.pad(edge, ((0, edge_rows(batch) - edge.shape[0]), (0, 0)))
    edge = rms_norm(edge.astype(F32), full_mixer_gain).astype(LOW)
    normed_all = jnp.concatenate([normed_low, edge], axis=0)
    decay_in = jnp.dot(normed_low, full_decay, preferred_element_type=F32).reshape(
        batch, length, 2 * H
    )
    rim_seg = passed_along(segment_ids[:, length - margin :], "seq", 1)
    rate = jnp.exp(decay_log)
    shifted_decay = decay_in[:, :, :H] + decay_bias
    log_decay = -rate * jax.nn.softplus(shifted_decay)
    beta = jax.nn.sigmoid(decay_in[:, :, H:])
    cols, rows = token_columns(log_decay, beta, segment_ids, rim_seg)
    heads = H // GROUPS
    made, states, pre_convs, full_qkv = [], [], [], []

    def mixer_group(g):
        weight = gathers[g].finish()
        full_qkv.append(weight)
        pre_convs.append(jnp.dot(normed_all, weight, preferred_element_type=F32).astype(LOW))
        made.append(mixer_forward(pre_convs[g], full_conv[g], cols, rows, g * heads, heads))
        states.append(Chain(made[g][4], made[g][5], "hsij,hsjv->hsiv", 1))

    def head_group(g, kept):
        _, _, local_part, carried, _, _ = made[g]
        state = states[g].finish()
        return heads_forward(
            local_part, carried, state, gate_out, full_head_gain, g * heads, kept
        )

    normed_all, cols, packed[1] = meet([gathers[0]], normed_all, cols, packed[1])
    gathers.append(ShardGather(packed[1]))
    begin(*gathers)
    mixer_group(0)
    begin(states[0])
    normed_all, packed[2], _ = meet([gathers[1]], normed_all, packed[2], made[0][1])
    gathers.append(ShardGather(packed[2]))
    begin(*gathers)
    mixer_group(1)
    begin(states[1])
    normed_all, out_shard, _ = meet([gathers[2], states[0]], normed_all, out_weight, made[1][1])
    gathers.append(ShardGather(out_shard))
    begin(gathers[2], states[0], gathers[3])
    mixer_group(2)
    begin(states[2])
    normed_gate, _ = meet([states[0], states[1]], normed_low, made[2][1])
    begin(states[0], states[1])
    gate_out = jnp.dot(normed_gate, full_gate, preferred_element_type=F32)
    (gate_out,) = meet([states[0], states[1], states[2], gathers[3]], gate_out)
    begin(states[1], states[2], gathers[3])
    gate_out = gate_out.reshape(batch, length, VD)
    heads_low = head_group(0, None)
    (heads_low,) = meet([states[1], states[2], gathers[3]], heads_low)
    begin(states[2])
    heads_low = head_group(1, heads_low)
    full_out = gathers[3].finish()
    (heads_low,) = meet([states[2]], heads_low)
    heads_low = head_group(2, heads_low)
    heads_low = heads_low.reshape(count, VD)
    middle = rows_in + jnp.dot(heads_low, full_out, preferred_element_type=F32)
    normed_ffn, pull_ffn_norm = jax.vjp(rms_norm, middle, full_ffn_gain)
    normed_ffn_low = normed_ffn.astype(LOW)
    grad_rows = out_cotangent.reshape(count, width)
    hidden_low, grad_gate_up_low = ffn_middle(normed_ffn_low, full_ffn_in, grad_rows, full_down)
    grad_in = jnp.einsum(
        "rd,rf->df", normed_ffn_low, grad_gate_up_low, preferred_element_type=F32
    )
    grad_gate_up_low, grad_in = meet([], grad_gate_up_low, grad_in.astype(LOW))
    r_in = ShardSum(grad_in, True)
    grad_normed_ffn = jnp.einsum(
        "rf,df->rd", grad_gate_up_low, full_ffn_in, preferred_element_type=F32
    )
    grad_middle_norm, grad_ffn_gain = pull_ffn_norm(grad_normed_ffn)
    grad_middle = grad_rows.astype(F32) + grad_middle_norm
    grad_branch = grad_middle.astype(LOW)
    grad_heads = jnp.einsum("rd,vd->rv", grad_branch, full_out, preferred_element_type=F32)
    grad_heads = grad_heads.reshape(batch, length, VD)
    back, grad_states = [], []

    def heads_back(g, grad, kept):
        _, _, local_part, carried, _, _ = made[g]
        back.append(
            heads_backward(
                local_part, carried, states[g].value, gate_out, full_head_gain, grad,
                g * heads, kept,
            )
        )
        grad_states.append(Chain(made[g][4], back[g][3], "hsji,hsjv->hsiv", -1))
        begin(grad_states[g])
        return back[g][1]

    kept = heads_back(0, grad_heads, None)
    grad_heads, kept = meet([], grad_heads, kept)
    kept = heads_back(1, grad_heads, kept)
    grad_heads, kept = meet([grad_states[0]], grad_heads, kept)
    begin(grad_states[0])
    grad_gate_low = heads_back(2, grad_heads, kept)
    hidden_late, heads_late, grad_gate_low = meet(
        [grad_states[0], grad_states[1]], hidden_low, heads_low, grad_gate_low
    )
    begin(grad_states[0], grad_states[1])
    grad_down = jnp.einsum("rf,rd->fd", hidden_late, grad_rows, preferred_element_type=F32)
    heads_late, grad_down, grad_gate_low = meet(
        grad_states, heads_late, grad_down.astype(LOW), grad_gate_low
    )
    p_down = scatter(grad_down)
    begin(grad_states[1], grad_states[2])
    grad_gate_low = grad_gate_low.reshape(count, VD)
    grad_out = jnp.einsum("rv,rd->vd", heads_late, grad_branch, preferred_element_type=F32)
    grad_out, r_in.value, grad_gate_low = meet(
        [], grad_out.astype(LOW), r_in.value, grad_gate_low
    )
    p_out = scatter(grad_out)
    begin(r_in)
    grad_gate = jnp.einsum("rd,rc->dc", normed_low, grad_gate_low, preferred_element_type=F32)
    mixed_a, grad_gate = meet(
        [grad_states[1], grad_states[2], r_in], back[0][0], grad_gate.astype(LOW)
    )
    r_gate = ShardSum(grad_gate)
    begin(grad_states[2], r_gate, r_in)

    run = heads * HEAD

    def mixer_back(g, grad_mixed, place, width, kept):
        t, uw, _, _, _, _ = made[g]
        return mixer_backward(
            pre_convs[g], full_conv[g], cols, rows, t, uw, states[g].value, grad_mixed,
            grad_states[g].finish(), g * heads, place, width, width, kept,
        )

    def rim_swap(grad_rim):
        return passed_along(grad_rim[:, RIM - margin :, :].astype(LOW), "seq", -1)

    def with_rim(grad_pre, came, grad_tail):
        grad_tail = (grad_tail[:, RIM - margin :, :] + came.astype(F32)).astype(LOW)
        grad_pre = lax.dynamic_update_slice(grad_pre, grad_tail, (0, length - margin, 0))
        return grad_pre.reshape(count, grad_pre.shape[2])

    def weight_grad(grad):
        return jnp.einsum("rd,rc->dc", normed_low, grad, preferred_element_type=F32).astype(LOW)

    def normed_part(grad, weight):
        return jnp.einsum("rc,dc->rd", grad, weight, preferred_element_type=F32)

    got_a = mixer_back(0, mixed_a, 0, 2 * run, [])
    mixed_b, *kept = meet([grad_states[2], r_gate, r_in], back[1][0], *got_a[:3])
    begin(r_gate, r_in)
    got_b = mixer_back(1, mixed_b, 1, 2 * run, kept)
    mixed_c, pre_ab, rim_ab, tail_ab, grad_gate_low, p_down = meet(
        [r_gate, r_in], back[2][0], *got_b[:3], grad_gate_low, p_down
    )
    r_down = ShardSum(p_down, ready=True)
    begin(r_gate, r_in, r_down)
    came_ab = rim_swap(rim_ab)
    grad_normed = normed_part(grad_gate_low, full_gate)
    pre_ab, came_ab, tail_ab, grad_normed = meet([], pre_ab, came_ab, tail_ab, grad_normed)
    pre_ab = with_rim(pre_ab, came_ab, tail_ab)
    grad_ab = weight_grad(pre_ab)
    mixed_c, grad_ab = meet([r_gate, r_down], mixed_c, grad_ab)
    p_ab = scatter(grad_ab)
    begin(r_gate, r_down)
    got_c = mixer_back(2, mixed_c, 0, run, [])
    pre_c, rim_c, tail_c, pre_ab, grad_normed, p_out = meet(
        [r_in, r_gate, r_down], *got_c[:3], pre_ab, grad_normed, p_out
    )
    r_out = ShardSum(p_out, ready=True)
    begin(r_gate, r_down, r_out)
    came_c = rim_swap(rim_c)
    grad_normed = grad_normed + normed_part(pre_ab[:, :run], full_qkv[0])
    pre_c, came_c, tail_c, grad_normed = meet([], pre_c, came_c, tail_c, grad_normed)
    pre_c = with_rim(pre_c, came_c, tail_c)
    grad_c = weight_grad(pre_c)
    grad_c, grad_normed = meet([r_gate, r_down, r_out], grad_c, grad_normed)
    sum_c = ShardSum(grad_c)
    begin(sum_c, r_out, r_gate, r_down)
    grad_normed = grad_normed + normed_part(pre_ab[:, run:], full_qkv[1])
    grad_normed, pre_c = meet([sum_c, r_out, r_gate], grad_normed, pre_c)
    begin(sum_c, r_out, r_gate)
    grad_normed = grad_normed + normed_part(pre_c, full_qkv[2])
    made_late = [item for got in (got_a, got_b, got_c) for item in got[3:5]]
    hidden_late, grad_normed, p_ab, *made_late = meet(
        [sum_c, r_out, r_gate],
        hidden_late, grad_normed, p_ab, *made_late, *[item[2] for item in back],
    )
    sum_ab = ShardSum(p_ab, ready=True)
    made_late, head_gains = made_late[: 2 * GROUPS], made_late[2 * GROUPS :]
    grad_head_gain = sum(jnp.sum(item, axis=(0, 1)) for item in head_gains)
    begin(sum_ab, sum_c, r_out)
    result = middle + jnp.dot(hidden_late, full_down, preferred_element_type=F32)
    output = result.astype(LOW).reshape(batch, length, width)
    grad_cols = jnp.concatenate(made_late[1::2], axis=0)
    conv_parts = made_late[::2]
    spans = [0, heads * DK, 2 * heads * DK, heads * HEAD]
    grad_conv = jnp.concatenate(
        [part[:, low:top] for low, top in zip(spans, spans[1:]) for part in conv_parts], axis=1
    )
    grad_log_decay = jnp.transpose(grad_cols[:, :, 0, :], (1, 2, 0))
    grad_decay_b = jnp.transpose(grad_cols[:, :, 1, :], (1, 2, 0))
    grad_decay_a = grad_log_decay * (-rate) * jax.nn.sigmoid(shifted_decay)
    grad_decay_bias = jnp.sum(grad_decay_a, axis=(0, 1))
    grad_decay_log = jnp.sum(grad_log_decay * log_decay, axis=(0, 1))
    grad_decay_low = jnp.concatenate([grad_decay_a, grad_decay_b], axis=-1).astype(LOW)
    grad_decay_low = grad_decay_low.reshape(count, 2 * H)
    grad_decay = jnp.einsum("rd,rc->dc", normed_low, grad_decay_low, preferred_element_type=F32)
    grad_normed = grad_normed + jnp.einsum(
        "rc,dc->rd", grad_decay_low, full_decay, preferred_element_type=F32
    )
    grad_rows_norm, grad_mixer_gain = pull_mixer_norm(grad_normed)
    input_grad = (grad_middle + grad_rows_norm).astype(LOW).reshape(batch, length, width)

    little = (
        grad_mixer_gain,
        grad_ffn_gain,
        grad_head_gain,
        grad_conv.reshape(-1),
        grad_decay.reshape(-1),
        grad_decay_log,
        grad_decay_bias,
    )
    small_grads = jnp.concatenate(little)
    movers = [r_in, r_gate, r_down, sum_ab, sum_c, r_out]
    (small_grads,) = meet(movers, small_grads)
    all_sum = AllSum(small_grads)
    movers.append(all_sum)
    while any(mover.todo for mover in movers):
        begin(*movers)
        meet(movers, small_grads)
    flat = all_sum.value
    sum_qkv = unpack_groups(sum_ab.value, sum_c.value)
    sum_down, sum_out = r_down.value, r_out.value
    parts, first = [], 0
    for item in little:
        parts.append(flat[first : first + item.size])
        first += item.size
    place = lax.axis_index("fsdp")

    def own(values, axis=0):
        size = values.shape[axis] // group
        return lax.dynamic_slice_in_dim(values, place * size, size, axis)

    return (
        output,
        input_grad,
        own(parts[0]),
        sum_qkv,
        r_gate.value.astype(F32),
        own(parts[4].reshape(width, 2 * H)),
        own(parts[3].reshape(CONV, C3), 1),
        parts[5],
        parts[6],
        own(parts[2]),
        sum_out.astype(F32),
        own(parts[1]),
        r_in.value.astype(F32),
        sum_down.astype(F32),
    )


def solution(mesh):
    rows = P(("dp", "fsdp"), "seq", None)
    split = P("fsdp", None)
    placed = (
        rows,
        P(("dp", "fsdp"), "seq"),
        rows,
        P("fsdp"),
        split,
        split,
        split,
        P(None, "fsdp"),
        P(),
        P(),
        P("fsdp"),
        split,
        P("fsdp"),
        split,
        split,
    )
    return jax.shard_map(
        local,
        mesh=mesh,
        in_specs=placed,
        out_specs=(
            rows,
            rows,
            P("fsdp"),
            split,
            split,
            split,
            P(None, "fsdp"),
            P(),
            P(),
            P("fsdp"),
            split,
            P("fsdp"),
            split,
            split,
        ),
        check_vma=False,
    )
```

```python
from functools import partial

import jax
import jax.numpy as jnp
from jax import lax
from jax.experimental import pallas as pl
from jax.experimental.pallas import tpu as pltpu
from jax.sharding import PartitionSpec as P

H = 6
DK = 128
DV = 256
CONV = 4
KD = 768
VD = 1536
C3 = 3072
RIM = 8
HEAD = 2 * DK + DV
GROUPS = 3

EPSILON = 1e-06
HEAD_EPSILON = 0.001
PRECISE = lax.Precision.HIGHEST
LOW = jnp.bfloat16
F32 = jnp.float32

NN = (((1,), (0,)), ((), ()))
NT = (((1,), (1,)), ((), ()))
TN = (((0,), (0,)), ((), ()))


def mm(left, right, dims=NN):
    return lax.dot_general(
        left.astype(LOW), right.astype(LOW), dims, preferred_element_type=F32
    )


def passed_along(value, axis, steps):
    count = lax.axis_size(axis)
    leading, last = (max(0, -steps), min(count, count - steps))
    return lax.ppermute(value, axis, [(source, source + steps) for source in range(leading, last)])


def rms_norm(values, gain):
    return values * lax.rsqrt(jnp.mean(values * values, axis=-1, keepdims=True) + EPSILON) * gain


def iotas(count):
    shape = (count, count)
    return lax.broadcasted_iota(jnp.int32, shape, 0), lax.broadcasted_iota(jnp.int32, shape, 1)


def conv_head(s, parts, rims, taps, cols, pad_ref):
    count = pad_ref.shape[1] - RIM
    margin = CONV - 1
    at = 0
    for part, rim in zip(parts, rims):
        width = part.shape[-1]
        pad_ref[s, RIM:, at : at + width] = part[s * count : (s + 1) * count, :].astype(F32)
        edge = rim[...].astype(F32)[margin * s : margin * (s + 1), :]
        pad_ref[s, RIM - margin : RIM, at : at + width] = edge
        at += width
    shifted = []
    total = None
    for tap in range(CONV):
        first = RIM - margin + tap
        values = pad_ref[s, first : first + count, :]
        if tap < margin:
            values = values * cols[:, 4 + tap : 5 + tap]
        shifted.append(values)
        term = values * taps[tap : tap + 1, :]
        total = term if total is None else total + term
    sig = jax.nn.sigmoid(total)
    return shifted, total, sig, total * sig


def unit(values):
    scale = lax.rsqrt(jnp.sum(values * values, axis=-1, keepdims=True) + EPSILON)
    return values * scale, scale


def decays(cols, rows, order, other):
    causal = (cols[:, 7:8] == rows[1:2, :]) & (order >= other)
    decay = jnp.exp(jnp.where(causal, cols[:, 0:1] - rows[0:1, :], -1e30))
    return decay, jnp.where(order > other, decay, 0.0)


def forward_kernel(
    q_ref, k_ref, v_ref, rq_ref, rk_ref, rv_ref, wq_ref, wk_ref, wv_ref, cols_ref, rows_ref,
    t_ref, uw_ref, local_ref, carried_ref,
    through_ref, offsets_ref, pad_ref,
):
    seqs, count = cols_ref.shape[1], cols_ref.shape[2]
    order, other = iotas(count)
    taps = jnp.concatenate([wq_ref[...], wk_ref[...], wv_ref[...]], axis=1)
    state = []
    for s in range(seqs):
        cols, rows = cols_ref[0, s], rows_ref[0, s]
        _, _, _, out = conv_head(
            s, (q_ref, k_ref, v_ref), (rq_ref, rk_ref, rv_ref), taps, cols, pad_ref
        )
        query = (unit(out[:, :DK])[0] * DK ** (-0.5)).astype(LOW)
        key = unit(out[:, DK : 2 * DK])[0].astype(LOW)
        value = out[:, 2 * DK :].astype(LOW)
        decay, strict = decays(cols, rows, order, other)
        beta, start, end = cols[:, 1:2], cols[:, 2:3], cols[:, 3:4]
        lower = beta * mm(key, key, NT) * strict
        attend = (mm(query, key, NT) * decay).astype(LOW)
        keyf = key.astype(F32)
        target = jnp.concatenate([beta * value.astype(F32), beta * start * keyf], axis=1).astype(LOW)
        state.append(dict(lower=lower, attend=attend, target=target, query=query,
                          ending=(end * keyf).astype(LOW), start=start))
    inverse, lowers = [], []
    joined = order ^ other
    eye = (joined == 0).astype(LOW)
    for x in state:
        lower = x["lower"].astype(LOW)
        lowers.append(lower)
        inverse.append(eye - lower * ((joined == 1) & (order > other)).astype(LOW))
    level = 1
    while (4 << level) <= count:
        pick = ((joined >> level) == 1).astype(LOW)
        half = [mm(lowers[s] * pick, inverse[s]).astype(LOW) for s in range(seqs)]
        for s in range(seqs):
            inverse[s] = inverse[s] - mm(inverse[s], half[s]).astype(LOW)
        level += 1
    mid = count // 2
    corner = [mm(lowers[s][mid:, :mid], inverse[s][:mid, :mid]) for s in range(seqs)]
    blank = jnp.zeros((mid, mid), LOW)
    for s in range(seqs):
        left = mm(inverse[s][mid:, mid:], corner[s]).astype(LOW)
        inverse[s] = jnp.concatenate(
            [
                jnp.concatenate([inverse[s][:mid, :mid], blank], axis=1),
                jnp.concatenate([-left, inverse[s][mid:, mid:]], axis=1),
            ],
            axis=0,
        )
    for s in range(seqs):
        x = state[s]
        t = inverse[s]
        t_ref[0, s] = t
        uw = mm(t, x["target"]).astype(LOW)
        uw_ref[0, s] = uw
        both = mm(x["attend"], uw)
        local_ref[s] = both[:, :DV]
        carried_ref[s] = (x["start"] * x["query"].astype(F32) - both[:, DV:]).astype(LOW)
        ends = mm(x["ending"], uw, TN)
        offsets_ref[0, s] = ends[:, :DV]
        small, small_other = iotas(DK)
        last = x["start"][count - 1 : count, :]
        through_ref[0, s] = (jnp.where(small == small_other, last, 0.0) - ends[:, DV:]).astype(LOW)


def heads_kernel(local_ref, carried_ref, state_ref, gate_ref, gain_ref, heads_ref):
    for s in range(local_ref.shape[0]):
        mixed = local_ref[s] + mm(carried_ref[s], state_ref[0, s])
        scale = lax.rsqrt(jnp.mean(mixed * mixed, axis=-1, keepdims=True) + HEAD_EPSILON)
        gate = gate_ref[s]
        heads_ref[s] = (mixed * scale * gain_ref[...] * (gate * jax.nn.sigmoid(gate))).astype(LOW)


def heads_back_kernel(
    local_ref, carried_ref, state_ref, gate_ref, gain_ref, grad_ref,
    mixed_ref, ggate_ref, ggain_ref, gstate_ref,
):
    gain = gain_ref[...]
    total = jnp.zeros_like(gain)
    for s in range(local_ref.shape[0]):
        mixed = local_ref[s] + mm(carried_ref[s], state_ref[0, s])
        scale = lax.rsqrt(jnp.mean(mixed * mixed, axis=-1, keepdims=True) + HEAD_EPSILON)
        normed = mixed * scale
        gate = gate_ref[s]
        sig = jax.nn.sigmoid(gate)
        act = gate * sig
        grad = grad_ref[s]
        gn = grad * normed
        total = total + jnp.sum(gn * act, axis=0, keepdims=True)
        ggate_ref[s] = (gn * gain * (sig + act * (1.0 - sig))).astype(LOW)
        e = grad * gain * act
        gmixed = (scale * (e - normed * jnp.mean(e * normed, axis=-1, keepdims=True))).astype(LOW)
        mixed_ref[s] = gmixed
        gstate_ref[0, s] = mm(carried_ref[s], gmixed, TN)
    ggain_ref[0] = total


def backward_kernel(
    q_ref, k_ref, v_ref, rq_ref, rk_ref, rv_ref, wq_ref, wk_ref, wv_ref, cols_ref, rows_ref,
    t_ref, uw_ref, state_ref, gout_ref, gend_ref,
    gpre_ref, grim_ref, gtail_ref, gtaps_ref, gcols_ref, pad_ref, shift_ref,
):
    seqs, count = cols_ref.shape[1], cols_ref.shape[2]
    order, other = iotas(count)
    taps = jnp.concatenate([wq_ref[...], wk_ref[...], wv_ref[...]], axis=1)
    before = (order < other).astype(LOW)
    head, heads = pl.program_id(0), pl.num_programs(0)
    at = (
        pl.ds(pl.multiple_of(head * DK, DK), DK),
        pl.ds(pl.multiple_of((heads + head) * DK, DK), DK),
        pl.ds(pl.multiple_of(2 * heads * DK + head * DV, DV), DV),
    )
    spans = ((0, DK), (DK, 2 * DK), (2 * DK, HEAD))
    gtaps = [None] * CONV
    for s in range(seqs):
        cols, rows = cols_ref[0, s], rows_ref[0, s]
        shifted, total, sig, out = conv_head(
            s, (q_ref, k_ref, v_ref), (rq_ref, rk_ref, rv_ref), taps, cols, pad_ref
        )
        qhat, qscale = unit(out[:, :DK])
        khat, kscale = unit(out[:, DK : 2 * DK])
        query = (qhat * DK ** (-0.5)).astype(LOW)
        key = khat.astype(LOW)
        value = out[:, 2 * DK :]
        decay, strict = decays(cols, rows, order, other)
        beta, start, end = cols[:, 1:2], cols[:, 2:3], cols[:, 3:4]
        keyf = key.astype(F32)
        weight = beta * strict
        lower = mm(key, key, NT) * weight
        attend = mm(query, key, NT) * decay
        state = state_ref[0, s]
        gend = gend_ref[0, s]
        gout = gout_ref[s]
        uw = uw_ref[0, s]
        fresh = uw[:, :DV].astype(F32) - mm(uw[:, DV:], state)
        freshl = fresh.astype(LOW)
        gfresh = mm(attend, gout, TN) + mm(end * keyf, gend)
        gtarget = mm(t_ref[0, s], gfresh, TN)
        gattend = mm(gout, freshl, NT)
        glower = -mm(gtarget, freshl, NT)
        cross = gattend * attend + glower * lower
        high = cross.astype(LOW)
        reach = mm(high, before) + mm(cross - high.astype(F32), before)
        gqk = (gattend * decay).astype(LOW)
        gkk = (glower * weight).astype(LOW)
        gout_state = mm(gout, state, NT)
        gtarget_state = beta * mm(gtarget, state, NT)
        ends = mm(freshl, gend, NT)
        gquery = mm(gqk, key) + start * gout_state
        gkey = (
            mm(gqk, query, TN)
            + mm(gkk, key)
            + mm(gkk, key, TN)
            - start * gtarget_state
            + end * ends
        )
        gvalue = beta * gtarget
        from_start = start * jnp.sum(
            query.astype(F32) * gout_state - keyf * gtarget_state, axis=-1, keepdims=True
        )
        to_end = end * jnp.sum(keyf * ends, axis=-1, keepdims=True)
        through = jnp.sum(gend.astype(F32) * state.astype(F32)) * start[count - 1 : count, :]
        glog = jnp.sum(jnp.where(order >= other, reach + from_start, to_end), axis=0, keepdims=True)
        gbeta = jnp.sum(gtarget * fresh, axis=-1, keepdims=True) * (1.0 - beta)
        gbeta = jnp.sum(jnp.where(order == other, gbeta, 0.0), axis=0, keepdims=True)
        gcols_ref[0, s] = jnp.concatenate(
            [glog + through, gbeta, jnp.zeros((6, count), F32)], axis=0
        )
        gq = gquery * DK ** (-0.5)
        gq = qscale * (gq - qhat * jnp.sum(qhat * gq, axis=-1, keepdims=True))
        gk = kscale * (gkey - khat * jnp.sum(khat * gkey, axis=-1, keepdims=True))
        gconv = jnp.concatenate([gq, gk, gvalue], axis=1) * (sig + out * (1.0 - sig))
        for tap in range(CONV):
            part = jnp.sum(gconv * shifted[tap], axis=0, keepdims=True)
            gtaps[tap] = part if gtaps[tap] is None else gtaps[tap] + part
        width = gconv.shape[1]
        blank = jnp.zeros((RIM, width), F32)
        back = None
        for tap in range(CONV):
            term = gconv * taps[tap : tap + 1, :]
            if tap < CONV - 1:
                term = term * cols[:, 4 + tap : 5 + tap]
            shift_ref[tap, 0:RIM, :] = blank
            shift_ref[tap, RIM : RIM + count, :] = term
            shift_ref[tap, RIM + count :, :] = blank
            first = CONV - 1 - tap
            moved = shift_ref[tap, first : first + RIM + count, :]
            back = moved if back is None else back + moved
        for place, (low, top) in zip(at, spans):
            gpre_ref[s, :, place] = back[RIM:, low:top].astype(LOW)
            grim_ref[s, :, place] = back[:RIM, low:top]
            gtail_ref[s, :, place] = back[count:, low:top]
    gtaps = jnp.concatenate(gtaps, axis=0)
    for place, (low, top) in zip(at, spans):
        gtaps_ref[:, place] = gtaps[:, low:top]


def per_head(seqs, rows, width, first=0):
    return pl.BlockSpec((1, seqs, rows, width), lambda h: (first + h, 0, 0, 0))


def by_column(seqs, count, width, first=0):
    return pl.BlockSpec((seqs, count, width), lambda h: (0, 0, first + h))


def head_specs(seqs, count, first, heads):
    def cut(rows, row, width, column):
        return pl.BlockSpec((rows, width), lambda h: (row, column + h))

    rows, edge = seqs * count, edge_rows(seqs)
    late = 2 * heads * DK // DV
    specs = [cut(rows, 0, DK, 0), cut(rows, 0, DK, heads), cut(rows, 0, DV, late)]
    at = rows // edge
    specs += [cut(edge, at, DK, 0), cut(edge, at, DK, heads), cut(edge, at, DV, late)]
    specs += [cut(CONV, 0, DK, 0), cut(CONV, 0, DK, heads), cut(CONV, 0, DV, late)]
    return specs + [per_head(seqs, count, 8, first), per_head(seqs, 8, count, first)]


def edge_rows(seqs):
    return -(-seqs * (CONV - 1) // 16) * 16


def whole(*shape):
    return pl.BlockSpec(shape, lambda h: (0,) * len(shape))


def params(limit=48):
    return pltpu.CompilerParams(
        dimension_semantics=("arbitrary",), vmem_limit_bytes=limit * 2**20
    )


def mixer_forward(pre_conv, taps, cols, rows, first, heads):
    seqs, count = cols.shape[1], cols.shape[2]
    return pl.pallas_call(
        forward_kernel,
        grid=(heads,),
        in_specs=head_specs(seqs, count, first, heads),
        out_specs=[
            per_head(seqs, count, count),
            per_head(seqs, count, DV + DK),
            by_column(seqs, count, DV),
            by_column(seqs, count, DK),
            per_head(seqs, DK, DK),
            per_head(seqs, DK, DV),
        ],
        out_shape=[
            jax.ShapeDtypeStruct((heads, seqs, count, count), LOW),
            jax.ShapeDtypeStruct((heads, seqs, count, DV + DK), LOW),
            jax.ShapeDtypeStruct((seqs, count, heads * DV), F32),
            jax.ShapeDtypeStruct((seqs, count, heads * DK), LOW),
            jax.ShapeDtypeStruct((heads, seqs, DK, DK), LOW),
            jax.ShapeDtypeStruct((heads, seqs, DK, DV), F32),
        ],
        scratch_shapes=[pltpu.VMEM((seqs, RIM + count, HEAD), F32)],
        compiler_params=params(),
        name="mixer_forward",
    )(*[pre_conv] * 6, *[taps] * 3, cols, rows)


def heads_forward(local_part, carried, state, gate, gain, first, kept):
    seqs, count = local_part.shape[0], local_part.shape[1]
    heads = state.shape[0]
    operands = [local_part, carried, state, gate, gain]
    in_specs = [
        by_column(seqs, count, DV),
        by_column(seqs, count, DK),
        per_head(seqs, DK, DV),
        by_column(seqs, count, DV, first),
        pl.BlockSpec((1, DV), lambda h: (0, 0)),
    ]
    aliases = {}
    if kept is not None:
        operands.append(kept)
        in_specs.append(pl.BlockSpec(memory_space=pl.ANY))
        aliases = {5: 0}

    def kernel(*refs):
        heads_kernel(*refs[:5], refs[-1])

    return pl.pallas_call(
        kernel,
        grid=(heads,),
        in_specs=in_specs,
        out_specs=by_column(seqs, count, DV, first),
        out_shape=jax.ShapeDtypeStruct((seqs, count, VD), LOW),
        input_output_aliases=aliases,
        compiler_params=params(),
        name="heads_forward",
    )(*operands)


def heads_backward(local_part, carried, state, gate, gain, grad, first, kept):
    seqs, count = local_part.shape[0], local_part.shape[1]
    heads = state.shape[0]
    operands = [local_part, carried, state, gate, gain, grad]
    in_specs = [
        by_column(seqs, count, DV),
        by_column(seqs, count, DK),
        per_head(seqs, DK, DV),
        by_column(seqs, count, DV, first),
        pl.BlockSpec((1, DV), lambda h: (0, 0)),
        by_column(seqs, count, DV, first),
    ]
    aliases = {}
    if kept is not None:
        operands.append(kept)
        in_specs.append(pl.BlockSpec(memory_space=pl.ANY))
        aliases = {6: 1}

    def kernel(*refs):
        heads_back_kernel(*refs[:6], *refs[-4:])

    return pl.pallas_call(
        kernel,
        grid=(heads,),
        in_specs=in_specs,
        out_specs=[
            by_column(seqs, count, DV),
            by_column(seqs, count, DV, first),
            pl.BlockSpec((1, 1, DV), lambda h: (h, 0, 0)),
            per_head(seqs, DK, DV),
        ],
        out_shape=[
            jax.ShapeDtypeStruct((seqs, count, heads * DV), LOW),
            jax.ShapeDtypeStruct((seqs, count, VD), LOW),
            jax.ShapeDtypeStruct((heads, 1, DV), F32),
            jax.ShapeDtypeStruct((heads, seqs, DK, DV), F32),
        ],
        input_output_aliases=aliases,
        compiler_params=params(),
        name="heads_backward",
    )(*operands)


def mixer_backward(
    pre_conv, taps, cols, rows, t, uw, state, gout, gend, first, place, width, rims, kept
):
    seqs, count = cols.shape[1], cols.shape[2]
    heads = state.shape[0]
    run = heads * HEAD

    def at(*shape):
        return pl.BlockSpec(shape, lambda h: (0, 0, place))

    operands = [*[pre_conv] * 6, *[taps] * 3, cols, rows, t, uw, state, gout, gend]
    inputs = len(operands)
    aliases = {inputs + i: i for i in range(len(kept))}

    def kernel(*refs):
        backward_kernel(*refs[:inputs], *refs[inputs + len(kept) :])

    return pl.pallas_call(
        kernel,
        grid=(heads,),
        in_specs=head_specs(seqs, count, first, heads)
        + [
            per_head(seqs, count, count),
            per_head(seqs, count, DV + DK),
            per_head(seqs, DK, DV),
            by_column(seqs, count, DV),
            per_head(seqs, DK, DV),
        ]
        + [pl.BlockSpec(memory_space=pl.ANY)] * len(kept),
        out_specs=[
            at(seqs, count, run),
            at(seqs, RIM, run),
            at(seqs, RIM, run),
            whole(CONV, run),
            per_head(seqs, 8, count),
        ],
        out_shape=[
            jax.ShapeDtypeStruct((seqs, count, width), LOW),
            jax.ShapeDtypeStruct((seqs, RIM, rims), F32),
            jax.ShapeDtypeStruct((seqs, RIM, rims), F32),
            jax.ShapeDtypeStruct((CONV, run), F32),
            jax.ShapeDtypeStruct((heads, seqs, 8, count), F32),
        ],
        scratch_shapes=[
            pltpu.VMEM((seqs, RIM + count, HEAD), F32),
            pltpu.VMEM((CONV, 2 * RIM + count, HEAD), F32),
        ],
        input_output_aliases=aliases,
        compiler_params=params(),
        name="mixer_backward",
    )(*operands, *kept)


def ffn_kernel(x_ref, up_ref, side_ref, grad_ref, down_ref, hidden_ref, back_ref):
    tile = up_ref.shape[1]
    half = back_ref.shape[1] // 2
    at = pl.program_id(0) * tile
    rows = x_ref.shape[0]
    step = 256 if rows % 256 == 0 else rows

    def part(i, _):
        here = pl.ds(pl.multiple_of(i * step, step), step)
        x = x_ref[here, :]
        a = mm(x, up_ref[...])
        b = mm(x, side_ref[...])
        grad = mm(grad_ref[here, :], down_ref[...], NT)
        sig = jax.nn.sigmoid(a)
        act = a * sig
        hidden_ref[here, :] = (act * b).astype(LOW)
        first = grad * b * (sig + act * (1.0 - sig))
        back_ref[here, pl.ds(pl.multiple_of(at, tile), tile)] = first.astype(LOW)
        back_ref[here, pl.ds(pl.multiple_of(half + at, tile), tile)] = (grad * act).astype(LOW)
        return 0

    lax.fori_loop(0, rows // step, part, 0)


def ffn_middle(x, weight, grad, down):
    rows, width = x.shape
    units = down.shape[0]
    tile = 256
    tiles = units // tile
    return pl.pallas_call(
        ffn_kernel,
        grid=(tiles,),
        in_specs=[
            pl.BlockSpec((rows, width), lambda j: (0, 0)),
            pl.BlockSpec((width, tile), lambda j: (0, j)),
            pl.BlockSpec((width, tile), lambda j: (0, tiles + j)),
            pl.BlockSpec((rows, width), lambda j: (0, 0)),
            pl.BlockSpec((tile, width), lambda j: (j, 0)),
        ],
        out_specs=[
            pl.BlockSpec((rows, tile), lambda j: (0, j)),
            pl.BlockSpec((rows, 2 * units), lambda j: (0, 0)),
        ],
        out_shape=[
            jax.ShapeDtypeStruct((rows, units), LOW),
            jax.ShapeDtypeStruct((rows, 2 * units), LOW),
        ],
        compiler_params=params(),
        name="ffn_middle",
    )(x, weight, weight, grad, down)


def group_cuts(g):
    heads = H // GROUPS
    return (
        (g * heads * DK, heads * DK),
        (KD + g * heads * DK, heads * DK),
        (2 * KD + g * heads * DV, heads * DV),
    )


def of_group(values, g):
    return jnp.concatenate([values[:, at : at + size] for at, size in group_cuts(g)], axis=1)


def pack_groups(weight):
    rows = weight.shape[0]
    width = C3 // GROUPS

    def kernel(weight_ref, *outs):
        for g, out in enumerate(outs):
            first = 0
            for at, size in group_cuts(g):
                out[:, first : first + size] = weight_ref[:, at : at + size]
                first += size

    return pl.pallas_call(
        kernel,
        out_shape=[jax.ShapeDtypeStruct((rows, width), weight.dtype)] * GROUPS,
        compiler_params=pltpu.CompilerParams(vmem_limit_bytes=48 * 2**20),
        name="pack_groups",
    )(weight)


def unpack_groups(first, last):
    rows = first.shape[0]
    run = C3 // GROUPS

    def kernel(first_ref, last_ref, qkv_ref):
        for g in range(GROUPS):
            part, at = (last_ref, 0) if g == GROUPS - 1 else (first_ref, g * run)
            for to, size in group_cuts(g):
                qkv_ref[:, to : to + size] = part[:, at : at + size].astype(F32)
                at += size

    return pl.pallas_call(
        kernel,
        out_shape=jax.ShapeDtypeStruct((rows, C3), F32),
        compiler_params=pltpu.CompilerParams(vmem_limit_bytes=48 * 2**20),
        name="unpack_groups",
    )(first, last)


def swap(values, axis, bit):
    count = lax.axis_size(axis)
    return lax.ppermute(values, axis, [(at, at ^ bit) for at in range(count)])


def my_bit(axis, bit):
    return (lax.axis_index(axis) // bit) % 2


def plus(left, right):
    return (left.astype(F32) + right.astype(F32)).astype(LOW)


def bits_of(axis):
    count, bits, bit = lax.axis_size(axis), [], 1
    while bit < count:
        bits.append(bit)
        bit *= 2
    return bits if bit == count else None


def split(values):
    return values.reshape((2, values.shape[0] // 2) + values.shape[1:])


class Mover:
    pending = None
    value = None

    def __init__(self):
        self.todo = []

    def begin(self):
        if self.todo:
            send, self.then = self.todo.pop(0)
            self.pending = send()
        return self

    def settle(self, came):
        self.pending = None
        self.value = self.then(came)

    def finish(self):
        while self.todo or self.pending is not None:
            if self.pending is None:
                self.begin()
            self.settle(self.pending)
        return self.value


def scattered_sums():
    return all(bits_of(axis) is not None for axis in ("fsdp", "dp", "seq"))


def scatter(grad):
    if not scattered_sums():
        shard = lax.psum_scatter(grad, "fsdp", scatter_dimension=0, tiled=True)
        return lax.psum(shard, ("dp", "seq"))
    return lax.psum_scatter(grad, ("fsdp", "dp"), scatter_dimension=0, tiled=True)


class ShardSum(Mover):
    def __init__(self, grad, scattered=False, ready=False):
        super().__init__()
        self.value = grad.astype(LOW)
        if ready and not scattered_sums():
            return
        self.plain = any(bits_of(axis) is None for axis in ("fsdp", "dp", "seq"))
        if self.plain:
            shard = lax.psum_scatter(self.value, "fsdp", scatter_dimension=0, tiled=True)
            self.value = lax.psum(shard, ("dp", "seq"))
            return
        if ready:
            scattered = True
        elif scattered:
            self.value = lax.psum_scatter(
                self.value, ("fsdp", "dp"), scatter_dimension=0, tiled=True
            )
        else:
            bits = bits_of("fsdp")
            self.value = self.value.reshape((2,) * len(bits) + (-1, grad.shape[1]))
            for at, bit in enumerate(bits):
                self.halved("fsdp", bit, len(bits) - 1 - at)
        undo = []
        for axis in ("dp", "seq"):
            bits = bits_of(axis)
            if axis == "dp" and scattered:
                undo += [(axis, bit) for bit in reversed(bits)]
                continue
            for bit in bits:
                if axis == "seq" and bit == bits[-1]:
                    self.added(axis, bit)
                else:
                    self.halved(axis, bit, None)
                    undo.append((axis, bit))
        for axis, bit in reversed(undo):
            self.joined(axis, bit)

    def halved(self, axis, bit, dim):
        def entries():
            return (split(self.value), 0) if dim is None else (self.value, dim)

        def send():
            values, at = entries()
            part = lax.dynamic_index_in_dim(values, 1 - my_bit(axis, bit), at, keepdims=False)
            return swap(part, axis, bit)

        def then(came):
            values, at = entries()
            part = lax.dynamic_index_in_dim(values, my_bit(axis, bit), at, keepdims=False)
            return plus(part, came)

        self.todo.append((send, then))

    def added(self, axis, bit):
        self.todo.append(
            (lambda: swap(self.value, axis, bit), lambda came: plus(self.value, came))
        )

    def joined(self, axis, bit):
        self.todo.append(
            (lambda: swap(self.value, axis, bit), lambda came: put_together(self.value, came, axis, bit))
        )


class Chain(Mover):
    def __init__(self, through, offsets, spec, step):
        super().__init__()
        last = lax.axis_size("seq") - 1
        for hop in range(last) if step > 0 else range(last, 0, -1):
            self.todo.append((partial(self.leave, through, offsets, spec, hop, step), self.take))

    def leave(self, through, offsets, spec, hop, step):
        leaving = offsets
        if self.value is not None:
            leaving = leaving + jnp.einsum(spec, through, self.value, preferred_element_type=F32)
        return lax.ppermute(leaving.astype(LOW), "seq", [(hop, hop + step)])

    def take(self, came):
        return came if self.value is None else self.value + came


class AllSum(Mover):
    def __init__(self, values):
        super().__init__()
        self.value = values
        for axis in ("fsdp", "dp", "seq"):
            count = lax.axis_size(axis)
            if bits_of(axis) is None or count > 4:
                self.value = lax.psum(self.value, axis)
            else:
                self.todo.append((partial(self.send, axis, count), self.take))

    def send(self, axis, count):
        return tuple(swap(self.value, axis, bit) for bit in range(1, count))

    def take(self, came):
        if len(came) == 1:
            return self.value + came[0]
        return (self.value + came[0]) + (came[1] + came[2])


def meet(movers, *arrays):
    movers = [mover for mover in movers if mover.pending is not None]
    arrays, came = lax.optimization_barrier((arrays, [mover.pending for mover in movers]))
    for mover, values in zip(movers, came):
        mover.settle(values)
    return arrays


def begin(*movers):
    for mover in movers:
        mover.begin()


def put_together(mine, came, axis, bit):
    first = my_bit(axis, bit) == 0
    both = jnp.where(first, jnp.stack([mine, came]), jnp.stack([came, mine]))
    return both.reshape((2 * mine.shape[0],) + mine.shape[1:])


class ShardGather(Mover):
    def __init__(self, shard):
        super().__init__()
        if lax.axis_size("fsdp") != 4:
            self.value = lax.all_gather(shard, "fsdp", axis=0, tiled=True)
            return
        beside = swap(shard, "fsdp", 1)
        self.todo = [
            (lambda: swap(shard, "fsdp", 2), lambda came: came),
            (
                lambda: swap(self.value, "fsdp", 1),
                lambda came: assemble((shard, beside, self.value, came)),
            ),
        ]


def gather_halves(shard):
    count = lax.axis_size("dp")
    part = shard.reshape((count, shard.shape[0] // count) + shard.shape[1:])
    part = lax.dynamic_index_in_dim(part, lax.axis_index("dp"), 0, keepdims=False)
    return lax.all_gather(part, ("fsdp", "dp"), axis=0, tiled=True)


def gather_small(values):
    if lax.axis_size("fsdp") != 4:
        return lax.all_gather(values, "fsdp", axis=0)
    me = lax.axis_index("fsdp")
    rows = [values] + [swap(values, "fsdp", bit) for bit in (1, 2, 3)]
    out = jnp.zeros((4, values.shape[0]), values.dtype)
    for i, row in enumerate(rows):
        out = lax.dynamic_update_slice(out, row[None], (me ^ i, 0))
    return out


def assemble(pieces):
    rows, width = pieces[0].shape
    tiles = 1
    rows_at = rows // tiles

    def piece_at(i):
        def at(j, t, me):
            return (jnp.where(j == i, t, jnp.where(j < i, 0, tiles - 1)), 0)

        return pl.BlockSpec((rows_at, width), at)

    def kernel(me_ref, *refs):
        for i in range(4):

            @pl.when(pl.program_id(0) == i)
            def _():
                refs[4][...] = refs[i][...]

    return pl.pallas_call(
        kernel,
        grid_spec=pltpu.PrefetchScalarGridSpec(
            num_scalar_prefetch=1,
            grid=(4, tiles),
            in_specs=[piece_at(i) for i in range(4)],
            out_specs=pl.BlockSpec((rows_at, width), lambda j, t, me: ((me[0] ^ j) * tiles + t, 0)),
        ),
        out_shape=jax.ShapeDtypeStruct((4 * rows, width), pieces[0].dtype),
        compiler_params=pltpu.CompilerParams(
            dimension_semantics=("arbitrary", "arbitrary"), vmem_limit_bytes=48 * 2**20
        ),
        name="assemble",
    )(lax.axis_index("fsdp").astype(jnp.int32).reshape(1), *pieces)


def token_columns(log_decay, beta, seg_ids, rim_seg):
    seqs, count = seg_ids.shape
    order = jnp.arange(count, dtype=jnp.int32)
    ones = (order[:, None] >= order[None, :]).astype(F32)
    running = jnp.einsum("ts,bsh->hbt", ones, log_decay, precision=PRECISE)
    ids = jnp.broadcast_to(seg_ids.astype(F32)[None], running.shape)
    alive = (seg_ids == rim_seg[:, -1:]).astype(F32)[None]
    ending = (seg_ids == seg_ids[:, -1:]).astype(F32)[None]
    start = jnp.exp(running) * alive
    end = jnp.exp(running[:, :, -1:] - running) * ending
    padded_ids = jnp.concatenate([rim_seg, seg_ids], axis=1)
    keeps = [
        jnp.broadcast_to(
            (padded_ids[:, tap : tap + count] == seg_ids).astype(F32)[None], running.shape
        )
        for tap in range(CONV - 1)
    ]
    betas = jnp.transpose(beta, (2, 0, 1))
    cols = jnp.stack([running, betas, start, end] + keeps + [ids], axis=-1)
    blank = jnp.zeros_like(running)
    rows = jnp.stack([running, ids] + [blank] * 6, axis=2)
    return cols, rows


def local(
    inputs,
    segment_ids,
    out_cotangent,
    mixer_gain,
    qkv_weight,
    gate_weight,
    decay_weight,
    conv_weight,
    decay_log,
    decay_bias,
    head_gain,
    out_weight,
    ffn_gain,
    ffn_in_weight,
    down_weight,
):
    batch, length, width = inputs.shape
    count = batch * length
    margin = CONV - 1
    group = lax.axis_size("fsdp")
    share = width // group
    small = jnp.concatenate(
        [
            mixer_gain,
            ffn_gain,
            head_gain,
            conv_weight.reshape(-1),
            decay_weight.reshape(-1),
        ]
    )
    small = gather_small(small)
    cuts = [mixer_gain.size, ffn_gain.size, head_gain.size, conv_weight.size, decay_weight.size]
    pieces, first = [], 0
    for size in cuts:
        pieces.append(small[:, first : first + size])
        first += size
    full_mixer_gain = pieces[0].reshape(-1).astype(F32)
    full_ffn_gain = pieces[1].reshape(-1).astype(F32)
    full_head_gain = pieces[2].reshape(1, -1).astype(F32)
    full_conv = jnp.transpose(pieces[3].reshape(group, CONV, -1), (1, 0, 2)).reshape(CONV, C3)
    full_conv = [of_group(full_conv.astype(F32), g) for g in range(GROUPS)]
    full_decay = pieces[4].reshape(width, 2 * H)
    packed = list(pack_groups(qkv_weight))
    gathers = [ShardGather(packed[0])]
    begin(gathers[0])
    full_gate = lax.all_gather(gate_weight, "fsdp", axis=0, tiled=True)
    full_down = gather_halves(down_weight)
    full_ffn_in = gather_halves(ffn_in_weight)

    rows_in = inputs.astype(F32).reshape(count, width)
    normed, pull_mixer_norm = jax.vjp(rms_norm, rows_in, full_mixer_gain)
    normed_low = normed.astype(LOW)
    edge = passed_along(inputs[:, length - margin :, :], "seq", 1).reshape(-1, width)
    edge = jnp.pad(edge, ((0, edge_rows(batch) - edge.shape[0]), (0, 0)))
    edge = rms_norm(edge.astype(F32), full_mixer_gain).astype(LOW)
    normed_all = jnp.concatenate([normed_low, edge], axis=0)
    decay_in = jnp.dot(normed_low, full_decay, preferred_element_type=F32).reshape(
        batch, length, 2 * H
    )
    rim_seg = passed_along(segment_ids[:, length - margin :], "seq", 1)
    rate = jnp.exp(decay_log)
    shifted_decay = decay_in[:, :, :H] + decay_bias
    log_decay = -rate * jax.nn.softplus(shifted_decay)
    beta = jax.nn.sigmoid(decay_in[:, :, H:])
    cols, rows = token_columns(log_decay, beta, segment_ids, rim_seg)
    heads = H // GROUPS
    made, states, pre_convs, full_qkv = [], [], [], []

    def mixer_group(g):
        weight = gathers[g].finish()
        full_qkv.append(weight)
        pre_convs.append(jnp.dot(normed_all, weight, preferred_element_type=F32).astype(LOW))
        made.append(mixer_forward(pre_convs[g], full_conv[g], cols, rows, g * heads, heads))
        states.append(Chain(made[g][4], made[g][5], "hsij,hsjv->hsiv", 1))

    def head_group(g, kept):
        _, _, local_part, carried, _, _ = made[g]
        state = states[g].finish()
        return heads_forward(
            local_part, carried, state, gate_out, full_head_gain, g * heads, kept
        )

    normed_all, cols, packed[1] = meet([gathers[0]], normed_all, cols, packed[1])
    gathers.append(ShardGather(packed[1]))
    begin(*gathers)
    mixer_group(0)
    begin(states[0])
    normed_all, packed[2], _ = meet([gathers[1]], normed_all, packed[2], made[0][1])
    gathers.append(ShardGather(packed[2]))
    begin(*gathers)
    mixer_group(1)
    begin(states[1])
    normed_all, out_shard, _ = meet([gathers[2], states[0]], normed_all, out_weight, made[1][1])
    gathers.append(ShardGather(out_shard))
    begin(gathers[2], states[0], gathers[3])
    mixer_group(2)
    begin(states[2])
    normed_gate, _ = meet([states[0], states[1]], normed_low, made[2][1])
    begin(states[0], states[1])
    gate_out = jnp.dot(normed_gate, full_gate, preferred_element_type=F32)
    (gate_out,) = meet([states[0], states[1], states[2], gathers[3]], gate_out)
    begin(states[1], states[2], gathers[3])
    gate_out = gate_out.reshape(batch, length, VD)
    heads_low = head_group(0, None)
    (heads_low,) = meet([states[1], states[2], gathers[3]], heads_low)
    begin(states[2])
    heads_low = head_group(1, heads_low)
    full_out = gathers[3].finish()
    (heads_low,) = meet([states[2]], heads_low)
    heads_low = head_group(2, heads_low)
    heads_low = heads_low.reshape(count, VD)
    middle = rows_in + jnp.dot(heads_low, full_out, preferred_element_type=F32)
    normed_ffn, pull_ffn_norm = jax.vjp(rms_norm, middle, full_ffn_gain)
    normed_ffn_low = normed_ffn.astype(LOW)
    grad_rows = out_cotangent.reshape(count, width)
    hidden_low, grad_gate_up_low = ffn_middle(normed_ffn_low, full_ffn_in, grad_rows, full_down)
    grad_in = jnp.einsum(
        "rd,rf->df", normed_ffn_low, grad_gate_up_low, preferred_element_type=F32
    )
    grad_gate_up_low, grad_in = meet([], grad_gate_up_low, grad_in.astype(LOW))
    r_in = ShardSum(grad_in, True)
    grad_normed_ffn = jnp.einsum(
        "rf,df->rd", grad_gate_up_low, full_ffn_in, preferred_element_type=F32
    )
    grad_middle_norm, grad_ffn_gain = pull_ffn_norm(grad_normed_ffn)
    grad_middle = grad_rows.astype(F32) + grad_middle_norm
    grad_branch = grad_middle.astype(LOW)
    grad_heads = jnp.einsum("rd,vd->rv", grad_branch, full_out, preferred_element_type=F32)
    grad_heads = grad_heads.reshape(batch, length, VD)
    back, grad_states = [], []

    def heads_back(g, grad, kept):
        _, _, local_part, carried, _, _ = made[g]
        back.append(
            heads_backward(
                local_part, carried, states[g].value, gate_out, full_head_gain, grad,
                g * heads, kept,
            )
        )
        grad_states.append(Chain(made[g][4], back[g][3], "hsji,hsjv->hsiv", -1))
        begin(grad_states[g])
        return back[g][1]

    kept = heads_back(0, grad_heads, None)
    grad_heads, kept = meet([], grad_heads, kept)
    kept = heads_back(1, grad_heads, kept)
    grad_heads, kept = meet([grad_states[0]], grad_heads, kept)
    begin(grad_states[0])
    grad_gate_low = heads_back(2, grad_heads, kept)
    hidden_late, heads_late, grad_gate_low = meet(
        [grad_states[0], grad_states[1]], hidden_low, heads_low, grad_gate_low
    )
    begin(grad_states[0], grad_states[1])
    grad_down = jnp.einsum("rf,rd->fd", hidden_late, grad_rows, preferred_element_type=F32)
    heads_late, grad_down, grad_gate_low = meet(
        grad_states, heads_late, grad_down.astype(LOW), grad_gate_low
    )
    p_down = scatter(grad_down)
    begin(grad_states[1], grad_states[2])
    grad_gate_low = grad_gate_low.reshape(count, VD)
    grad_out = jnp.einsum("rv,rd->vd", heads_late, grad_branch, preferred_element_type=F32)
    grad_gate = jnp.einsum("rd,rc->dc", normed_low, grad_gate_low, preferred_element_type=F32)
    mixed_a, grad_out, grad_gate, r_in.value = meet(
        [grad_states[1], grad_states[2]],
        back[0][0], grad_out.astype(LOW), grad_gate.astype(LOW), r_in.value,
    )
    p_out = scatter(grad_out)
    r_gate = ShardSum(grad_gate)
    begin(grad_states[2], r_gate, r_in)

    run = heads * HEAD

    def mixer_back(g, grad_mixed, place, width, kept):
        t, uw, _, _, _, _ = made[g]
        return mixer_backward(
            pre_convs[g], full_conv[g], cols, rows, t, uw, states[g].value, grad_mixed,
            grad_states[g].finish(), g * heads, place, width, width, kept,
        )

    def rim_swap(grad_rim):
        return passed_along(grad_rim[:, RIM - margin :, :].astype(LOW), "seq", -1)

    def with_rim(grad_pre, came, grad_tail):
        grad_tail = (grad_tail[:, RIM - margin :, :] + came.astype(F32)).astype(LOW)
        grad_pre = lax.dynamic_update_slice(grad_pre, grad_tail, (0, length - margin, 0))
        return grad_pre.reshape(count, grad_pre.shape[2])

    def weight_grad(grad):
        return jnp.einsum("rd,rc->dc", normed_low, grad, preferred_element_type=F32).astype(LOW)

    def normed_part(grad, weight):
        return jnp.einsum("rc,dc->rd", grad, weight, preferred_element_type=F32)

    got_a = mixer_back(0, mixed_a, 0, 2 * run, [])
    mixed_b, *kept = meet([grad_states[2], r_gate, r_in], back[1][0], *got_a[:3])
    begin(r_gate, r_in)
    got_b = mixer_back(1, mixed_b, 1, 2 * run, kept)
    mixed_c, pre_ab, rim_ab, tail_ab, grad_gate_low, p_down = meet(
        [r_gate], back[2][0], *got_b[:3], grad_gate_low, p_down
    )
    r_down = ShardSum(p_down, ready=True)
    begin(r_gate, r_down)
    came_ab = rim_swap(rim_ab)
    grad_normed = normed_part(grad_gate_low, full_gate)
    pre_ab, came_ab, tail_ab, grad_normed = meet([], pre_ab, came_ab, tail_ab, grad_normed)
    pre_ab = with_rim(pre_ab, came_ab, tail_ab)
    grad_ab = weight_grad(pre_ab)
    mixed_c, grad_ab = meet([r_gate, r_down, r_in], mixed_c, grad_ab)
    p_ab = scatter(grad_ab)
    begin(r_gate, r_down, r_in)
    got_c = mixer_back(2, mixed_c, 0, run, [])
    pre_c, rim_c, tail_c, pre_ab, grad_normed, p_out = meet(
        [r_in, r_gate, r_down], *got_c[:3], pre_ab, grad_normed, p_out
    )
    r_out = ShardSum(p_out, ready=True)
    begin(r_in, r_gate, r_down, r_out)
    came_c = rim_swap(rim_c)
    grad_normed = grad_normed + normed_part(pre_ab[:, :run], full_qkv[0])
    pre_c, came_c, tail_c, grad_normed = meet([], pre_c, came_c, tail_c, grad_normed)
    pre_c = with_rim(pre_c, came_c, tail_c)
    grad_c = weight_grad(pre_c)
    grad_c, grad_normed = meet([r_gate, r_down, r_out], grad_c, grad_normed)
    sum_c = ShardSum(grad_c)
    begin(sum_c, r_out, r_gate, r_down)
    grad_normed = grad_normed + normed_part(pre_ab[:, run:], full_qkv[1])
    grad_normed, pre_c = meet([sum_c, r_out, r_gate], grad_normed, pre_c)
    begin(sum_c, r_out, r_gate)
    grad_normed = grad_normed + normed_part(pre_c, full_qkv[2])
    made_late = [item for got in (got_a, got_b, got_c) for item in got[3:5]]
    hidden_late, grad_normed, p_ab, *made_late = meet(
        [sum_c, r_out, r_gate, r_in],
        hidden_late, grad_normed, p_ab, *made_late, *[item[2] for item in back],
    )
    sum_ab = ShardSum(p_ab, ready=True)
    made_late, head_gains = made_late[: 2 * GROUPS], made_late[2 * GROUPS :]
    grad_head_gain = sum(jnp.sum(item, axis=(0, 1)) for item in head_gains)
    begin(sum_ab, sum_c, r_out)
    result = middle + jnp.dot(hidden_late, full_down, preferred_element_type=F32)
    output = result.astype(LOW).reshape(batch, length, width)
    grad_cols = jnp.concatenate(made_late[1::2], axis=0)
    conv_parts = made_late[::2]
    spans = [0, heads * DK, 2 * heads * DK, heads * HEAD]
    grad_conv = jnp.concatenate(
        [part[:, low:top] for low, top in zip(spans, spans[1:]) for part in conv_parts], axis=1
    )
    grad_log_decay = jnp.transpose(grad_cols[:, :, 0, :], (1, 2, 0))
    grad_decay_b = jnp.transpose(grad_cols[:, :, 1, :], (1, 2, 0))
    grad_decay_a = grad_log_decay * (-rate) * jax.nn.sigmoid(shifted_decay)
    grad_decay_bias = jnp.sum(grad_decay_a, axis=(0, 1))
    grad_decay_log = jnp.sum(grad_log_decay * log_decay, axis=(0, 1))
    grad_decay_low = jnp.concatenate([grad_decay_a, grad_decay_b], axis=-1).astype(LOW)
    grad_decay_low = grad_decay_low.reshape(count, 2 * H)
    grad_decay = jnp.einsum("rd,rc->dc", normed_low, grad_decay_low, preferred_element_type=F32)
    grad_normed = grad_normed + jnp.einsum(
        "rc,dc->rd", grad_decay_low, full_decay, preferred_element_type=F32
    )
    grad_rows_norm, grad_mixer_gain = pull_mixer_norm(grad_normed)
    input_grad = (grad_middle + grad_rows_norm).astype(LOW).reshape(batch, length, width)

    little = (
        grad_mixer_gain,
        grad_ffn_gain,
        grad_head_gain,
        grad_conv.reshape(-1),
        grad_decay.reshape(-1),
        grad_decay_log,
        grad_decay_bias,
    )
    small_grads = jnp.concatenate(little)
    movers = [r_in, r_gate, r_down, sum_ab, sum_c, r_out]
    (small_grads,) = meet(movers, small_grads)
    all_sum = AllSum(small_grads)
    movers.append(all_sum)
    while any(mover.todo for mover in movers):
        begin(*movers)
        meet(movers, small_grads)
    flat = all_sum.value
    sum_qkv = unpack_groups(sum_ab.value, sum_c.value)
    sum_down, sum_out = r_down.value, r_out.value
    parts, first = [], 0
    for item in little:
        parts.append(flat[first : first + item.size])
        first += item.size
    place = lax.axis_index("fsdp")

    def own(values, axis=0):
        size = values.shape[axis] // group
        return lax.dynamic_slice_in_dim(values, place * size, size, axis)

    return (
        output,
        input_grad,
        own(parts[0]),
        sum_qkv,
        r_gate.value.astype(F32),
        own(parts[4].reshape(width, 2 * H)),
        own(parts[3].reshape(CONV, C3), 1),
        parts[5],
        parts[6],
        own(parts[2]),
        sum_out.astype(F32),
        own(parts[1]),
        r_in.value.astype(F32),
        sum_down.astype(F32),
    )


def solution(mesh):
    rows = P(("dp", "fsdp"), "seq", None)
    split = P("fsdp", None)
    placed = (
        rows,
        P(("dp", "fsdp"), "seq"),
        rows,
        P("fsdp"),
        split,
        split,
        split,
        P(None, "fsdp"),
        P(),
        P(),
        P("fsdp"),
        split,
        P("fsdp"),
        split,
        split,
    )
    return jax.shard_map(
        local,
        mesh=mesh,
        in_specs=placed,
        out_specs=(
            rows,
            rows,
            P("fsdp"),
            split,
            split,
            split,
            P(None, "fsdp"),
            P(),
            P(),
            P("fsdp"),
            split,
            P("fsdp"),
            split,
            split,
        ),
        check_vma=False,
    )
```
